256 devices in a mesh: half: 2 (over x_lo), dom: 16 (over y, x_hi, core), slab: 8 (over z).
Axes of the slice: x: 4 (x_hi: 2, x_lo: 2; x = x_hi * 2 + x_lo), y: 4, z: 8, core: 2. Of those that a mesh axis runs over, the one named last changes fastest.
Arguments:
- images: bfloat16 [2, 128, 384, 384], P('half', 'dom', 'slab'), may hold values from -6 to 6
- orientation: int32 [2, 128], P('half', 'dom'), may hold values from 0 to 511, as said below
- offsets: int32 [2, 128, 2], P('half', 'dom'), may hold values from -16 to 16
- defocus_class: int32 [2, 128], P('half', 'dom'), may hold values from 0 to 15
- defocus: float32 [16], replicated, may hold values from 150 to 900
- ori_slot: int32 [512], replicated, may hold values from 0 to 511, as said below
- half_maps: bfloat16 [2, 512, 384, 384], P('half', 'dom', 'slab'), may hold values from -8 to 8
Outputs:
- scores: float32 [2, 128], P('half', 'dom')
- new_maps: float32 [2, 512, 384, 384], P('half', 'dom', 'slab')
- shell_corr: float32 [267], replicated
The draws below stay inside these ranges and needn't reach their ends.
Inputs may be any that keep to these rules, and one draw needn't show every extreme that they name: Let owner = ori_slot[orientation[h, p]] // 32. In each block of the 8 particles of one half-set on one index of dom, at most 2 particles share an owner; in each half-set one owner takes exactly 2 particles from every block, and the other owners' counts in a block differ by at most one. `ori_slot`: a permutation of 0 .. 511.
All inputs are finite; a program needn't handle non-finite values.
Results may differ from the reference program's by a relative error of at most 0.0017.
Values may be sent and summed in bfloat16 or wider, within the bound.
A program may use at most 64 MiB of HBM per device.

```python
import math
import jax
import jax.numpy as jnp
from jax import lax

BOX = 384
KX = 192
SHIFTS = 32
PART_DEV = 8
ORI_DEV = 32
CLASSES = 16
OWNERS = 16
PARTICLES = 128
ORIENTS = 512
NSHELL = 267


def owner_plan(key):
    return jax.random.permutation(jax.random.fold_in(key, 11), ORIENTS).astype(jnp.int32)


def draw_ori_slot(key, part):
    return owner_plan(key)


def draw_orientation(key, part):
    plan = owner_plan(key)
    inverse = jnp.argsort(plan).astype(jnp.int32)
    slot_cap = max(2, 3 * PART_DEV // OWNERS)
    hot_owner = jax.random.randint(jax.random.fold_in(key, 12), (2, 1, 1), 0, OWNERS)
    block_shift = jax.random.randint(jax.random.fold_in(key, 15), (2, OWNERS, 1), 0, OWNERS - 1)
    position = jnp.arange(PART_DEV, dtype=jnp.int32)[None, None, :]
    cold_step = 1 + jnp.mod(position - slot_cap + block_shift, OWNERS - 1)
    owner_of = jnp.where(position < slot_cap, hot_owner, jnp.mod(hot_owner + cold_step, OWNERS))
    owner_of = jnp.broadcast_to(owner_of, (2, OWNERS, PART_DEV)).astype(jnp.int32)
    random_keys = jax.random.randint(jax.random.fold_in(key, 13), (2, OWNERS, PART_DEV), 0, 1 << 20) * PART_DEV + position
    order = jnp.argsort(random_keys, axis=-1)
    owner_of = jnp.take_along_axis(owner_of, order, axis=-1)
    local_row = jax.random.randint(jax.random.fold_in(key, 14), (2, OWNERS, PART_DEV), 0, ORI_DEV)
    slot_of = owner_of * ORI_DEV + local_row
    return jnp.take(inverse, slot_of).reshape(2, PARTICLES).astype(jnp.int32)


def draw_half_maps(key, part):
    half_cols = BOX // 2
    row_ids = jnp.arange(BOX, dtype=jnp.int32)
    signed_rows = jnp.where(row_ids < half_cols, row_ids, row_ids - BOX)
    columns = jnp.arange(half_cols, dtype=jnp.int32)
    squared = signed_rows[:, None] * signed_rows[:, None] + columns[None, :] * columns[None, :]
    radius = jnp.floor(jnp.sqrt(squared.astype(jnp.float32))).astype(jnp.int32)
    radius = radius - (radius * radius > squared).astype(jnp.int32) + ((radius + 1) * (radius + 1) <= squared).astype(jnp.int32)
    shells = jnp.clip(radius - 1, 0, NSHELL - 1)
    key_signal = jax.random.fold_in(key, 21)
    key_noise = jax.random.fold_in(key, 22)
    key_shell = jax.random.fold_in(key, 23)
    signal = jax.random.truncated_normal(key_signal, -5.0, 5.0, (ORIENTS, BOX, BOX), jnp.float32)
    noise = jax.random.truncated_normal(key_noise, -5.0, 5.0, (2, ORIENTS, BOX, BOX), jnp.float32)
    row_spread = 10.0
    odd_factor = 1.8
    row_alternate = 1.7
    shell_scale = jnp.exp(jax.random.uniform(key_shell, (NSHELL,), jnp.float32, math.log(0.2), math.log(4.0)))
    orient_ids = jnp.arange(ORIENTS, dtype=jnp.int32)
    row_scale = jnp.power(row_spread, orient_ids.astype(jnp.float32) / max(ORIENTS - 1, 1))
    row_scale = row_scale * jnp.where(jnp.mod(orient_ids, 2) == 1, row_alternate, 1.0 / row_alternate)
    row_sq = (signed_rows[:, None] * signed_rows[:, None]).astype(jnp.float32)
    angle_part = row_sq / jnp.maximum(squared, 1).astype(jnp.float32)
    column_part = jnp.where(jnp.mod(columns, 2) == 1, odd_factor, 1.0)[None, :]
    shell_map = jnp.take(shell_scale, shells) * jnp.exp(2.0 * angle_part - 1.0) * column_part
    shell_pair = jnp.concatenate([shell_map, shell_map], axis=-1)
    scale = row_scale[:, None, None] * shell_pair[None]
    maps = (signal[None] + scale[None] * noise) / jnp.sqrt(1.0 + scale * scale)[None]
    return maps.astype(jnp.bfloat16)


def place_ends(entries, rng, low, top_value):
    longest = entries.shape.index(max(entries.shape))
    spots = []
    for shift in (0, 1):
        where = [jax.random.randint(jax.random.fold_in(rng, axis), (), 0, length) for axis, length in enumerate(entries.shape)]
        where[longest] = (where[longest] + shift) % entries.shape[longest]
        spots.append(tuple(where))
    return entries.at[spots[0]].set(low).at[spots[1]].set(top_value)


def block_scale(key, shape, shards, least, top_value):
    def one(dim, shards_of):
        heights = jax.random.uniform(jax.random.fold_in(jax.random.fold_in(key, 6), dim), (shards_of,), jnp.float32, least / len(shards), top_value / len(shards))
        return jnp.repeat(jnp.exp(heights), shape[dim] // shards_of).reshape((-1,) + (1,) * (len(shape) - dim - 1))

    gain = one(*shards[0])
    for cut in shards[1:]:
        gain = gain * one(*cut)
    return gain


def bell_draw(own_key, dims, deviation, bound, shards=(), kind=jnp.bfloat16):
    array = deviation * jax.random.normal(own_key, dims, jnp.float32)
    if shards:
        array = array * block_scale(own_key, dims, shards, -0.22, 0.18)
    return jnp.clip(array, -bound, bound).astype(kind)


def setup_inputs(seed: int = 0) -> dict:
    splits = jax.random.split(jax.random.key(seed), 8)
    return {
        "images": bell_draw(splits[0], (2, PARTICLES, BOX, 2 * KX), 1.0, 6.0, ((0, 2), (1, 16), (2, 8))),
        "orientation": draw_orientation(jax.random.fold_in(splits[7], 71), 0),
        "offsets": place_ends(jax.random.randint(splits[2], (2, PARTICLES, 2), -16, 17), jax.random.fold_in(splits[2], 1), -16, 16).astype(jnp.int32),
        "defocus_class": place_ends(jax.random.randint(splits[3], (2, PARTICLES), 0, CLASSES), jax.random.fold_in(splits[3], 1), 0, CLASSES - 1).astype(jnp.int32),
        "defocus": jnp.clip(jnp.exp(jax.random.uniform(splits[4], (CLASSES,), jnp.float32, math.log(150.0), math.log(900.0))), 150.0, 900.0),
        "ori_slot": draw_ori_slot(jax.random.fold_in(splits[7], 71), 0),
        "half_maps": draw_half_maps(jax.random.fold_in(splits[7], 71), 0),
    }


def shell_index(signed_rows, columns, shell_count):
    squared = signed_rows[:, None] * signed_rows[:, None] + columns[None, :] * columns[None, :]
    radius = jnp.floor(jnp.sqrt(squared.astype(jnp.float32))).astype(jnp.int32)
    radius = radius - (radius * radius > squared).astype(jnp.int32) + ((radius + 1) * (radius + 1) <= squared).astype(jnp.int32)
    return (jnp.clip(radius - 1, 0, shell_count - 1), squared)

def shell_sum(values, shells):
    return jax.ops.segment_sum(values.reshape(-1), shells.reshape(-1), num_segments=NSHELL)

def ctf_table(defocus, squared, box_size):
    gamma_arg = defocus[:, None, None] * (squared.astype(jnp.float32)[None] / float(box_size * box_size))
    return -(0.995 * jnp.sin(gamma_arg) + 0.1 * jnp.cos(gamma_arg))

def window_table(frequency, box_size, window_side):
    offsets_in = jnp.arange(window_side, dtype=jnp.int32) - window_side // 2
    phase_idx = jnp.mod(frequency[:, None] * offsets_in[None, :], box_size)
    angles = phase_idx.astype(jnp.float32) * (2.0 * math.pi / box_size)
    return (jnp.cos(angles), jnp.sin(angles))

def column_matrix(cos_x, sin_x):
    top_half = jnp.concatenate([cos_x, sin_x], axis=1)
    low_half = jnp.concatenate([-sin_x, cos_x], axis=1)
    return jnp.concatenate([top_half, low_half], axis=0).astype(jnp.bfloat16)

def row_matrix(cos_y, sin_y):
    return jnp.stack([cos_y, -sin_y], axis=1).astype(jnp.bfloat16)

def power_sum(left_map, right_map, half_cols):
    product = left_map * right_map
    return lax.optimization_barrier(jnp.sum(product[..., :half_cols] + product[..., half_cols:], axis=0))

def reference(images, orientation, offsets, defocus_class, defocus, ori_slot, half_maps):
    box_size = BOX
    half_cols = box_size // 2
    row_ids = jnp.arange(box_size, dtype=jnp.int32)
    signed_rows = jnp.where(row_ids < half_cols, row_ids, row_ids - box_size)
    columns = jnp.arange(half_cols, dtype=jnp.int32)
    shells, squared = shell_index(signed_rows, columns, NSHELL)
    first_map = half_maps[0].astype(jnp.float32)
    second_map = half_maps[1].astype(jnp.float32)
    cross_sum = shell_sum(power_sum(first_map, second_map, half_cols), shells)
    first_sum = shell_sum(power_sum(first_map, first_map, half_cols), shells)
    second_sum = shell_sum(power_sum(second_map, second_map, half_cols), shells)
    shell_corr = cross_sum / jnp.sqrt(first_sum * second_sum + 1e-06)
    weight = jnp.take(jnp.maximum(shell_corr, 0.1), shells)
    weight_pair = jnp.concatenate([weight, weight], axis=-1)
    ctf = ctf_table(defocus, squared, box_size)
    cos_x, sin_x = window_table(columns, box_size, SHIFTS)
    cos_y, sin_y = window_table(signed_rows, box_size, SHIFTS)
    col_table = column_matrix(cos_x, sin_x)
    row_table = row_matrix(cos_y, sin_y).astype(jnp.float32)
    block_size = math.gcd(PARTICLES, 32)
    block_count = PARTICLES // block_size
    score_list = []
    map_list = []
    for half_index in range(2):
        maps_half = half_maps[half_index]

        def block_step(carry, inputs):
            numer, ctf_sum = carry
            img_blk, ori_blk, off_blk, cls_blk = inputs
            slots = jnp.take(ori_slot, ori_blk).astype(jnp.int32)
            chosen = jnp.take(maps_half, slots, axis=0).astype(jnp.float32)
            ctf_rows = jnp.take(ctf, cls_blk, axis=0)
            img_float = img_blk.astype(jnp.float32)
            x_real = img_float[..., :half_cols]
            x_imag = img_float[..., half_cols:]
            phase_idx = jnp.mod(columns[None, None, :] * off_blk[:, 0][:, None, None] + signed_rows[None, :, None] * off_blk[:, 1][:, None, None], box_size)
            angles = phase_idx.astype(jnp.float32) * (2.0 * math.pi / box_size)
            cos_t = jnp.cos(angles)
            sin_t = jnp.sin(angles)
            al_real = x_real * cos_t + x_imag * sin_t
            al_imag = x_imag * cos_t - x_real * sin_t
            p_real = chosen[..., :half_cols]
            p_imag = chosen[..., half_cols:]
            prod_real = weight * ctf_rows * (al_real * p_real + al_imag * p_imag)
            prod_imag = weight * ctf_rows * (al_real * p_imag - al_imag * p_real)
            prod = jnp.concatenate([prod_real, prod_imag], axis=-1).astype(jnp.bfloat16)
            section = jnp.dot(prod.reshape(-1, 2 * half_cols), col_table, preferred_element_type=jnp.float32)
            section = section.astype(jnp.bfloat16).reshape(block_size, box_size, 2, SHIFTS)
            corr = jnp.einsum('nycj,yci->nji', section.astype(jnp.float32), row_table)
            energy = lax.optimization_barrier(jnp.sum(weight * ctf_rows * ctf_rows * (p_real * p_real + p_imag * p_imag), axis=(1, 2)))
            block_scores = lax.optimization_barrier(jnp.max(corr, axis=(1, 2))) / jnp.sqrt(energy + 1e-06)
            contrib = jnp.concatenate([ctf_rows * al_real, ctf_rows * al_imag], axis=-1).astype(jnp.bfloat16)
            numer = numer.at[slots].add(contrib.astype(jnp.float32))
            ctf_sum = ctf_sum.at[slots].add(ctf_rows * ctf_rows)
            return ((numer, ctf_sum), block_scores)
        init = (jnp.zeros((ORIENTS, box_size, 2 * half_cols), jnp.float32), jnp.zeros((ORIENTS, box_size, half_cols), jnp.float32))
        inputs = (images[half_index].reshape(block_count, block_size, box_size, 2 * half_cols), orientation[half_index].reshape(block_count, block_size), offsets[half_index].reshape(block_count, block_size, 2), defocus_class[half_index].reshape(block_count, block_size))
        (numer, ctf_sum), block_scores = lax.scan(block_step, init, inputs)
        ctf_pair = jnp.concatenate([ctf_sum, ctf_sum], axis=-1)
        new_half = (numer + maps_half.astype(jnp.float32) / weight_pair) / (ctf_pair + 1.0 / weight_pair)
        score_list.append(block_scores.reshape(PARTICLES))
        map_list.append(new_half)
    return (jnp.stack(score_list, axis=0), jnp.stack(map_list, axis=0), shell_corr)
```

```python
import functools
import math

import jax
import jax.numpy as jnp
import ml_dtypes
import numpy as np
from jax import lax
from jax.experimental import pallas as pl
from jax.experimental.pallas import tpu as pltpu
from jax.sharding import PartitionSpec as P

BOX = 384
KX = 192
SHIFTS = 32
NSHELL = 267
ROWS = 48
SLABS = 8
DOMS = 16
PART = 8
ORI = 32
CLASSES = 16
SLOTS = 32
SHELLS = 384
CHUNK = 4
NCHUNK = 4
F32 = jnp.float32
BF16 = jnp.bfloat16
I32 = jnp.int32
MESH = pl.DeviceIdType.MESH


def tables():
    row = np.arange(BOX)
    ky = np.where(row < KX, row, row - BOX)
    kx = np.arange(KX)
    q = ky[:, None] ** 2 + kx[None, :] ** 2
    radius = np.floor(np.sqrt(q.astype(np.float64))).astype(np.int64)
    radius -= radius * radius > q
    radius += (radius + 1) * (radius + 1) <= q
    shell = np.clip(radius - 1, 0, NSHELL - 1)
    base = np.array([0, 0, 0, 128, 128, 0, 0, 0])
    local = shell.reshape(SLABS, ROWS, KX) - base[:, None, None]
    assert local.min() >= 0 and local.max() < 256
    shell_of = np.concatenate([local, local], axis=-1).astype(np.int32)
    ends = np.zeros((SLABS, ROWS, 256), np.int32)
    for s in range(256):
        ends[:, :, s] = (local <= s).sum(-1)
    freq = np.concatenate([q, q], axis=-1).reshape(SLABS, ROWS, BOX).astype(np.float32)
    freq = freq / np.float32(BOX * BOX)
    unit = np.float32(2.0 * math.pi / BOX)

    def trig(index):
        angle = (np.mod(index, BOX).astype(np.float32) * unit).astype(np.float32)
        return np.cos(angle).astype(np.float32), np.sin(angle).astype(np.float32)

    shift = np.arange(33) - 16
    cx, sx = trig(shift[:, None] * kx[None, :])
    tx = np.zeros((33, 8, BOX), np.float32)
    tx[:, 0] = np.concatenate([cx, cx], -1)
    tx[:, 1] = np.concatenate([sx, sx], -1)
    tx[:, 2] = np.concatenate([cx, -cx], -1)
    tx[:, 3] = np.concatenate([sx, -sx], -1)
    cy, sy = trig(ky[:, None] * shift[None, :])
    ty = np.zeros((SLABS, 2, ROWS, 128), np.float32)
    ty[:, 0, :, :33] = cy.reshape(SLABS, ROWS, 33)
    ty[:, 1, :, :33] = sy.reshape(SLABS, ROWS, 33)

    window = np.arange(SHIFTS) - SHIFTS // 2
    wcx, wsx = trig(kx[:, None] * window[None, :])
    wcy, wsy = trig(ky[:, None] * window[None, :])
    col_re = np.concatenate([wcx, -wsx], axis=0)
    col_im = np.concatenate([wsx, wcx], axis=0)
    col = np.zeros((4 * BOX, 256), np.float32)
    for k in range(4):
        col[k * BOX : (k + 1) * BOX, 32 * k : 32 * k + 32] = col_re
        col[k * BOX : (k + 1) * BOX, 128 + 32 * k : 160 + 32 * k] = col_im
    wcy = wcy.reshape(SLABS, ROWS, SHIFTS).transpose(0, 2, 1)
    wsy = wsy.reshape(SLABS, ROWS, SHIFTS).transpose(0, 2, 1)
    rowt = np.concatenate([wcy, -wsy], axis=-1)
    tri = (np.arange(BOX)[:, None] % KX <= np.arange(256)[None, :]).astype(np.float32)
    bf = ml_dtypes.bfloat16
    return (
        shell_of, ends, freq, tx, ty, col.astype(bf), rowt.astype(bf), tri.astype(bf),
    )


def flip_halves(x):
    return pltpu.roll(x, KX, 1)


def ctf_rows(freq, defocus):
    g = defocus * freq
    phi = math.atan2(0.1, 0.995)
    m = jnp.floor((g + phi) * (1.0 / math.pi) + 0.5)
    t = ((g - m * 3.140625) - m * 9.67653589793e-4) + phi
    odd = m - 2.0 * jnp.floor(m * 0.5)
    t2 = t * t
    p = -1.0 / 39916800.0
    for c in (1.0 / 362880.0, -1.0 / 5040.0, 1.0 / 120.0, -1.0 / 6.0, 1.0):
        p = p * t2 + c
    scale = math.sqrt(0.995 * 0.995 + 0.01)
    return (p * t) * ((2.0 * odd - 1.0) * scale)


def split3(x):
    hi = x.astype(BF16)
    rest = x - hi.astype(F32)
    mid = rest.astype(BF16)
    low = (rest - mid.astype(F32)).astype(BF16)
    return hi, mid, low


def main_kernel(
    ori_ref, off_ref, cls_ref, defocus_ref, slot_ref,
    img_hbm, map_hbm,
    shell_hbm, ends_hbm, freq_hbm, tx_hbm, ty_hbm, col_hbm, rowt_hbm, tri_hbm,
    score_ref, corr_ref, weight_ref, contrib_hbm, ctf_hbm, meta_hbm,
    img, maps, other, shell_of, ends, freq, tx, ty, col, rowt, tri,
    packed, items, contrib, vprod, eprod, ctf, eyb, meta_out, meta_in, meta_own, meta_all,
    ar1, ar2, ar3, arx, prod, part, parts_in, ret, ret_out,
    load_sem, map_send, map_recv, img_send, img_recv, meta_send, meta_recv, own_sem,
    ar1_send, ar1_recv, ar2_send, ar2_recv, ar3_send, ar3_recv,
    part_send, part_recv, ret_send, ret_recv, out_sem,
):
    h = lax.axis_index("half")
    d = lax.axis_index("dom")
    z = lax.axis_index("slab")
    y = d // 4
    q = d % 4

    def remote(src, dst, send, recv, where):
        return pltpu.make_async_remote_copy(
            src_ref=src, dst_ref=dst, send_sem=send, recv_sem=recv,
            device_id=where, device_id_type=MESH,
        )

    loads = [
        (map_hbm, maps), (img_hbm, img), (freq_hbm.at[z], freq), (ty_hbm.at[z], ty),
        (tx_hbm, tx), (tri_hbm, tri), (ends_hbm.at[z], ends), (shell_hbm.at[z], shell_of),
        (col_hbm, col), (rowt_hbm.at[z], rowt),
    ]
    loads = [pltpu.make_async_copy(a, b, load_sem.at[i]) for i, (a, b) in enumerate(loads)]
    for c in loads:
        c.start()
    (ld_map, ld_img, ld_freq, ld_ty, ld_tx, ld_tri, ld_ends, ld_shell, ld_col, ld_rowt) = loads

    barrier = pltpu.get_barrier_semaphore()
    pl.semaphore_signal(barrier, inc=1, device_id={"half": 1 - h}, device_id_type=MESH)
    for r in range(1, DOMS):
        pl.semaphore_signal(barrier, inc=1, device_id={"dom": (d + r) % DOMS}, device_id_type=MESH)
    for r in range(1, 4):
        pl.semaphore_signal(
            barrier, inc=1, device_id={"half": 1 - h, "dom": y * 4 + (q + r) % 4}, device_id_type=MESH
        )
    for r in range(1, SLABS):
        pl.semaphore_signal(barrier, inc=1, device_id={"slab": (z + r) % SLABS}, device_id_type=MESH)

    lane1 = lax.broadcasted_iota(I32, (1, 128), 1)
    owner_row = lax.broadcasted_iota(I32, (DOMS, 128), 0)
    lane16 = lax.broadcasted_iota(I32, (DOMS, 128), 1)
    owners = []
    ranks = []
    message = jnp.zeros((DOMS, 128), I32)
    for p in range(PART):
        place = slot_ref[ori_ref[p]]
        owner = place // ORI
        rank = jnp.int32(0)
        for before in owners:
            rank = rank + jnp.where(before == owner, 1, 0)
        owners.append(owner)
        ranks.append(rank)
        fields = (cls_ref[p], off_ref[p, 0] + 16, off_ref[p, 1] + 16, place % ORI, jnp.int32(1), jnp.int32(p))
        at = lane16 - 8 * rank
        for f, value in enumerate(fields):
            message = jnp.where((owner_row == owner) & (at == f), value, message)
    for o in range(DOMS):
        meta_out[o] = message[o : o + 1]
    own_copy = pltpu.make_async_copy(meta_out, meta_own, own_sem.at[0])
    own_copy.start()

    pl.semaphore_wait(barrier, 1 + (DOMS - 1) + 3 + (SLABS - 1))

    map_copies = []
    for c in range(NCHUNK):
        source = map_hbm.at[pl.ds((1 - h) * (ORI // 2) + c * CHUNK, CHUNK)]
        copy = remote(
            source, other.at[pl.ds(c * CHUNK, CHUNK)], map_send.at[c], map_recv.at[c], {"half": 1 - h}
        )
        copy.start()
        map_copies.append(copy)

    meta_copies = []
    for r in range(1, DOMS):
        o = (d + r) % DOMS
        copy = remote(meta_out.at[o], meta_in.at[d], meta_send.at[r], meta_recv.at[d], {"dom": o})
        copy.start()
        meta_copies.append(copy)
    own_copy.wait()
    ld_img.wait()

    def pack(o, carry):
        for e in range(2):
            packed[o, e] = img[meta_own[o, 0, 8 * e + 5]]
        return carry

    lax.fori_loop(0, DOMS, pack, 0)
    img_copies = []
    for r in range(1, DOMS):
        o = (d + r) % DOMS
        copy = remote(packed.at[o], items.at[d], img_send.at[r], img_recv.at[d], {"dom": o})
        copy.start()
        img_copies.append(copy)
    self_img = pltpu.make_async_copy(packed.at[d], items.at[d], own_sem.at[1])
    self_img.start()
    self_meta = pltpu.make_async_copy(meta_out.at[d], meta_in.at[d], own_sem.at[2])
    self_meta.start()

    ld_freq.wait()

    def one_class(k, carry):
        ctf[k] = ctf_rows(freq[...], defocus_ref[k])
        return carry

    lax.fori_loop(0, CLASSES, one_class, 0)
    ctf_out = pltpu.make_async_copy(ctf, ctf_hbm, out_sem.at[0])
    ctf_out.start()
    ld_ty.wait()
    for part_of in range(2):
        for s in range(33):
            eyb[s, part_of] = jnp.broadcast_to(ty[part_of, :, s : s + 1], (ROWS, 128))

    ld_map.wait()

    def own_power(i, total):
        m = maps[i].astype(F32)
        return total + m * m

    own_sq = lax.fori_loop(0, ORI, own_power, jnp.zeros((ROWS, BOX), F32))
    cross = jnp.zeros((ROWS, BOX), F32)
    for c in range(NCHUNK):
        map_copies[c].wait_recv()

        def cross_term(i, total):
            mine = maps[h * (ORI // 2) + c * CHUNK + i].astype(F32)
            return total + mine * other[c * CHUNK + i].astype(F32)

        cross = lax.fori_loop(0, CHUNK, cross_term, cross)

    ld_tri.wait()
    ld_ends.wait()
    pieces = jnp.concatenate(list(split3(cross)) + list(split3(own_sq)), axis=0)
    running = jnp.dot(pieces, tri[...], preferred_element_type=F32)
    lane = lax.broadcasted_iota(I32, (1, 128), 1)
    sums = []
    for v in range(2):
        o = 3 * ROWS * v
        c = running[o : o + ROWS] + (running[o + ROWS : o + 2 * ROWS] + running[o + 2 * ROWS : o + 3 * ROWS])
        blocks = []
        for b in range(2):
            e = ends[:, 128 * b : 128 * b + 128]
            low = jnp.take_along_axis(c[:, :128], jnp.clip(e - 1, 0, 127), axis=1)
            high = jnp.take_along_axis(c[:, 128:], jnp.clip(e - 129, 0, 127), axis=1)
            got = jnp.where(e > 128, high, jnp.where(e > 0, low, 0.0))
            blocks.append(jnp.sum(got, axis=0, keepdims=True))
        first = blocks[0] - jnp.where(lane == 0, 0.0, pltpu.roll(blocks[0], 1, 1))
        carry_in = jnp.where(lane == 0, blocks[0][:, 127:128], pltpu.roll(blocks[1], 1, 1))
        sums.append((first, blocks[1] - carry_in))
    shifted = (z == 3) | (z == 4)
    sub = lax.broadcasted_iota(I32, (8, 128), 0)
    for b in range(3):
        rows = []
        for v in range(2):
            s0, s1 = sums[v]
            zero = jnp.zeros((1, 128), F32)
            plain = (s0, s1, zero)[b]
            moved = (zero, s0, s1)[b]
            rows.append(jnp.where(shifted, moved, plain))
        block = jnp.where(sub == 0, rows[0], jnp.where(sub == 1 + h, rows[1], 0.0))
        arx[0, :, 128 * b : 128 * b + 128] = block

    g = h * 4 + q
    ar1_copies = []
    for r in range(1, 8):
        to = (g + r) % 8
        copy = remote(
            arx.at[0], ar1.at[g], ar1_send.at[r], ar1_recv.at[g], {"half": to // 4, "dom": y * 4 + to % 4}
        )
        copy.start()
        ar1_copies.append(copy)

    for r in range(1, DOMS):
        s = (d + r) % DOMS
        remote(meta_out.at[s], meta_in.at[s], meta_send.at[r], meta_recv.at[s], {"dom": s}).wait_recv()
    self_meta.wait()
    to_smem = pltpu.make_async_copy(meta_in, meta_all, own_sem.at[3])
    to_smem.start()
    meta_save = pltpu.make_async_copy(meta_in, meta_hbm, out_sem.at[1])
    meta_save.start()
    ld_tx.wait()
    for r in range(1, DOMS):
        s = (d + r) % DOMS
        remote(packed.at[s], items.at[s], img_send.at[r], img_recv.at[s], {"dom": s}).wait_recv()
    self_img.wait()
    to_smem.wait()
    low_half = lax.broadcasted_iota(I32, (ROWS, BOX), 1) < KX

    def one_item(n, carry):
        b = n // 2
        at = 8 * (n % 2)
        phase_x = tx[meta_all[b, 0, at + 1]]
        phase_y = eyb[meta_all[b, 0, at + 2]]
        cy = jnp.concatenate([phase_y[0]] * 3, axis=1)
        sy = jnp.concatenate([phase_y[1]] * 3, axis=1)
        cos_t = phase_x[0:1] * cy - phase_x[1:2] * sy
        sin_t = phase_x[3:4] * cy + phase_x[2:3] * sy
        x = items[b, n % 2].astype(F32)
        c = ctf[meta_all[b, 0, at]] * meta_all[b, 0, at + 4].astype(F32)
        zz = c * (x * cos_t + flip_halves(x) * sin_t)
        contrib[n] = zz.astype(BF16)
        m = maps[meta_all[b, 0, at + 3]].astype(F32)
        straight = zz * m
        crossed = zz * flip_halves(m)
        vprod[n] = jnp.where(low_half, straight, -crossed) + flip_halves(
            jnp.where(low_half, crossed, straight)
        )
        cm = c * m
        eprod[n] = cm * cm
        return carry

    lax.fori_loop(0, 12, one_item, 0)
    total = arx[0]
    for r in range(1, 8):
        s = (g + r) % 8
        remote(
            arx.at[0], ar1.at[s], ar1_send.at[r], ar1_recv.at[s], {"half": s // 4, "dom": y * 4 + s % 4}
        ).wait_recv()
        total = total + ar1[s]
    arx[1] = total
    ar2_copies = []
    for r in range(1, 4):
        to = (y + r) % 4
        copy = remote(arx.at[1], ar2.at[y], ar2_send.at[r], ar2_recv.at[y], {"dom": to * 4 + q})
        copy.start()
        ar2_copies.append(copy)
    lax.fori_loop(12, 22, one_item, 0)
    for r in range(1, 4):
        s = (y + r) % 4
        remote(arx.at[1], ar2.at[s], ar2_send.at[r], ar2_recv.at[s], {"dom": s * 4 + q}).wait_recv()
        total = total + ar2[s]
    arx[2] = total
    ar3_copies = []
    for r in range(1, SLABS):
        to = (z + r) % SLABS
        copy = remote(arx.at[2], ar3.at[z], ar3_send.at[r], ar3_recv.at[z], {"slab": to})
        copy.start()
        ar3_copies.append(copy)
    lax.fori_loop(22, SLOTS, one_item, 0)
    contrib_out = pltpu.make_async_copy(contrib, contrib_hbm, out_sem.at[2])
    contrib_out.start()
    ar3[z] = total
    for r in range(1, SLABS):
        s = (z + r) % SLABS
        remote(arx.at[2], ar3.at[s], ar3_send.at[r], ar3_recv.at[s], {"slab": s}).wait_recv()
    total = ar3[0]
    for s in range(1, SLABS):
        total = total + ar3[s]

    fsc = total[0:1] / jnp.sqrt(total[1:2] * total[2:3] + 1e-06)
    corr_ref[...] = fsc
    floor = jnp.maximum(fsc, 0.1)
    table0 = jnp.where(shifted, floor[:, 128:256], floor[:, 0:128])
    table1 = jnp.where(shifted, floor[:, 256:384], floor[:, 128:256])
    table0 = jnp.broadcast_to(table0, (ROWS, 128))
    table1 = jnp.broadcast_to(table1, (ROWS, 128))
    ld_shell.wait()
    for b in range(3):
        at = shell_of[:, 128 * b : 128 * b + 128]
        low = jnp.take_along_axis(table0, jnp.minimum(at, 127), axis=1)
        high = jnp.take_along_axis(table1, jnp.maximum(at - 128, 0), axis=1)
        weight_ref[:, 128 * b : 128 * b + 128] = jnp.where(at < 128, low, high)
    w = weight_ref[...]

    def weigh(t, carry):
        for k in range(4):
            prod[t, :, BOX * k : BOX * k + BOX] = (vprod[4 * t + k] * w).astype(BF16)
            e = jnp.sum(eprod[4 * t + k] * w, axis=0, keepdims=True)
            part[t, 32 + k : 33 + k, :] = e[:, 0:128] + e[:, 128:256] + e[:, 256:384]
        return carry

    lax.fori_loop(0, SLABS, weigh, 0)
    ld_col.wait()
    ld_rowt.wait()
    section = jnp.dot(
        prod[...].reshape(SLABS * ROWS, 4 * BOX), col[...], preferred_element_type=F32
    ).astype(BF16)
    stacked = jnp.concatenate(
        [
            jnp.concatenate(
                [section[ROWS * t : ROWS * t + ROWS, :128], section[ROWS * t : ROWS * t + ROWS, 128:]], axis=0
            )
            for t in range(SLABS)
        ],
        axis=1,
    )
    partial = jnp.dot(rowt[...], stacked, preferred_element_type=F32)
    for t in range(SLABS):
        part[t, 0:32, :] = partial[:, 128 * t : 128 * t + 128]

    part_copies = []
    for r in range(1, SLABS):
        to = (z + r) % SLABS
        copy = remote(part.at[to], parts_in.at[z], part_send.at[r], part_recv.at[z], {"slab": to})
        copy.start()
        part_copies.append(copy)
    whole = part[z]
    for r in range(1, SLABS):
        s = (z + r) % SLABS
        remote(part.at[s], parts_in.at[s], part_send.at[r], part_recv.at[s], {"slab": s}).wait_recv()
        whole = whole + parts_in[s]
    best = jnp.max(whole[0:32], axis=0, keepdims=True)
    answer = jnp.zeros((1, 128), F32)
    for k in range(4):
        top = jnp.max(jnp.where(lane1 // 32 == k, best, -jnp.inf), axis=1, keepdims=True)
        energy = jnp.sum(whole[32 + k : 33 + k], axis=1, keepdims=True)
        answer = jnp.where(lane1 == k, top / jnp.sqrt(energy + 1e-06), answer)
    ret_out[...] = answer

    for e in range(2):
        for r in range(SLABS):
            holder = 2 * z + e
            to = (z + r) % SLABS
            copy = remote(
                ret_out, ret.at[d], ret_send.at[8 * e + r], ret_recv.at[d], {"dom": holder, "slab": to}
            )
            if r == 0:
                pl.when(holder != d)(copy.start)
            else:
                copy.start()

    @pl.when(d // 2 == z)
    def _():
        ret[d] = answer

    for r in range(DOMS):
        s = (d + r) % DOMS
        copy = remote(ret_out, ret.at[s], ret_send.at[r], ret_recv.at[s], {"dom": s, "slab": d // 2})
        if r == 0:
            pl.when(d // 2 != z)(copy.wait_recv)
        else:
            copy.wait_recv()
    scores = jnp.zeros((1, 128), F32)
    for p in range(PART):
        row = ret[owners[p]]
        value = jnp.sum(jnp.where(lane1 == 2 * (d % 2) + ranks[p], row, 0.0), axis=1, keepdims=True)
        scores = jnp.where(lane1 == p, value, scores)
    score_ref[...] = scores[:, :PART]

    for copy in map_copies + meta_copies + img_copies + ar1_copies + ar2_copies + ar3_copies + part_copies:
        copy.wait_send()
    for e in range(2):
        for r in range(SLABS):
            holder = 2 * z + e
            to = (z + r) % SLABS
            copy = remote(
                ret_out, ret.at[d], ret_send.at[8 * e + r], ret_recv.at[d], {"dom": holder, "slab": to}
            )
            if r == 0:
                pl.when(holder != d)(copy.wait_send)
            else:
                copy.wait_send()
    ctf_out.wait()
    meta_save.wait()
    contrib_out.wait()


def run_main(orientation, offsets, classes, defocus, slots, images, maps, consts):
    smem = pl.BlockSpec(memory_space=pltpu.SMEM)
    hbm = pl.BlockSpec(memory_space=pl.ANY)
    vmem = pl.BlockSpec(memory_space=pltpu.VMEM)
    v = pltpu.VMEM
    dma = pltpu.SemaphoreType.DMA
    return pl.pallas_call(
        main_kernel,
        out_shape=(
            jax.ShapeDtypeStruct((1, PART), F32),
            jax.ShapeDtypeStruct((1, SHELLS), F32),
            jax.ShapeDtypeStruct((ROWS, BOX), F32),
            jax.ShapeDtypeStruct((SLOTS, ROWS, BOX), BF16),
            jax.ShapeDtypeStruct((CLASSES, ROWS, BOX), F32),
            jax.ShapeDtypeStruct((DOMS, 1, 128), I32),
        ),
        in_specs=[smem] * 5 + [hbm] * 10,
        out_specs=(vmem, vmem, vmem, hbm, hbm, hbm),
        scratch_shapes=[
            v((PART, ROWS, BOX), BF16),
            v((ORI, ROWS, BOX), BF16),
            v((ORI // 2, ROWS, BOX), BF16),
            v((ROWS, BOX), I32),
            v((ROWS, 256), I32),
            v((ROWS, BOX), F32),
            v((33, 8, BOX), F32),
            v((2, ROWS, 128), F32),
            v((4 * BOX, 256), BF16),
            v((SHIFTS, 2 * ROWS), BF16),
            v((BOX, 256), BF16),
            v((DOMS, 2, ROWS, BOX), BF16),
            v((DOMS, 2, ROWS, BOX), BF16),
            v((SLOTS, ROWS, BOX), BF16),
            v((SLOTS, ROWS, BOX), F32),
            v((SLOTS, ROWS, BOX), F32),
            v((CLASSES, ROWS, BOX), F32),
            v((33, 2, ROWS, 128), F32),
            v((DOMS, 1, 128), I32),
            v((DOMS, 1, 128), I32),
            pltpu.SMEM((DOMS, 1, 128), I32),
            pltpu.SMEM((DOMS, 1, 128), I32),
            v((8, 8, SHELLS), F32),
            v((4, 8, SHELLS), F32),
            v((8, 8, SHELLS), F32),
            v((3, 8, SHELLS), F32),
            v((SLABS, ROWS, 4 * BOX), BF16),
            v((SLABS, 40, 128), F32),
            v((SLABS, 40, 128), F32),
            v((DOMS, 1, 128), F32),
            v((1, 128), F32),
            dma((10,)),
            dma((NCHUNK,)), dma((NCHUNK,)),
            dma((DOMS,)), dma((DOMS,)),
            dma((DOMS,)), dma((DOMS,)),
            dma((4,)),
            dma((8,)), dma((8,)),
            dma((4,)), dma((4,)),
            dma((8,)), dma((8,)),
            dma((8,)), dma((8,)),
            dma((16,)), dma((16,)),
            dma((3,)),
        ],
        compiler_params=pltpu.CompilerParams(
            collective_id=0, has_side_effects=True, vmem_limit_bytes=48 * 1024 * 1024
        ),
        name="refine",
    )(orientation, offsets, classes, defocus, slots, images, maps, *consts)


STRIP = 16


def maps_kernel(meta, contrib, maps, ctf, weight, out, bottom):
    w = weight[...]
    inverse = 1.0 / w

    def init(r, carry):
        out[r] = maps[r].astype(F32) * inverse
        bottom[r] = inverse
        return carry

    lax.fori_loop(0, ORI, init, 0)

    def add(n, carry):
        b = n // 2
        at = 8 * (n % 2)

        @pl.when(meta[b, at + 4] != 0)
        def _():
            row = meta[b, at + 3]
            c = ctf[meta[b, at]]
            out[row] += contrib[n].astype(F32)
            bottom[row] += c * c

        return carry

    lax.fori_loop(0, SLOTS, add, 0)

    def finish(r, carry):
        out[r] = out[r] / bottom[r]
        return carry

    lax.fori_loop(0, ORI, finish, 0)


def run_maps(meta, contrib, maps, ctf, weight):
    def block(count):
        return pl.BlockSpec((count, STRIP, BOX), lambda i: (0, i, 0))

    return pl.pallas_call(
        maps_kernel,
        grid=(ROWS // STRIP,),
        out_shape=jax.ShapeDtypeStruct((ORI, ROWS, BOX), F32),
        in_specs=[
            pl.BlockSpec(memory_space=pltpu.SMEM),
            block(SLOTS), block(ORI), block(CLASSES),
            pl.BlockSpec((STRIP, BOX), lambda i: (i, 0)),
        ],
        out_specs=block(ORI),
        scratch_shapes=[pltpu.VMEM((ORI, STRIP, BOX), F32)],
        compiler_params=pltpu.CompilerParams(vmem_limit_bytes=32 * 1024 * 1024),
        name="new_maps",
    )(meta, contrib, maps, ctf, weight)


def on_device(consts, images, orientation, offsets, defocus_class, defocus, ori_slot, half_maps):
    scores, fsc, weight, contrib, ctf, meta = run_main(
        orientation[0], offsets[0], defocus_class[0], defocus, ori_slot, images[0], half_maps[0], consts
    )
    new_maps = run_maps(meta[:, 0], contrib, half_maps[0], ctf, weight)
    return scores, new_maps[None], fsc[0, :NSHELL]


def solution(mesh):
    in_specs = (
        P("half", "dom", "slab", None),
        P("half", "dom"),
        P("half", "dom", None),
        P("half", "dom"),
        P(),
        P(),
        P("half", "dom", "slab", None),
    )
    out_specs = (P("half", "dom"), P("half", "dom", "slab", None), P())
    return jax.shard_map(
        functools.partial(on_device, tables()),
        mesh=mesh, in_specs=in_specs, out_specs=out_specs, check_vma=False,
    )
```

```python
import functools
import math

import jax
import jax.numpy as jnp
import ml_dtypes
import numpy as np
from jax import lax
from jax.experimental import pallas as pl
from jax.experimental.pallas import tpu as pltpu
from jax.sharding import PartitionSpec as P

BOX = 384
KX = 192
SHIFTS = 32
NSHELL = 267
ROWS = 48
SLABS = 8
DOMS = 16
PART = 8
ORI = 32
CLASSES = 16
SLOTS = 32
SHELLS = 384
CHUNK = 4
NCHUNK = 4
F32 = jnp.float32
BF16 = jnp.bfloat16
I32 = jnp.int32
MESH = pl.DeviceIdType.MESH
FAR8 = (4, 3, 5, 2, 6, 1, 7)
NEAR8 = FAR8[::-1]
FAR4 = (2, 1, 3)
NEAR4 = FAR4[::-1]


def tables():
    row = np.arange(BOX)
    ky = np.where(row < KX, row, row - BOX)
    kx = np.arange(KX)
    q = ky[:, None] ** 2 + kx[None, :] ** 2
    radius = np.floor(np.sqrt(q.astype(np.float64))).astype(np.int64)
    radius -= radius * radius > q
    radius += (radius + 1) * (radius + 1) <= q
    shell = np.clip(radius - 1, 0, NSHELL - 1)
    base = np.array([0, 0, 0, 128, 128, 0, 0, 0])
    local = shell.reshape(SLABS, ROWS, KX) - base[:, None, None]
    assert local.min() >= 0 and local.max() < 256
    shell_of = np.concatenate([local, local], axis=-1).astype(np.int32)
    ends = np.zeros((SLABS, ROWS, 256), np.int32)
    for s in range(256):
        ends[:, :, s] = (local <= s).sum(-1)
    freq = np.concatenate([q, q], axis=-1).reshape(SLABS, ROWS, BOX).astype(np.float32)
    freq = freq / np.float32(BOX * BOX)
    unit = np.float32(2.0 * math.pi / BOX)

    def trig(index):
        angle = (np.mod(index, BOX).astype(np.float32) * unit).astype(np.float32)
        return np.cos(angle).astype(np.float32), np.sin(angle).astype(np.float32)

    shift = np.arange(33) - 16
    cx, sx = trig(shift[:, None] * kx[None, :])
    tx = np.zeros((33, 8, BOX), np.float32)
    tx[:, 0] = np.concatenate([cx, cx], -1)
    tx[:, 1] = np.concatenate([sx, sx], -1)
    tx[:, 2] = np.concatenate([cx, -cx], -1)
    tx[:, 3] = np.concatenate([sx, -sx], -1)
    cy, sy = trig(ky[:, None] * shift[None, :])
    ty = np.zeros((SLABS, 2, ROWS, 128), np.float32)
    ty[:, 0, :, :33] = cy.reshape(SLABS, ROWS, 33)
    ty[:, 1, :, :33] = sy.reshape(SLABS, ROWS, 33)

    window = np.arange(SHIFTS) - SHIFTS // 2
    wcx, wsx = trig(kx[:, None] * window[None, :])
    wcy, wsy = trig(ky[:, None] * window[None, :])
    col_re = np.concatenate([wcx, -wsx], axis=0)
    col_im = np.concatenate([wsx, wcx], axis=0)
    col = np.zeros((4 * BOX, 256), np.float32)
    for k in range(4):
        col[k * BOX : (k + 1) * BOX, 32 * k : 32 * k + 32] = col_re
        col[k * BOX : (k + 1) * BOX, 128 + 32 * k : 160 + 32 * k] = col_im
    wcy = wcy.reshape(SLABS, ROWS, SHIFTS).transpose(0, 2, 1)
    wsy = wsy.reshape(SLABS, ROWS, SHIFTS).transpose(0, 2, 1)
    rowt = np.concatenate([wcy, -wsy], axis=-1)
    tri = (np.arange(BOX)[:, None] % KX <= np.arange(256)[None, :]).astype(np.float32)
    bf = ml_dtypes.bfloat16
    return (
        shell_of, ends, freq, tx, ty, col.astype(bf), rowt.astype(bf), tri.astype(bf),
    )


def flip_halves(x):
    return pltpu.roll(x, KX, 1)


def ctf_rows(freq, defocus):
    g = defocus * freq
    phi = math.atan2(0.1, 0.995)
    m = jnp.floor((g + phi) * (1.0 / math.pi) + 0.5)
    t = ((g - m * 3.140625) - m * 9.67653589793e-4) + phi
    odd = m - 2.0 * jnp.floor(m * 0.5)
    t2 = t * t
    p = -1.0 / 39916800.0
    for c in (1.0 / 362880.0, -1.0 / 5040.0, 1.0 / 120.0, -1.0 / 6.0, 1.0):
        p = p * t2 + c
    scale = math.sqrt(0.995 * 0.995 + 0.01)
    return (p * t) * ((2.0 * odd - 1.0) * scale)


def split3(x):
    hi = x.astype(BF16)
    rest = x - hi.astype(F32)
    mid = rest.astype(BF16)
    low = (rest - mid.astype(F32)).astype(BF16)
    return hi, mid, low


def main_kernel(
    ori_hbm, off_hbm, cls_hbm, defocus_hbm, slot_hbm, img_hbm, map_hbm,
    shell_hbm, ends_hbm, freq_hbm, tx_hbm, ty_hbm, col_hbm, rowt_hbm, tri_hbm,
    score_ref, corr_ref, new_ref,
    ori_ref, off_ref, cls_ref, defocus_ref, slot_ref,
    img, maps, other, shell_of, ends, freq, tx, ty, col, rowt, tri, weight_ref,
    packed, stage, regular, extra, contrib, vprod, eprod, ctf, eyb,
    meta_out, meta_stage, meta_in, meta_own, meta_all, link_v, link,
    ar1, ar2, ar3, arx, prod, part, parts_in, ret, ret_out,
    load_sem, own_sem, ring_sem, map_send, map_recv,
    img1_send, img1_recv, img2_send, img2_recv, ext_send, ext_recv,
    meta1_send, meta1_recv, meta2_send, meta2_recv,
    ar1_send, ar1_recv, ar2_send, ar2_recv, ar3_send, ar3_recv,
    part_send, part_recv, ret_send, ret_recv,
):
    h = lax.axis_index("half")
    d = lax.axis_index("dom")
    z = lax.axis_index("slab")
    y = d // 4
    q = d % 4
    g = h * 4 + q

    def flip(bits):
        hi = (q // 2 + bits // 2) % 2
        lo = (q % 2 + bits % 2) % 2
        return hi * 2 + lo

    def remote(src, dst, send, recv, where):
        return pltpu.make_async_remote_copy(
            src_ref=src, dst_ref=dst, send_sem=send, recv_sem=recv,
            device_id=where, device_id_type=MESH,
        )

    def signal(sem, where):
        pl.semaphore_signal(sem, inc=1, device_id=where, device_id_type=MESH)

    barrier = pltpu.get_barrier_semaphore()
    for r in FAR8:
        to = (g + r) % 8
        signal(barrier, {"half": to // 4, "dom": y * 4 + to % 4})
    for r in FAR4:
        signal(barrier, {"dom": (y + r) % 4 * 4 + q})
    for r in (1, SLABS - 1):
        signal(barrier, {"slab": (z + r) % SLABS})

    loads = [
        (ori_hbm, ori_ref), (off_hbm, off_ref), (cls_hbm, cls_ref), (slot_hbm, slot_ref),
        (defocus_hbm, defocus_ref), (img_hbm, img), (freq_hbm.at[z], freq), (ty_hbm.at[z], ty),
        (map_hbm, maps), (tri_hbm, tri), (ends_hbm.at[z], ends), (tx_hbm, tx),
        (shell_hbm.at[z], shell_of), (col_hbm, col), (rowt_hbm.at[z], rowt),
    ]
    loads = [pltpu.make_async_copy(a, b, load_sem.at[i]) for i, (a, b) in enumerate(loads)]
    for c in loads:
        c.start()
    ld_small = loads[:4]
    (ld_defocus, ld_img, ld_freq, ld_ty, ld_map, ld_tri, ld_ends, ld_tx, ld_shell, ld_col, ld_rowt) = loads[4:]

    for c in ld_small:
        c.wait()
    lane1 = lax.broadcasted_iota(I32, (1, 128), 1)
    owner_row = lax.broadcasted_iota(I32, (DOMS, 128), 0)
    lane16 = lax.broadcasted_iota(I32, (DOMS, 128), 1)
    owners = []
    ranks = []
    second = jnp.int32(0)
    message = jnp.zeros((DOMS, 128), I32)
    for p in range(PART):
        place = slot_ref[ori_ref[p]]
        owner = place // ORI
        rank = jnp.int32(0)
        for before in owners:
            rank = rank + jnp.where(before == owner, 1, 0)
        owners.append(owner)
        ranks.append(rank)
        second = jnp.where(rank == 1, p, second)
        fields = (cls_ref[p], off_ref[0, p] + 16, off_ref[1, p] + 16, place % ORI, jnp.int32(1), jnp.int32(p))
        at = lane16 - 8 * rank
        for f, value in enumerate(fields):
            message = jnp.where((owner_row == owner) & (at == f), value, message)
    for o in range(DOMS):
        meta_out[o // 4, o % 4] = message[o : o + 1]
    own_copy = pltpu.make_async_copy(meta_out, meta_own, own_sem.at[0])
    own_copy.start()

    pl.semaphore_wait(barrier, 7 + 3 + 2)

    map_copies = []
    for c in range(NCHUNK):
        source = map_hbm.at[pl.ds((1 - h) * (ORI // 2) + c * CHUNK, CHUNK)]
        copy = remote(
            source, other.at[pl.ds(c * CHUNK, CHUNK)], map_send.at[c], map_recv.at[c], {"half": 1 - h}
        )
        copy.start()
        map_copies.append(copy)
    copies = list(map_copies)

    def ring(k):
        for r in (1, SLABS - 1):
            signal(ring_sem.at[k], {"slab": (z + r) % SLABS})

    ring(0)

    for r in FAR4:
        to = (y + r) % 4
        copy = remote(
            meta_out.at[to], meta_stage.at[:, y], meta1_send.at[r], meta1_recv.at[y], {"dom": to * 4 + q}
        )
        copy.start()
        copies.append(copy)
    own_copy.wait()
    ld_img.wait()

    def pack(o, carry):
        packed[o // 4, o % 4] = img[meta_own[o // 4, o % 4, 0, 5]]
        return carry

    lax.fori_loop(0, DOMS, pack, 0)
    for t in range(4):
        packed[t, 4] = img[second]
    for r in FAR4:
        to = (y + r) % 4
        copy = remote(packed.at[to], stage.at[:, y], img1_send.at[r], img1_recv.at[y], {"dom": to * 4 + q})
        copy.start()
        copies.append(copy)
    own_img = pltpu.make_async_copy(packed.at[y], stage.at[:, y], own_sem.at[1])
    own_img.start()
    own_meta = pltpu.make_async_copy(meta_out.at[y], meta_stage.at[:, y], own_sem.at[2])
    own_meta.start()
    pl.semaphore_wait(ring_sem.at[0], 2)
    ring(1)

    ld_freq.wait()
    ld_defocus.wait()

    def one_class(k, carry):
        ctf[k] = ctf_rows(freq[...], defocus_ref[k])
        return carry

    lax.fori_loop(0, CLASSES, one_class, 0)
    pl.semaphore_wait(ring_sem.at[1], 2)
    ring(2)
    ld_ty.wait()
    for part_of in range(2):
        for s in range(33):
            eyb[s, part_of] = jnp.broadcast_to(ty[part_of, :, s : s + 1], (ROWS, 128))

    for r in FAR4:
        s = (y + r) % 4
        remote(meta_out.at[s], meta_stage.at[:, s], meta1_send.at[r], meta1_recv.at[s], {"dom": s * 4 + q}).wait_recv()
    own_meta.wait()
    for bits in (3, 2, 1):
        to = flip(bits)
        copy = remote(
            meta_stage.at[to], meta_in.at[q], meta2_send.at[bits], meta2_recv.at[q], {"dom": y * 4 + to}
        )
        copy.start()
        copies.append(copy)
    last_meta = pltpu.make_async_copy(meta_stage.at[q], meta_in.at[q], own_sem.at[3])
    last_meta.start()

    ld_map.wait()

    def own_power(i, total):
        m = maps[i].astype(F32)
        return total + m * m

    own_sq = lax.fori_loop(0, ORI, own_power, jnp.zeros((ROWS, BOX), F32))
    pl.semaphore_wait(ring_sem.at[2], 2)
    cross = jnp.zeros((ROWS, BOX), F32)
    for c in range(NCHUNK):
        if c == NCHUNK - 1:
            for r in FAR4:
                s = (y + r) % 4
                remote(
                    packed.at[s], stage.at[:, s], img1_send.at[r], img1_recv.at[s], {"dom": s * 4 + q}
                ).wait_recv()
            own_img.wait()
            for kind, (src, dst, send, recv) in enumerate(
                ((stage.at[4], extra, ext_send, ext_recv), (stage.at[flip(1)], regular, img2_send, img2_recv))
            ):
                copy = remote(src, dst.at[q], send.at[1], recv.at[q], {"dom": y * 4 + flip(1)})
                copy.start()
                copies.append(copy)
            own_regular = pltpu.make_async_copy(stage.at[q], regular.at[q], own_sem.at[4])
            own_regular.start()
            own_extra = pltpu.make_async_copy(stage.at[4], extra.at[q], own_sem.at[5])
            own_extra.start()
        map_copies[c].wait_recv()

        def cross_term(i, total):
            mine = maps[h * (ORI // 2) + c * CHUNK + i].astype(F32)
            return total + mine * other[c * CHUNK + i].astype(F32)

        cross = lax.fori_loop(0, CHUNK, cross_term, cross)

    copy = remote(stage.at[4], extra.at[q], ext_send.at[2], ext_recv.at[q], {"dom": y * 4 + flip(2)})
    copy.start()
    copies.append(copy)
    for bits in (2, 3):
        to = flip(bits)
        copy = remote(stage.at[to], regular.at[q], img2_send.at[bits], img2_recv.at[q], {"dom": y * 4 + to})
        copy.start()
        copies.append(copy)

    ld_tri.wait()
    ld_ends.wait()
    pieces = jnp.concatenate(list(split3(cross)) + list(split3(own_sq)), axis=0)
    running = jnp.dot(pieces, tri[...], preferred_element_type=F32)
    lane = lax.broadcasted_iota(I32, (1, 128), 1)
    sums = []
    for v in range(2):
        o = 3 * ROWS * v
        c = running[o : o + ROWS] + (running[o + ROWS : o + 2 * ROWS] + running[o + 2 * ROWS : o + 3 * ROWS])
        blocks = []
        for b in range(2):
            e = ends[:, 128 * b : 128 * b + 128]
            low = jnp.take_along_axis(c[:, :128], jnp.clip(e - 1, 0, 127), axis=1)
            high = jnp.take_along_axis(c[:, 128:], jnp.clip(e - 129, 0, 127), axis=1)
            got = jnp.where(e > 128, high, jnp.where(e > 0, low, 0.0))
            blocks.append(jnp.sum(got, axis=0, keepdims=True))
        first = blocks[0] - jnp.where(lane == 0, 0.0, pltpu.roll(blocks[0], 1, 1))
        carry_in = jnp.where(lane == 0, blocks[0][:, 127:128], pltpu.roll(blocks[1], 1, 1))
        sums.append((first, blocks[1] - carry_in))
    shifted = (z == 3) | (z == 4)
    sub = lax.broadcasted_iota(I32, (8, 128), 0)
    for b in range(3):
        rows = []
        for v in range(2):
            s0, s1 = sums[v]
            zero = jnp.zeros((1, 128), F32)
            plain = (s0, s1, zero)[b]
            moved = (zero, s0, s1)[b]
            rows.append(jnp.where(shifted, moved, plain))
        block = jnp.where(sub == 0, rows[0], jnp.where(sub == 1 + h, rows[1], 0.0))
        arx[0, :, 128 * b : 128 * b + 128] = block

    for r in FAR8:
        to = (g + r) % 8
        copy = remote(
            arx.at[0], ar1.at[g], ar1_send.at[r], ar1_recv.at[g], {"half": to // 4, "dom": y * 4 + to % 4}
        )
        copy.start()
        copies.append(copy)

    last_meta.wait()
    for bits in (1, 2, 3):
        s = flip(bits)
        remote(meta_stage.at[s], meta_in.at[s], meta2_send.at[bits], meta2_recv.at[s], {"dom": y * 4 + s}).wait_recv()
    to_smem = pltpu.make_async_copy(meta_in, meta_all, own_sem.at[6])
    to_smem.start()

    numbers = jnp.concatenate([meta_in[c, t] for c in range(4) for t in range(4)], axis=0).astype(F32)

    def field(f):
        return jnp.sum(jnp.where(lane16 == f, numbers, 0.0), axis=1, keepdims=True)

    key = jnp.concatenate(
        [jnp.where(field(8 * e + 4) > 0.5, field(8 * e + 3), -1.0) for e in range(2)], axis=0
    )
    item_lane = lax.broadcasted_iota(I32, (SLOTS, 128), 1)
    item_row = lax.broadcasted_iota(I32, (SLOTS, 128), 0)
    across = jnp.sum(jnp.where(item_lane == item_row, key, 0.0), axis=0, keepdims=True)
    where_f = item_lane.astype(F32)
    last = jnp.max(
        jnp.where((across == item_row.astype(F32)) & (item_lane < SLOTS), where_f, -1.0), axis=1, keepdims=True
    )
    same = (across == key) & (item_lane < item_row) & (key >= 0.0)
    previous = jnp.max(jnp.where(same, where_f, -1.0), axis=1, keepdims=True)
    link_v[...] = jnp.where(item_lane == 0, last, jnp.where(item_lane == 1, previous, 0.0)).astype(I32)
    link_copy = pltpu.make_async_copy(link_v, link, own_sem.at[7])
    link_copy.start()

    ld_tx.wait()
    own_regular.wait()
    own_extra.wait()
    to_smem.wait()
    low_half = lax.broadcasted_iota(I32, (ROWS, BOX), 1) < KX

    def items_of(source, column, e):
        def one_item(t, carry):
            at = 8 * e
            phase_x = tx[meta_all[column, t, 0, at + 1]]
            phase_y = eyb[meta_all[column, t, 0, at + 2]]
            cy = jnp.concatenate([phase_y[0]] * 3, axis=1)
            sy = jnp.concatenate([phase_y[1]] * 3, axis=1)
            cos_t = phase_x[0:1] * cy - phase_x[1:2] * sy
            sin_t = phase_x[3:4] * cy + phase_x[2:3] * sy
            x = source[column, t].astype(F32)
            c = ctf[meta_all[column, t, 0, at]] * meta_all[column, t, 0, at + 4].astype(F32)
            zz = c * (x * cos_t + flip_halves(x) * sin_t)
            contrib[16 * e + 4 * column + t] = zz.astype(BF16)
            m = maps[meta_all[column, t, 0, at + 3]].astype(F32)
            straight = zz * m
            crossed = zz * flip_halves(m)
            n = 2 * (4 * t + column) + e
            vprod[n] = jnp.where(low_half, straight, -crossed) + flip_halves(
                jnp.where(low_half, crossed, straight)
            )
            cm = c * m
            eprod[n] = cm * cm
            return carry

        lax.fori_loop(0, 4, one_item, 0)

    def wait_regular(bits):
        s = flip(bits)
        remote(
            stage.at[s], regular.at[s], img2_send.at[bits], img2_recv.at[s], {"dom": y * 4 + s}
        ).wait_recv()

    def wait_extra(bits):
        s = flip(bits)
        remote(stage.at[4], extra.at[s], ext_send.at[bits], ext_recv.at[s], {"dom": y * 4 + s}).wait_recv()

    items_of(regular, q, 0)
    items_of(extra, q, 1)
    total = arx[0]
    for r in NEAR8:
        s = (g + r) % 8
        remote(
            arx.at[0], ar1.at[s], ar1_send.at[r], ar1_recv.at[s], {"half": s // 4, "dom": y * 4 + s % 4}
        ).wait_recv()
        total = total + ar1[s]
    arx[1] = total
    for r in FAR4:
        to = (y + r) % 4
        copy = remote(arx.at[1], ar2.at[y], ar2_send.at[r], ar2_recv.at[y], {"dom": to * 4 + q})
        copy.start()
        copies.append(copy)
    wait_extra(1)
    items_of(extra, flip(1), 1)
    wait_regular(1)
    items_of(regular, flip(1), 0)
    for r in NEAR4:
        s = (y + r) % 4
        remote(arx.at[1], ar2.at[s], ar2_send.at[r], ar2_recv.at[s], {"dom": s * 4 + q}).wait_recv()
        total = total + ar2[s]
    arx[2] = total
    for r in FAR8:
        to = (z + r) % SLABS
        copy = remote(arx.at[2], ar3.at[z], ar3_send.at[r], ar3_recv.at[z], {"slab": to})
        copy.start()
        copies.append(copy)
    wait_extra(2)
    copy = remote(
        extra.at[flip(2)], extra.at[flip(2)], ext_send.at[3], ext_recv.at[flip(2)], {"dom": y * 4 + flip(1)}
    )
    copy.start()
    copies.append(copy)
    items_of(extra, flip(2), 1)
    wait_regular(2)
    items_of(regular, flip(2), 0)
    wait_extra(3)
    items_of(extra, flip(3), 1)
    wait_regular(3)
    items_of(regular, flip(3), 0)
    ar3[z] = total
    for r in NEAR8:
        s = (z + r) % SLABS
        remote(arx.at[2], ar3.at[s], ar3_send.at[r], ar3_recv.at[s], {"slab": s}).wait_recv()
    total = ar3[0]
    for s in range(1, SLABS):
        total = total + ar3[s]

    fsc = total[0:1] / jnp.sqrt(total[1:2] * total[2:3] + 1e-06)
    corr_ref[...] = fsc
    floor = jnp.maximum(fsc, 0.1)
    table0 = jnp.where(shifted, floor[:, 128:256], floor[:, 0:128])
    table1 = jnp.where(shifted, floor[:, 256:384], floor[:, 128:256])
    table0 = jnp.broadcast_to(table0, (ROWS, 128))
    table1 = jnp.broadcast_to(table1, (ROWS, 128))
    ld_shell.wait()
    for b in range(3):
        at = shell_of[:, 128 * b : 128 * b + 128]
        low = jnp.take_along_axis(table0, jnp.minimum(at, 127), axis=1)
        high = jnp.take_along_axis(table1, jnp.maximum(at - 128, 0), axis=1)
        weight_ref[:, 128 * b : 128 * b + 128] = jnp.where(at < 128, low, high)
    w = weight_ref[...]

    def weigh(t, carry):
        for k in range(4):
            prod[t, :, BOX * k : BOX * k + BOX] = (vprod[4 * t + k] * w).astype(BF16)
            e = jnp.sum(eprod[4 * t + k] * w, axis=0, keepdims=True)
            part[t, 32 + k : 33 + k, :] = e[:, 0:128] + e[:, 128:256] + e[:, 256:384]
        return carry

    lax.fori_loop(0, SLABS, weigh, 0)
    ld_col.wait()
    ld_rowt.wait()
    section = jnp.dot(
        prod[...].reshape(SLABS * ROWS, 4 * BOX), col[...], preferred_element_type=F32
    ).astype(BF16)
    stacked = jnp.concatenate(
        [
            jnp.concatenate(
                [section[ROWS * t : ROWS * t + ROWS, :128], section[ROWS * t : ROWS * t + ROWS, 128:]], axis=0
            )
            for t in range(SLABS)
        ],
        axis=1,
    )
    partial = jnp.dot(rowt[...], stacked, preferred_element_type=F32)
    for t in range(SLABS):
        part[t, 0:32, :] = partial[:, 128 * t : 128 * t + 128]

    for r in FAR8:
        to = (z + r) % SLABS
        copy = remote(part.at[to], parts_in.at[z], part_send.at[r], part_recv.at[z], {"slab": to})
        copy.start()
        copies.append(copy)

    link_copy.wait()

    def add_item(u, carry):
        e = u // 16
        before = link[u, 1]
        has = jnp.where(before >= 0, 1.0, 0.0)
        from_u = jnp.minimum(jnp.maximum(before, 0), SLOTS - 1)
        column = (u % 16) // 4
        t = u % 4
        c = ctf[meta_all[column, t, 0, 8 * e]]
        valid = meta_all[column, t, 0, 8 * e + 4].astype(F32)
        vprod[u] = contrib[u].astype(F32) + has * vprod[from_u]
        eprod[u] = (c * c) * valid + has * eprod[from_u]
        return carry

    lax.fori_loop(0, SLOTS, add_item, 0)
    whole = part[z]
    for r in NEAR8:
        s = (z + r) % SLABS
        remote(part.at[s], parts_in.at[s], part_send.at[r], part_recv.at[s], {"slab": s}).wait_recv()
        whole = whole + parts_in[s]
    best = jnp.max(whole[0:32], axis=0, keepdims=True)
    answer = jnp.zeros((1, 128), F32)
    for k in range(4):
        top = jnp.max(jnp.where(lane1 // 32 == k, best, -jnp.inf), axis=1, keepdims=True)
        energy = jnp.sum(whole[32 + k : 33 + k], axis=1, keepdims=True)
        answer = jnp.where(lane1 == k, top / jnp.sqrt(energy + 1e-06), answer)
    ret_out[...] = answer

    def score_copy(e, r):
        return remote(
            ret_out, ret.at[d], ret_send.at[8 * e + r], ret_recv.at[d],
            {"dom": 2 * z + e, "slab": (z + r) % SLABS},
        )

    for r in FAR8:
        for e in range(2):
            score_copy(e, r).start()
    for e in range(2):
        pl.when(2 * z + e != d)(score_copy(e, 0).start)

    @pl.when(d // 2 == z)
    def _():
        ret[d] = answer

    def one_slice(r, carry):
        at = link[r, 0]
        has = jnp.where(at >= 0, 1.0, 0.0)
        at = jnp.minimum(jnp.maximum(at, 0), SLOTS - 1)
        inverse = 1.0 / weight_ref[...]
        top = has * vprod[at] + maps[r].astype(F32) * inverse
        new_ref[r] = top / (has * eprod[at] + inverse)
        return carry

    lax.fori_loop(0, ORI, one_slice, 0)

    for r in range(DOMS):
        s = (d + r) % DOMS
        copy = remote(ret_out, ret.at[s], ret_send.at[r], ret_recv.at[s], {"dom": s, "slab": d // 2})
        if r == 0:
            pl.when(d // 2 != z)(copy.wait_recv)
        else:
            copy.wait_recv()
    scores = jnp.zeros((1, 128), F32)
    for p in range(PART):
        row = ret[owners[p]]
        value = jnp.sum(jnp.where(lane1 == 2 * (d % 2) + ranks[p], row, 0.0), axis=1, keepdims=True)
        scores = jnp.where(lane1 == p, value, scores)
    score_ref[...] = scores[:, :PART]

    for copy in copies:
        copy.wait_send()
    for e in range(2):
        for r in FAR8:
            score_copy(e, r).wait_send()
        pl.when(2 * z + e != d)(score_copy(e, 0).wait_send)


def run_main(*operands):
    hbm = pl.BlockSpec(memory_space=pltpu.HBM)
    vmem = pl.BlockSpec(memory_space=pltpu.VMEM)
    v = pltpu.VMEM
    smem = pltpu.SMEM
    dma = pltpu.SemaphoreType.DMA
    return pl.pallas_call(
        main_kernel,
        out_shape=(
            jax.ShapeDtypeStruct((1, PART), F32),
            jax.ShapeDtypeStruct((1, SHELLS), F32),
            jax.ShapeDtypeStruct((ORI, ROWS, BOX), F32),
        ),
        in_specs=[hbm] * 15,
        out_specs=(vmem, vmem, vmem),
        scratch_shapes=[
            smem((PART,), I32), smem((2, PART), I32), smem((PART,), I32), smem((CLASSES,), F32),
            smem((512,), I32),
            v((PART, ROWS, BOX), BF16),
            v((ORI, ROWS, BOX), BF16),
            v((ORI // 2, ROWS, BOX), BF16),
            v((ROWS, BOX), I32),
            v((ROWS, 256), I32),
            v((ROWS, BOX), F32),
            v((33, 8, BOX), F32),
            v((2, ROWS, 128), F32),
            v((4 * BOX, 256), BF16),
            v((SHIFTS, 2 * ROWS), BF16),
            v((BOX, 256), BF16),
            v((ROWS, BOX), F32),
            v((4, 5, ROWS, BOX), BF16),
            v((5, 4, ROWS, BOX), BF16),
            v((4, 4, ROWS, BOX), BF16),
            v((4, 4, ROWS, BOX), BF16),
            v((SLOTS, ROWS, BOX), BF16),
            v((SLOTS, ROWS, BOX), F32),
            v((SLOTS, ROWS, BOX), F32),
            v((CLASSES, ROWS, BOX), F32),
            v((33, 2, ROWS, 128), F32),
            v((4, 4, 1, 128), I32),
            v((4, 4, 1, 128), I32),
            v((4, 4, 1, 128), I32),
            smem((4, 4, 1, 128), I32),
            smem((4, 4, 1, 128), I32),
            v((SLOTS, 128), I32),
            smem((SLOTS, 128), I32),
            v((8, 8, SHELLS), F32),
            v((4, 8, SHELLS), F32),
            v((8, 8, SHELLS), F32),
            v((3, 8, SHELLS), F32),
            v((SLABS, ROWS, 4 * BOX), BF16),
            v((SLABS, 40, 128), F32),
            v((SLABS, 40, 128), F32),
            v((DOMS, 1, 128), F32),
            v((1, 128), F32),
            dma((15,)),
            dma((8,)),
            pltpu.SemaphoreType.REGULAR((3,)),
            dma((NCHUNK,)), dma((NCHUNK,)),
            dma((4,)), dma((4,)),
            dma((4,)), dma((4,)),
            dma((4,)), dma((4,)),
            dma((4,)), dma((4,)),
            dma((4,)), dma((4,)),
            dma((8,)), dma((8,)),
            dma((4,)), dma((4,)),
            dma((8,)), dma((8,)),
            dma((8,)), dma((8,)),
            dma((16,)), dma((16,)),
        ],
        compiler_params=pltpu.CompilerParams(
            collective_id=0, has_side_effects=True, vmem_limit_bytes=60 * 1024 * 1024
        ),
        name="refine",
    )(*operands)


def on_device(consts, images, orientation, offsets, defocus_class, defocus, ori_slot, half_maps):
    scores, fsc, new_maps = run_main(
        orientation[0], offsets[0].T, defocus_class[0], defocus, ori_slot, images[0], half_maps[0], *consts
    )
    return scores, new_maps[None], fsc[0, :NSHELL]


def solution(mesh):
    in_specs = (
        P("half", "dom", "slab", None),
        P("half", "dom"),
        P("half", "dom", None),
        P("half", "dom"),
        P(),
        P(),
        P("half", "dom", "slab", None),
    )
    out_specs = (P("half", "dom"), P("half", "dom", "slab", None), P())
    return jax.shard_map(
        functools.partial(on_device, tables()),
        mesh=mesh, in_specs=in_specs, out_specs=out_specs, check_vma=False,
    )
```

```python
import functools
import math

import jax
import jax.numpy as jnp
import ml_dtypes
import numpy as np
from jax import lax
from jax.experimental import pallas as pl
from jax.experimental.pallas import tpu as pltpu
from jax.sharding import PartitionSpec as P

BOX = 384
KX = 192
SHIFTS = 32
NSHELL = 267
ROWS = 48
SLABS = 8
DOMS = 16
PART = 8
ORI = 32
CLASSES = 16
SLOTS = 32
SHELLS = 384
CHUNK = 4
NCHUNK = 4
F32 = jnp.float32
BF16 = jnp.bfloat16
I32 = jnp.int32
MESH = pl.DeviceIdType.MESH
FAR8 = (4, 3, 5, 2, 6, 1, 7)
NEAR8 = FAR8[::-1]
FAR4 = (2, 1, 3)
NEAR4 = FAR4[::-1]


def tables():
    row = np.arange(BOX)
    ky = np.where(row < KX, row, row - BOX)
    kx = np.arange(KX)
    q = ky[:, None] ** 2 + kx[None, :] ** 2
    radius = np.floor(np.sqrt(q.astype(np.float64))).astype(np.int64)
    radius -= radius * radius > q
    radius += (radius + 1) * (radius + 1) <= q
    shell = np.clip(radius - 1, 0, NSHELL - 1)
    base = np.array([0, 0, 0, 128, 128, 0, 0, 0])
    local = shell.reshape(SLABS, ROWS, KX) - base[:, None, None]
    assert local.min() >= 0 and local.max() < 256
    shell_of = np.concatenate([local, local], axis=-1).astype(np.int32)
    ends = np.zeros((SLABS, ROWS, 256), np.int32)
    for s in range(256):
        ends[:, :, s] = (local <= s).sum(-1)
    freq = np.concatenate([q, q], axis=-1).reshape(SLABS, ROWS, BOX).astype(np.float32)
    freq = freq / np.float32(BOX * BOX)
    unit = np.float32(2.0 * math.pi / BOX)

    def trig(index):
        angle = (np.mod(index, BOX).astype(np.float32) * unit).astype(np.float32)
        return np.cos(angle).astype(np.float32), np.sin(angle).astype(np.float32)

    shift = np.arange(33) - 16
    cx, sx = trig(shift[:, None] * kx[None, :])
    tx = np.zeros((33, 8, BOX), np.float32)
    tx[:, 0] = np.concatenate([cx, cx], -1)
    tx[:, 1] = np.concatenate([sx, sx], -1)
    tx[:, 2] = np.concatenate([cx, -cx], -1)
    tx[:, 3] = np.concatenate([sx, -sx], -1)
    cy, sy = trig(ky[:, None] * shift[None, :])
    ty = np.zeros((SLABS, 2, ROWS, 128), np.float32)
    ty[:, 0, :, :33] = cy.reshape(SLABS, ROWS, 33)
    ty[:, 1, :, :33] = sy.reshape(SLABS, ROWS, 33)

    window = np.arange(SHIFTS) - SHIFTS // 2
    wcx, wsx = trig(kx[:, None] * window[None, :])
    wcy, wsy = trig(ky[:, None] * window[None, :])
    col_re = np.concatenate([wcx, -wsx], axis=0)
    col_im = np.concatenate([wsx, wcx], axis=0)
    col = np.zeros((4 * BOX, 256), np.float32)
    for k in range(4):
        col[k * BOX : (k + 1) * BOX, 32 * k : 32 * k + 32] = col_re
        col[k * BOX : (k + 1) * BOX, 128 + 32 * k : 160 + 32 * k] = col_im
    wcy = wcy.reshape(SLABS, ROWS, SHIFTS).transpose(0, 2, 1)
    wsy = wsy.reshape(SLABS, ROWS, SHIFTS).transpose(0, 2, 1)
    rowt = np.concatenate([wcy, -wsy], axis=-1)
    tri = (np.arange(BOX)[:, None] % KX <= np.arange(256)[None, :]).astype(np.float32)
    bf = ml_dtypes.bfloat16
    return (
        shell_of, ends, freq, tx, ty, col.astype(bf), rowt.astype(bf), tri.astype(bf),
    )


def flip_halves(x):
    return pltpu.roll(x, KX, 1)


def ctf_rows(freq, defocus):
    g = defocus * freq
    phi = math.atan2(0.1, 0.995)
    m = jnp.floor((g + phi) * (1.0 / math.pi) + 0.5)
    t = ((g - m * 3.140625) - m * 9.67653589793e-4) + phi
    odd = m - 2.0 * jnp.floor(m * 0.5)
    t2 = t * t
    p = -1.0 / 39916800.0
    for c in (1.0 / 362880.0, -1.0 / 5040.0, 1.0 / 120.0, -1.0 / 6.0, 1.0):
        p = p * t2 + c
    scale = math.sqrt(0.995 * 0.995 + 0.01)
    return (p * t) * ((2.0 * odd - 1.0) * scale)


def split3(x):
    hi = x.astype(BF16)
    rest = x - hi.astype(F32)
    mid = rest.astype(BF16)
    low = (rest - mid.astype(F32)).astype(BF16)
    return hi, mid, low


def main_kernel(
    ori_hbm, off_hbm, cls_hbm, defocus_hbm, slot_hbm, img_hbm, map_hbm,
    shell_hbm, ends_hbm, freq_hbm, tx_hbm, ty_hbm, col_hbm, rowt_hbm, tri_hbm,
    score_ref, corr_ref, new_hbm,
    ori_ref, off_ref, cls_ref, defocus_ref, slot_ref,
    img, maps, other, shell_of, ends, freq, tx, ty, col, rowt, tri, weight_ref,
    packed, stage, regular, extra, contrib, vprod, eprod, ctf, eyb,
    meta_out, meta_stage, meta_in, meta_own, meta_all, link_v, link,
    new_ref, ar1, ar2, ar3, arx, prod, part, parts_in, ret, ret_out,
    load_sem, own_sem, ring_sem, map_send, map_recv,
    img1_send, img1_recv, img2_send, img2_recv, ext_send, ext_recv,
    meta1_send, meta1_recv, meta2_send, meta2_recv,
    ar1_send, ar1_recv, ar2_send, ar2_recv, ar3_send, ar3_recv,
    part_send, part_recv, ret_send, ret_recv, new_sem,
):
    h = lax.axis_index("half")
    d = lax.axis_index("dom")
    z = lax.axis_index("slab")
    y = d // 4
    q = d % 4
    g = h * 4 + q

    def flip(bits):
        hi = (q // 2 + bits // 2) % 2
        lo = (q % 2 + bits % 2) % 2
        return hi * 2 + lo

    def remote(src, dst, send, recv, where):
        return pltpu.make_async_remote_copy(
            src_ref=src, dst_ref=dst, send_sem=send, recv_sem=recv,
            device_id=where, device_id_type=MESH,
        )

    def signal(sem, where):
        pl.semaphore_signal(sem, inc=1, device_id=where, device_id_type=MESH)

    barrier = pltpu.get_barrier_semaphore()
    for r in FAR8:
        to = (g + r) % 8
        signal(barrier, {"half": to // 4, "dom": y * 4 + to % 4})
    for r in FAR4:
        signal(barrier, {"dom": (y + r) % 4 * 4 + q})
    for r in (1, SLABS - 1):
        signal(barrier, {"slab": (z + r) % SLABS})

    loads = [
        (ori_hbm, ori_ref), (off_hbm, off_ref), (cls_hbm, cls_ref), (slot_hbm, slot_ref),
        (defocus_hbm, defocus_ref), (img_hbm, img), (freq_hbm.at[z], freq), (ty_hbm.at[z], ty),
        (map_hbm, maps), (tri_hbm, tri), (ends_hbm.at[z], ends), (tx_hbm, tx),
        (shell_hbm.at[z], shell_of), (col_hbm, col), (rowt_hbm.at[z], rowt),
    ]
    loads = [pltpu.make_async_copy(a, b, load_sem.at[i]) for i, (a, b) in enumerate(loads)]
    for c in loads:
        c.start()
    ld_small = loads[:4]
    (ld_defocus, ld_img, ld_freq, ld_ty, ld_map, ld_tri, ld_ends, ld_tx, ld_shell, ld_col, ld_rowt) = loads[4:]

    for c in ld_small:
        c.wait()
    lane1 = lax.broadcasted_iota(I32, (1, 128), 1)
    owner_row = lax.broadcasted_iota(I32, (DOMS, 128), 0)
    lane16 = lax.broadcasted_iota(I32, (DOMS, 128), 1)
    owners = []
    ranks = []
    second = jnp.int32(0)
    message = jnp.zeros((DOMS, 128), I32)
    for p in range(PART):
        place = slot_ref[ori_ref[p]]
        owner = place // ORI
        rank = jnp.int32(0)
        for before in owners:
            rank = rank + jnp.where(before == owner, 1, 0)
        owners.append(owner)
        ranks.append(rank)
        second = jnp.where(rank == 1, p, second)
        fields = (cls_ref[p], off_ref[0, p] + 16, off_ref[1, p] + 16, place % ORI, jnp.int32(1), jnp.int32(p))
        at = lane16 - 8 * rank
        for f, value in enumerate(fields):
            message = jnp.where((owner_row == owner) & (at == f), value, message)
    for o in range(DOMS):
        meta_out[o // 4, o % 4] = message[o : o + 1]
    own_copy = pltpu.make_async_copy(meta_out, meta_own, own_sem.at[0])
    own_copy.start()

    pl.semaphore_wait(barrier, 7 + 3 + 2)

    map_copies = []
    for c in range(NCHUNK):
        source = map_hbm.at[pl.ds((1 - h) * (ORI // 2) + c * CHUNK, CHUNK)]
        copy = remote(
            source, other.at[pl.ds(c * CHUNK, CHUNK)], map_send.at[c], map_recv.at[c], {"half": 1 - h}
        )
        copy.start()
        map_copies.append(copy)
    copies = list(map_copies)

    def ring(k):
        for r in (1, SLABS - 1):
            signal(ring_sem.at[k], {"slab": (z + r) % SLABS})

    ring(0)

    for r in FAR4:
        to = (y + r) % 4
        copy = remote(
            meta_out.at[to], meta_stage.at[:, y], meta1_send.at[r], meta1_recv.at[y], {"dom": to * 4 + q}
        )
        copy.start()
        copies.append(copy)
    own_copy.wait()
    ld_img.wait()

    def pack(o, carry):
        packed[o // 4, o % 4] = img[meta_own[o // 4, o % 4, 0, 5]]
        return carry

    lax.fori_loop(0, DOMS, pack, 0)
    for t in range(4):
        packed[t, 4] = img[second]
    for r in FAR4:
        to = (y + r) % 4
        copy = remote(packed.at[to], stage.at[:, y], img1_send.at[r], img1_recv.at[y], {"dom": to * 4 + q})
        copy.start()
        copies.append(copy)
    own_img = pltpu.make_async_copy(packed.at[y], stage.at[:, y], own_sem.at[1])
    own_img.start()
    own_meta = pltpu.make_async_copy(meta_out.at[y], meta_stage.at[:, y], own_sem.at[2])
    own_meta.start()
    pl.semaphore_wait(ring_sem.at[0], 2)
    ring(1)

    ld_freq.wait()
    ld_defocus.wait()

    def one_class(k, carry):
        ctf[k] = ctf_rows(freq[...], defocus_ref[k])
        return carry

    lax.fori_loop(0, CLASSES, one_class, 0)
    pl.semaphore_wait(ring_sem.at[1], 2)
    ring(2)
    ld_ty.wait()
    for part_of in range(2):
        for s in range(33):
            eyb[s, part_of] = jnp.broadcast_to(ty[part_of, :, s : s + 1], (ROWS, 128))

    for r in FAR4:
        s = (y + r) % 4
        remote(meta_out.at[s], meta_stage.at[:, s], meta1_send.at[r], meta1_recv.at[s], {"dom": s * 4 + q}).wait_recv()
    own_meta.wait()
    for bits in (3, 2, 1):
        to = flip(bits)
        copy = remote(
            meta_stage.at[to], meta_in.at[q], meta2_send.at[bits], meta2_recv.at[q], {"dom": y * 4 + to}
        )
        copy.start()
        copies.append(copy)
    last_meta = pltpu.make_async_copy(meta_stage.at[q], meta_in.at[q], own_sem.at[3])
    last_meta.start()

    ld_map.wait()

    def own_power(i, total):
        m = maps[i].astype(F32)
        return total + m * m

    own_sq = lax.fori_loop(0, ORI, own_power, jnp.zeros((ROWS, BOX), F32))
    pl.semaphore_wait(ring_sem.at[2], 2)
    cross = jnp.zeros((ROWS, BOX), F32)
    for c in range(NCHUNK):
        if c == NCHUNK - 1:
            for r in FAR4:
                s = (y + r) % 4
                remote(
                    packed.at[s], stage.at[:, s], img1_send.at[r], img1_recv.at[s], {"dom": s * 4 + q}
                ).wait_recv()
            own_img.wait()
            for kind, (src, dst, send, recv) in enumerate(
                ((stage.at[4], extra, ext_send, ext_recv), (stage.at[flip(1)], regular, img2_send, img2_recv))
            ):
                copy = remote(src, dst.at[q], send.at[1], recv.at[q], {"dom": y * 4 + flip(1)})
                copy.start()
                copies.append(copy)
            own_regular = pltpu.make_async_copy(stage.at[q], regular.at[q], own_sem.at[4])
            own_regular.start()
            own_extra = pltpu.make_async_copy(stage.at[4], extra.at[q], own_sem.at[5])
            own_extra.start()
        map_copies[c].wait_recv()

        def cross_term(i, total):
            mine = maps[h * (ORI // 2) + c * CHUNK + i].astype(F32)
            return total + mine * other[c * CHUNK + i].astype(F32)

        cross = lax.fori_loop(0, CHUNK, cross_term, cross)

    copy = remote(stage.at[4], extra.at[q], ext_send.at[2], ext_recv.at[q], {"dom": y * 4 + flip(2)})
    copy.start()
    copies.append(copy)
    for bits in (2, 3):
        to = flip(bits)
        copy = remote(stage.at[to], regular.at[q], img2_send.at[bits], img2_recv.at[q], {"dom": y * 4 + to})
        copy.start()
        copies.append(copy)

    ld_tri.wait()
    ld_ends.wait()
    pieces = jnp.concatenate(list(split3(cross)) + list(split3(own_sq)), axis=0)
    running = jnp.dot(pieces, tri[...], preferred_element_type=F32)
    lane = lax.broadcasted_iota(I32, (1, 128), 1)
    sums = []
    for v in range(2):
        o = 3 * ROWS * v
        c = running[o : o + ROWS] + (running[o + ROWS : o + 2 * ROWS] + running[o + 2 * ROWS : o + 3 * ROWS])
        blocks = []
        for b in range(2):
            e = ends[:, 128 * b : 128 * b + 128]
            low = jnp.take_along_axis(c[:, :128], jnp.clip(e - 1, 0, 127), axis=1)
            high = jnp.take_along_axis(c[:, 128:], jnp.clip(e - 129, 0, 127), axis=1)
            got = jnp.where(e > 128, high, jnp.where(e > 0, low, 0.0))
            blocks.append(jnp.sum(got, axis=0, keepdims=True))
        first = blocks[0] - jnp.where(lane == 0, 0.0, pltpu.roll(blocks[0], 1, 1))
        carry_in = jnp.where(lane == 0, blocks[0][:, 127:128], pltpu.roll(blocks[1], 1, 1))
        sums.append((first, blocks[1] - carry_in))
    shifted = (z == 3) | (z == 4)
    zero = jnp.zeros((1, 128), F32)
    for v in range(3):
        s0, s1 = sums[min(v, 1)]
        for b in range(3):
            block = jnp.where(shifted, (zero, s0, s1)[b], (s0, s1, zero)[b])
            if v > 0:
                block = jnp.where(h == v - 1, block, zero)
            arx[0, :, SHELLS * v + 128 * b : SHELLS * v + 128 * b + 128] = block

    for r in FAR8:
        to = (z + r) % SLABS
        copy = remote(arx.at[0], ar1.at[z], ar1_send.at[r], ar1_recv.at[z], {"slab": to})
        copy.start()
        copies.append(copy)

    last_meta.wait()
    for bits in (1, 2, 3):
        s = flip(bits)
        remote(meta_stage.at[s], meta_in.at[s], meta2_send.at[bits], meta2_recv.at[s], {"dom": y * 4 + s}).wait_recv()
    to_smem = pltpu.make_async_copy(meta_in, meta_all, own_sem.at[6])
    to_smem.start()

    numbers = jnp.concatenate([meta_in[c, t] for c in range(4) for t in range(4)], axis=0).astype(F32)

    def field(f):
        return jnp.sum(jnp.where(lane16 == f, numbers, 0.0), axis=1, keepdims=True)

    key = jnp.concatenate(
        [jnp.where(field(8 * e + 4) > 0.5, field(8 * e + 3), -1.0) for e in range(2)], axis=0
    )
    item_lane = lax.broadcasted_iota(I32, (SLOTS, 128), 1)
    item_row = lax.broadcasted_iota(I32, (SLOTS, 128), 0)
    across = jnp.sum(jnp.where(item_lane == item_row, key, 0.0), axis=0, keepdims=True)
    where_f = item_lane.astype(F32)
    last = jnp.max(
        jnp.where((across == item_row.astype(F32)) & (item_lane < SLOTS), where_f, -1.0), axis=1, keepdims=True
    )
    same = (across == key) & (item_lane < item_row) & (key >= 0.0)
    previous = jnp.max(jnp.where(same, where_f, -1.0), axis=1, keepdims=True)
    link_v[...] = jnp.where(item_lane == 0, last, jnp.where(item_lane == 1, previous, 0.0)).astype(I32)
    link_copy = pltpu.make_async_copy(link_v, link, own_sem.at[7])
    link_copy.start()

    ld_tx.wait()
    own_regular.wait()
    own_extra.wait()
    to_smem.wait()
    low_half = lax.broadcasted_iota(I32, (ROWS, BOX), 1) < KX

    def items_of(source, column, e):
        def one_item(t, carry):
            at = 8 * e
            phase_x = tx[meta_all[column, t, 0, at + 1]]
            phase_y = eyb[meta_all[column, t, 0, at + 2]]
            cy = jnp.concatenate([phase_y[0]] * 3, axis=1)
            sy = jnp.concatenate([phase_y[1]] * 3, axis=1)
            cos_t = phase_x[0:1] * cy - phase_x[1:2] * sy
            sin_t = phase_x[3:4] * cy + phase_x[2:3] * sy
            x = source[column, t].astype(F32)
            c = ctf[meta_all[column, t, 0, at]] * meta_all[column, t, 0, at + 4].astype(F32)
            zz = c * (x * cos_t + flip_halves(x) * sin_t)
            contrib[16 * e + 4 * column + t] = zz.astype(BF16)
            m = maps[meta_all[column, t, 0, at + 3]].astype(F32)
            straight = zz * m
            crossed = zz * flip_halves(m)
            n = 2 * (4 * t + column) + e
            vprod[n] = jnp.where(low_half, straight, -crossed) + flip_halves(
                jnp.where(low_half, crossed, straight)
            )
            cm = c * m
            eprod[n] = cm * cm
            return carry

        lax.fori_loop(0, 4, one_item, 0)

    def wait_regular(bits):
        s = flip(bits)
        remote(
            stage.at[s], regular.at[s], img2_send.at[bits], img2_recv.at[s], {"dom": y * 4 + s}
        ).wait_recv()

    def wait_extra(bits):
        s = flip(bits)
        remote(stage.at[4], extra.at[s], ext_send.at[bits], ext_recv.at[s], {"dom": y * 4 + s}).wait_recv()

    items_of(regular, q, 0)
    items_of(extra, q, 1)
    wait_extra(1)
    items_of(extra, flip(1), 1)
    ar1[z] = arx[0]
    for r in NEAR8:
        s = (z + r) % SLABS
        remote(arx.at[0], ar1.at[s], ar1_send.at[r], ar1_recv.at[s], {"slab": s}).wait_recv()
    total = ar1[0]
    for s in range(1, SLABS):
        total = total + ar1[s]
    arx[1] = total
    for r in FAR4:
        to = (y + r) % 4
        copy = remote(arx.at[1], ar2.at[y], ar2_send.at[r], ar2_recv.at[y], {"dom": to * 4 + q})
        copy.start()
        copies.append(copy)
    wait_regular(1)
    items_of(regular, flip(1), 0)
    wait_extra(2)
    copy = remote(
        extra.at[flip(2)], extra.at[flip(2)], ext_send.at[3], ext_recv.at[flip(2)], {"dom": y * 4 + flip(1)}
    )
    copy.start()
    copies.append(copy)
    ar2[y] = total
    for r in NEAR4:
        s = (y + r) % 4
        remote(arx.at[1], ar2.at[s], ar2_send.at[r], ar2_recv.at[s], {"dom": s * 4 + q}).wait_recv()
    total = ar2[0]
    for s in range(1, 4):
        total = total + ar2[s]
    arx[2] = total
    for r in FAR8:
        to = (g + r) % 8
        copy = remote(
            arx.at[2], ar3.at[g], ar3_send.at[r], ar3_recv.at[g], {"half": to // 4, "dom": y * 4 + to % 4}
        )
        copy.start()
        copies.append(copy)
    items_of(extra, flip(2), 1)
    wait_regular(2)
    items_of(regular, flip(2), 0)
    wait_extra(3)
    items_of(extra, flip(3), 1)
    wait_regular(3)
    items_of(regular, flip(3), 0)
    ar3[g] = total
    for r in NEAR8:
        s = (g + r) % 8
        remote(
            arx.at[2], ar3.at[s], ar3_send.at[r], ar3_recv.at[s], {"half": s // 4, "dom": y * 4 + s % 4}
        ).wait_recv()
    total = ar3[0]
    for s in range(1, 8):
        total = total + ar3[s]

    power = total[:, SHELLS : 2 * SHELLS] * total[:, 2 * SHELLS : 3 * SHELLS]
    fsc = total[:, :SHELLS] / jnp.sqrt(power + 1e-06)
    corr_ref[...] = fsc
    floor = jnp.maximum(fsc, 0.1)
    table0 = jnp.where(shifted, floor[:, 128:256], floor[:, 0:128])
    table1 = jnp.where(shifted, floor[:, 256:384], floor[:, 128:256])
    table0 = jnp.broadcast_to(table0, (ROWS, 128))
    table1 = jnp.broadcast_to(table1, (ROWS, 128))
    ld_shell.wait()
    for b in range(3):
        at = shell_of[:, 128 * b : 128 * b + 128]
        low = jnp.take_along_axis(table0, jnp.minimum(at, 127), axis=1)
        high = jnp.take_along_axis(table1, jnp.maximum(at - 128, 0), axis=1)
        weight_ref[:, 128 * b : 128 * b + 128] = jnp.where(at < 128, low, high)
    w = weight_ref[...]

    def weigh(t, carry):
        energies = []
        for k in range(4):
            prod[t, :, BOX * k : BOX * k + BOX] = (vprod[4 * t + k] * w).astype(BF16)
            e = jnp.sum(eprod[4 * t + k] * w, axis=0, keepdims=True)
            energies.append(e[:, 0:128] + e[:, 128:256] + e[:, 256:384])
        energies = jnp.concatenate(energies, axis=0)
        part[t, 32:48, :] = jnp.concatenate(list(split3(energies)) + [jnp.zeros((4, 128), BF16)], axis=0)
        return carry

    lax.fori_loop(0, SLABS, weigh, 0)
    ld_col.wait()
    ld_rowt.wait()
    section = jnp.dot(
        prod[...].reshape(SLABS * ROWS, 4 * BOX), col[...], preferred_element_type=F32
    ).astype(BF16)
    stacked = jnp.concatenate(
        [
            jnp.concatenate(
                [section[ROWS * t : ROWS * t + ROWS, :128], section[ROWS * t : ROWS * t + ROWS, 128:]], axis=0
            )
            for t in range(SLABS)
        ],
        axis=1,
    )
    partial = jnp.dot(rowt[...], stacked, preferred_element_type=F32)
    for t in range(SLABS):
        part[t, 0:32, :] = partial[:, 128 * t : 128 * t + 128].astype(BF16)

    for r in FAR8:
        to = (z + r) % SLABS
        copy = remote(part.at[to], parts_in.at[z], part_send.at[r], part_recv.at[z], {"slab": to})
        copy.start()
        copies.append(copy)

    link_copy.wait()

    def add_item(u, carry):
        e = u // 16
        before = link[u, 1]
        has = jnp.where(before >= 0, 1.0, 0.0)
        from_u = jnp.minimum(jnp.maximum(before, 0), SLOTS - 1)
        column = (u % 16) // 4
        t = u % 4
        c = ctf[meta_all[column, t, 0, 8 * e]]
        valid = meta_all[column, t, 0, 8 * e + 4].astype(F32)
        vprod[u] = contrib[u].astype(F32) + has * vprod[from_u]
        eprod[u] = (c * c) * valid + has * eprod[from_u]
        return carry

    lax.fori_loop(0, SLOTS, add_item, 0)
    whole = part[z].astype(F32)
    for r in NEAR8:
        s = (z + r) % SLABS
        remote(part.at[s], parts_in.at[s], part_send.at[r], part_recv.at[s], {"slab": s}).wait_recv()
        whole = whole + parts_in[s].astype(F32)
    best = jnp.max(whole[0:32], axis=0, keepdims=True)
    answer = jnp.zeros((1, 128), F32)
    for k in range(4):
        top = jnp.max(jnp.where(lane1 // 32 == k, best, -jnp.inf), axis=1, keepdims=True)
        energy = whole[32 + k : 33 + k] + (whole[36 + k : 37 + k] + whole[40 + k : 41 + k])
        energy = jnp.sum(energy, axis=1, keepdims=True)
        answer = jnp.where(lane1 == k, top / jnp.sqrt(energy + 1e-06), answer)
    ret_out[...] = answer

    def score_copy(e, r):
        return remote(
            ret_out, ret.at[d], ret_send.at[8 * e + r], ret_recv.at[d],
            {"dom": 2 * z + e, "slab": (z + r) % SLABS},
        )

    for r in FAR8:
        for e in range(2):
            score_copy(e, r).start()
    for e in range(2):
        pl.when(2 * z + e != d)(score_copy(e, 0).start)

    @pl.when(d // 2 == z)
    def _():
        ret[d] = answer

    def one_slice(r, carry):
        at = link[r, 0]
        has = jnp.where(at >= 0, 1.0, 0.0)
        at = jnp.minimum(jnp.maximum(at, 0), SLOTS - 1)
        inverse = 1.0 / weight_ref[...]
        top = has * vprod[at] + maps[r].astype(F32) * inverse
        new_ref[r] = top / (has * eprod[at] + inverse)
        return carry

    new_copies = []
    for t in range(4):
        lax.fori_loop(8 * t, 8 * t + 8, one_slice, 0)
        block = pl.ds(8 * t, 8)
        copy = pltpu.make_async_copy(new_ref.at[block], new_hbm.at[block], new_sem.at[t])
        copy.start()
        new_copies.append(copy)

    for r in range(DOMS):
        s = (d + r) % DOMS
        copy = remote(ret_out, ret.at[s], ret_send.at[r], ret_recv.at[s], {"dom": s, "slab": d // 2})
        if r == 0:
            pl.when(d // 2 != z)(copy.wait_recv)
        else:
            copy.wait_recv()
    scores = jnp.zeros((1, 128), F32)
    for p in range(PART):
        row = ret[owners[p]]
        value = jnp.sum(jnp.where(lane1 == 2 * (d % 2) + ranks[p], row, 0.0), axis=1, keepdims=True)
        scores = jnp.where(lane1 == p, value, scores)
    score_ref[...] = scores[:, :PART]

    for copy in copies:
        copy.wait_send()
    for e in range(2):
        for r in FAR8:
            score_copy(e, r).wait_send()
        pl.when(2 * z + e != d)(score_copy(e, 0).wait_send)
    for copy in new_copies:
        copy.wait()


DELIVER = 8


def deliver_kernel(score_in, corr_in, new_in, score_out, corr_out, new_out, sem):
    step = ORI // DELIVER
    copies = []
    for t in range(DELIVER):
        block = pl.ds(step * t, step)
        copies.append(pltpu.make_async_copy(new_in.at[block], new_out.at[block], sem.at[t]))
    for copy in copies:
        copy.start()
    score_out[...] = score_in[...]
    corr_out[...] = corr_in[0, :NSHELL]
    for copy in copies:
        copy.wait()


def deliver(scores, fsc, new_maps):
    hbm = pl.BlockSpec(memory_space=pl.ANY)
    vmem = pl.BlockSpec(memory_space=pltpu.VMEM)
    return pl.pallas_call(
        deliver_kernel,
        out_shape=(
            jax.ShapeDtypeStruct((1, PART), F32),
            jax.ShapeDtypeStruct((NSHELL,), F32),
            jax.ShapeDtypeStruct((ORI, ROWS, BOX), F32),
        ),
        in_specs=[vmem, vmem, hbm],
        out_specs=(vmem, vmem, hbm),
        scratch_shapes=[pltpu.SemaphoreType.DMA((DELIVER,))],
        compiler_params=pltpu.CompilerParams(vmem_limit_bytes=60 * 1024 * 1024),
        name="deliver",
    )(scores, fsc, new_maps)


def run_main(*operands):
    hbm = pl.BlockSpec(memory_space=pltpu.HBM)
    vmem = pl.BlockSpec(memory_space=pltpu.VMEM)
    v = pltpu.VMEM
    smem = pltpu.SMEM
    dma = pltpu.SemaphoreType.DMA
    return pl.pallas_call(
        main_kernel,
        out_shape=(
            jax.ShapeDtypeStruct((1, PART), F32),
            jax.ShapeDtypeStruct((1, SHELLS), F32),
            jax.ShapeDtypeStruct((ORI, ROWS, BOX), F32),
        ),
        in_specs=[hbm] * 15,
        out_specs=(vmem, vmem, pl.BlockSpec(memory_space=pl.ANY)),
        scratch_shapes=[
            smem((PART,), I32), smem((2, PART), I32), smem((PART,), I32), smem((CLASSES,), F32),
            smem((512,), I32),
            v((PART, ROWS, BOX), BF16),
            v((ORI, ROWS, BOX), BF16),
            v((ORI // 2, ROWS, BOX), BF16),
            v((ROWS, BOX), I32),
            v((ROWS, 256), I32),
            v((ROWS, BOX), F32),
            v((33, 8, BOX), F32),
            v((2, ROWS, 128), F32),
            v((4 * BOX, 256), BF16),
            v((SHIFTS, 2 * ROWS), BF16),
            v((BOX, 256), BF16),
            v((ROWS, BOX), F32),
            v((4, 5, ROWS, BOX), BF16),
            v((5, 4, ROWS, BOX), BF16),
            v((4, 4, ROWS, BOX), BF16),
            v((4, 4, ROWS, BOX), BF16),
            v((SLOTS, ROWS, BOX), BF16),
            v((SLOTS, ROWS, BOX), F32),
            v((SLOTS, ROWS, BOX), F32),
            v((CLASSES, ROWS, BOX), F32),
            v((33, 2, ROWS, 128), F32),
            v((4, 4, 1, 128), I32),
            v((4, 4, 1, 128), I32),
            v((4, 4, 1, 128), I32),
            smem((4, 4, 1, 128), I32),
            smem((4, 4, 1, 128), I32),
            v((SLOTS, 128), I32),
            smem((SLOTS, 128), I32),
            v((ORI, ROWS, BOX), F32),
            v((8, 1, 3 * SHELLS), F32),
            v((4, 1, 3 * SHELLS), F32),
            v((8, 1, 3 * SHELLS), F32),
            v((3, 1, 3 * SHELLS), F32),
            v((SLABS, ROWS, 4 * BOX), BF16),
            v((SLABS, 48, 128), BF16),
            v((SLABS, 48, 128), BF16),
            v((DOMS, 1, 128), F32),
            v((1, 128), F32),
            dma((15,)),
            dma((8,)),
            pltpu.SemaphoreType.REGULAR((3,)),
            dma((NCHUNK,)), dma((NCHUNK,)),
            dma((4,)), dma((4,)),
            dma((4,)), dma((4,)),
            dma((4,)), dma((4,)),
            dma((4,)), dma((4,)),
            dma((4,)), dma((4,)),
            dma((8,)), dma((8,)),
            dma((4,)), dma((4,)),
            dma((8,)), dma((8,)),
            dma((8,)), dma((8,)),
            dma((16,)), dma((16,)),
            dma((4,)),
        ],
        compiler_params=pltpu.CompilerParams(
            collective_id=0, has_side_effects=True, vmem_limit_bytes=60 * 1024 * 1024
        ),
        name="refine",
    )(*operands)


def on_device(consts, images, orientation, offsets, defocus_class, defocus, ori_slot, half_maps):
    scores, fsc, new_maps = run_main(
        orientation[0], offsets[0].T, defocus_class[0], defocus, ori_slot, images[0], half_maps[0], *consts
    )
    scores, fsc, new_maps = deliver(scores, fsc, new_maps)
    return scores, new_maps[None], fsc


def solution(mesh):
    in_specs = (
        P("half", "dom", "slab", None),
        P("half", "dom"),
        P("half", "dom", None),
        P("half", "dom"),
        P(),
        P(),
        P("half", "dom", "slab", None),
    )
    out_specs = (P("half", "dom"), P("half", "dom", "slab", None), P())
    return jax.shard_map(
        functools.partial(on_device, tables()),
        mesh=mesh, in_specs=in_specs, out_specs=out_specs, check_vma=False,
    )
```

```python
import functools
import math

import jax
import jax.numpy as jnp
import ml_dtypes
import numpy as np
from jax import lax
from jax.experimental import pallas as pl
from jax.experimental.pallas import tpu as pltpu
from jax.sharding import PartitionSpec as P

BOX = 384
KX = 192
SHIFTS = 32
NSHELL = 267
ROWS = 48
SLABS = 8
DOMS = 16
PART = 8
ORI = 32
CLASSES = 16
SLOTS = 32
SHELLS = 384
CHUNK = 4
NCHUNK = 4
F32 = jnp.float32
BF16 = jnp.bfloat16
I32 = jnp.int32
MESH = pl.DeviceIdType.MESH
FAR8 = (4, 3, 5, 2, 6, 1, 7)
NEAR8 = FAR8[::-1]
FAR4 = (2, 1, 3)
NEAR4 = FAR4[::-1]


def tables():
    row = np.arange(BOX)
    ky = np.where(row < KX, row, row - BOX)
    kx = np.arange(KX)
    q = ky[:, None] ** 2 + kx[None, :] ** 2
    radius = np.floor(np.sqrt(q.astype(np.float64))).astype(np.int64)
    radius -= radius * radius > q
    radius += (radius + 1) * (radius + 1) <= q
    shell = np.clip(radius - 1, 0, NSHELL - 1)
    base = np.array([0, 0, 0, 128, 128, 0, 0, 0])
    local = shell.reshape(SLABS, ROWS, KX) - base[:, None, None]
    assert local.min() >= 0 and local.max() < 256
    shell_of = np.concatenate([local, local], axis=-1).astype(np.int32)
    ends = np.zeros((SLABS, ROWS, 256), np.int32)
    for s in range(256):
        ends[:, :, s] = (local <= s).sum(-1)
    freq = np.concatenate([q, q], axis=-1).reshape(SLABS, ROWS, BOX).astype(np.float32)
    freq = freq / np.float32(BOX * BOX)
    unit = np.float32(2.0 * math.pi / BOX)

    def trig(index):
        angle = (np.mod(index, BOX).astype(np.float32) * unit).astype(np.float32)
        return np.cos(angle).astype(np.float32), np.sin(angle).astype(np.float32)

    shift = np.arange(33) - 16
    cx, sx = trig(shift[:, None] * kx[None, :])
    tx = np.zeros((33, 8, BOX), np.float32)
    tx[:, 0] = np.concatenate([cx, cx], -1)
    tx[:, 1] = np.concatenate([sx, sx], -1)
    tx[:, 2] = np.concatenate([cx, -cx], -1)
    tx[:, 3] = np.concatenate([sx, -sx], -1)
    cy, sy = trig(ky[:, None] * shift[None, :])
    ty = np.zeros((SLABS, 2, ROWS, 128), np.float32)
    ty[:, 0, :, :33] = cy.reshape(SLABS, ROWS, 33)
    ty[:, 1, :, :33] = sy.reshape(SLABS, ROWS, 33)

    window = np.arange(SHIFTS) - SHIFTS // 2
    wcx, wsx = trig(kx[:, None] * window[None, :])
    wcy, wsy = trig(ky[:, None] * window[None, :])
    col_re = np.concatenate([wcx, -wsx], axis=0)
    col_im = np.concatenate([wsx, wcx], axis=0)
    col = np.zeros((4 * BOX, 256), np.float32)
    for k in range(4):
        col[k * BOX : (k + 1) * BOX, 32 * k : 32 * k + 32] = col_re
        col[k * BOX : (k + 1) * BOX, 128 + 32 * k : 160 + 32 * k] = col_im
    wcy = wcy.reshape(SLABS, ROWS, SHIFTS).transpose(0, 2, 1)
    wsy = wsy.reshape(SLABS, ROWS, SHIFTS).transpose(0, 2, 1)
    rowt = np.concatenate([wcy, -wsy], axis=-1)
    tri = (np.arange(BOX)[:, None] % KX <= np.arange(256)[None, :]).astype(np.float32)
    bf = ml_dtypes.bfloat16
    return (
        shell_of, ends, freq, tx, ty, col.astype(bf), rowt.astype(bf), tri.astype(bf),
    )


def flip_halves(x):
    return pltpu.roll(x, KX, 1)


def ctf_rows(freq, defocus):
    g = defocus * freq
    phi = math.atan2(0.1, 0.995)
    m = jnp.floor((g + phi) * (1.0 / math.pi) + 0.5)
    t = ((g - m * 3.140625) - m * 9.67653589793e-4) + phi
    odd = m - 2.0 * jnp.floor(m * 0.5)
    t2 = t * t
    p = -1.0 / 39916800.0
    for c in (1.0 / 362880.0, -1.0 / 5040.0, 1.0 / 120.0, -1.0 / 6.0, 1.0):
        p = p * t2 + c
    scale = math.sqrt(0.995 * 0.995 + 0.01)
    return (p * t) * ((2.0 * odd - 1.0) * scale)


def split3(x):
    hi = x.astype(BF16)
    rest = x - hi.astype(F32)
    mid = rest.astype(BF16)
    low = (rest - mid.astype(F32)).astype(BF16)
    return hi, mid, low


def main_kernel(
    ori_hbm, off_hbm, cls_hbm, defocus_hbm, slot_hbm, img_hbm, map_hbm,
    shell_hbm, ends_hbm, freq_hbm, tx_hbm, ty_hbm, col_hbm, rowt_hbm, tri_hbm,
    score_ref, corr_ref, new_hbm,
    ori_ref, off_ref, cls_ref, defocus_ref, slot_ref,
    img, maps, other, shell_of, ends, freq, tx, ty, col, rowt, tri, weight_ref,
    packed, stage, regular, extra, contrib, vprod, eprod, ctf, eyb,
    meta_out, meta_stage, meta_in, meta_own, meta_all, link_v, link,
    new_ref, ar1, ar2, ar3, arx, prod, part, parts_in, ret, ret_out,
    load_sem, own_sem, ring_sem, map_send, map_recv,
    img1_send, img1_recv, img2_send, img2_recv, ext_send, ext_recv,
    meta1_send, meta1_recv, meta2_send, meta2_recv,
    ar1_send, ar1_recv, ar2_send, ar2_recv, ar3_send, ar3_recv,
    part_send, part_recv, ret_send, ret_recv, new_sem,
):
    h = lax.axis_index("half")
    d = lax.axis_index("dom")
    z = lax.axis_index("slab")
    y = d // 4
    q = d % 4
    g = h * 4 + q

    def flip(bits):
        hi = (q // 2 + bits // 2) % 2
        lo = (q % 2 + bits % 2) % 2
        return hi * 2 + lo

    def remote(src, dst, send, recv, where):
        return pltpu.make_async_remote_copy(
            src_ref=src, dst_ref=dst, send_sem=send, recv_sem=recv,
            device_id=where, device_id_type=MESH,
        )

    def signal(sem, where):
        pl.semaphore_signal(sem, inc=1, device_id=where, device_id_type=MESH)

    barrier = pltpu.get_barrier_semaphore()
    for r in FAR8:
        to = (g + r) % 8
        signal(barrier, {"half": to // 4, "dom": y * 4 + to % 4})
    for r in FAR4:
        signal(barrier, {"dom": (y + r) % 4 * 4 + q})
    for r in (1, SLABS - 1):
        signal(barrier, {"slab": (z + r) % SLABS})

    loads = [
        (ori_hbm, ori_ref), (off_hbm, off_ref), (cls_hbm, cls_ref), (slot_hbm, slot_ref),
        (defocus_hbm, defocus_ref), (img_hbm, img), (freq_hbm.at[z], freq), (ty_hbm.at[z], ty),
        (map_hbm, maps), (tri_hbm, tri), (ends_hbm.at[z], ends), (tx_hbm, tx),
        (shell_hbm.at[z], shell_of), (col_hbm, col), (rowt_hbm.at[z], rowt),
    ]
    loads = [pltpu.make_async_copy(a, b, load_sem.at[i]) for i, (a, b) in enumerate(loads)]
    for c in loads:
        c.start()
    ld_small = loads[:4]
    (ld_defocus, ld_img, ld_freq, ld_ty, ld_map, ld_tri, ld_ends, ld_tx, ld_shell, ld_col, ld_rowt) = loads[4:]

    for c in ld_small:
        c.wait()
    lane1 = lax.broadcasted_iota(I32, (1, 128), 1)
    owner_row = lax.broadcasted_iota(I32, (DOMS, 128), 0)
    lane16 = lax.broadcasted_iota(I32, (DOMS, 128), 1)
    owners = []
    ranks = []
    second = jnp.int32(0)
    message = jnp.zeros((DOMS, 128), I32)
    for p in range(PART):
        place = slot_ref[ori_ref[p]]
        owner = place // ORI
        rank = jnp.int32(0)
        for before in owners:
            rank = rank + jnp.where(before == owner, 1, 0)
        owners.append(owner)
        ranks.append(rank)
        second = jnp.where(rank == 1, p, second)
        fields = (cls_ref[p], off_ref[0, p] + 16, off_ref[1, p] + 16, place % ORI, jnp.int32(1), jnp.int32(p))
        at = lane16 - 8 * rank
        for f, value in enumerate(fields):
            message = jnp.where((owner_row == owner) & (at == f), value, message)
    for o in range(DOMS):
        meta_out[o // 4, o % 4] = message[o : o + 1]
    own_copy = pltpu.make_async_copy(meta_out, meta_own, own_sem.at[0])
    own_copy.start()

    pl.semaphore_wait(barrier, 7 + 3 + 2)

    map_copies = []
    for c in range(NCHUNK):
        source = map_hbm.at[pl.ds((1 - h) * (ORI // 2) + c * CHUNK, CHUNK)]
        copy = remote(
            source, other.at[pl.ds(c * CHUNK, CHUNK)], map_send.at[c], map_recv.at[c], {"half": 1 - h}
        )
        copy.start()
        map_copies.append(copy)
    copies = list(map_copies)

    def ring(k):
        for r in (1, SLABS - 1):
            signal(ring_sem.at[k], {"slab": (z + r) % SLABS})

    ring(0)

    for r in FAR4:
        to = (y + r) % 4
        copy = remote(
            meta_out.at[to], meta_stage.at[:, y], meta1_send.at[r], meta1_recv.at[y], {"dom": to * 4 + q}
        )
        copy.start()
        copies.append(copy)
    own_copy.wait()
    ld_img.wait()

    def pack(o, carry):
        packed[o // 4, o % 4] = img[meta_own[o // 4, o % 4, 0, 5]]
        return carry

    lax.fori_loop(0, DOMS, pack, 0)
    for t in range(4):
        packed[t, 4] = img[second]
    for r in FAR4:
        to = (y + r) % 4
        copy = remote(packed.at[to], stage.at[:, y], img1_send.at[r], img1_recv.at[y], {"dom": to * 4 + q})
        copy.start()
        copies.append(copy)
    own_img = pltpu.make_async_copy(packed.at[y], stage.at[:, y], own_sem.at[1])
    own_img.start()
    own_meta = pltpu.make_async_copy(meta_out.at[y], meta_stage.at[:, y], own_sem.at[2])
    own_meta.start()
    pl.semaphore_wait(ring_sem.at[0], 2)
    ring(1)

    ld_freq.wait()
    ld_defocus.wait()

    def one_class(k, carry):
        ctf[k] = ctf_rows(freq[...], defocus_ref[k])
        return carry

    lax.fori_loop(0, CLASSES, one_class, 0)
    pl.semaphore_wait(ring_sem.at[1], 2)
    ring(2)
    ld_ty.wait()
    for part_of in range(2):
        for s in range(33):
            eyb[s, part_of] = jnp.broadcast_to(ty[part_of, :, s : s + 1], (ROWS, 128))

    for r in FAR4:
        s = (y + r) % 4
        remote(meta_out.at[s], meta_stage.at[:, s], meta1_send.at[r], meta1_recv.at[s], {"dom": s * 4 + q}).wait_recv()
    own_meta.wait()
    for bits in (3, 2, 1):
        to = flip(bits)
        copy = remote(
            meta_stage.at[to], meta_in.at[q], meta2_send.at[bits], meta2_recv.at[q], {"dom": y * 4 + to}
        )
        copy.start()
        copies.append(copy)
    last_meta = pltpu.make_async_copy(meta_stage.at[q], meta_in.at[q], own_sem.at[3])
    last_meta.start()

    ld_map.wait()

    def own_power(i, total):
        m = maps[i].astype(F32)
        return total + m * m

    own_sq = lax.fori_loop(0, ORI, own_power, jnp.zeros((ROWS, BOX), F32))
    pl.semaphore_wait(ring_sem.at[2], 2)
    cross = jnp.zeros((ROWS, BOX), F32)
    for c in range(NCHUNK):
        if c == NCHUNK - 1:
            for r in FAR4:
                s = (y + r) % 4
                remote(
                    packed.at[s], stage.at[:, s], img1_send.at[r], img1_recv.at[s], {"dom": s * 4 + q}
                ).wait_recv()
            own_img.wait()
            for kind, (src, dst, send, recv) in enumerate(
                ((stage.at[4], extra, ext_send, ext_recv), (stage.at[flip(1)], regular, img2_send, img2_recv))
            ):
                copy = remote(src, dst.at[q], send.at[1], recv.at[q], {"dom": y * 4 + flip(1)})
                copy.start()
                copies.append(copy)
            own_regular = pltpu.make_async_copy(stage.at[q], regular.at[q], own_sem.at[4])
            own_regular.start()
            own_extra = pltpu.make_async_copy(stage.at[4], extra.at[q], own_sem.at[5])
            own_extra.start()
        map_copies[c].wait_recv()

        def cross_term(i, total):
            mine = maps[h * (ORI // 2) + c * CHUNK + i].astype(F32)
            return total + mine * other[c * CHUNK + i].astype(F32)

        cross = lax.fori_loop(0, CHUNK, cross_term, cross)

    copy = remote(stage.at[4], extra.at[q], ext_send.at[2], ext_recv.at[q], {"dom": y * 4 + flip(2)})
    copy.start()
    copies.append(copy)
    for bits in (2, 3):
        to = flip(bits)
        copy = remote(stage.at[to], regular.at[q], img2_send.at[bits], img2_recv.at[q], {"dom": y * 4 + to})
        copy.start()
        copies.append(copy)

    ld_tri.wait()
    ld_ends.wait()
    pieces = jnp.concatenate(list(split3(cross)) + list(split3(own_sq)), axis=0)
    running = jnp.dot(pieces, tri[...], preferred_element_type=F32)
    lane = lax.broadcasted_iota(I32, (1, 128), 1)
    sums = []
    for v in range(2):
        o = 3 * ROWS * v
        c = running[o : o + ROWS] + (running[o + ROWS : o + 2 * ROWS] + running[o + 2 * ROWS : o + 3 * ROWS])
        blocks = []
        for b in range(2):
            e = ends[:, 128 * b : 128 * b + 128]
            low = jnp.take_along_axis(c[:, :128], jnp.clip(e - 1, 0, 127), axis=1)
            high = jnp.take_along_axis(c[:, 128:], jnp.clip(e - 129, 0, 127), axis=1)
            got = jnp.where(e > 128, high, jnp.where(e > 0, low, 0.0))
            blocks.append(jnp.sum(got, axis=0, keepdims=True))
        first = blocks[0] - jnp.where(lane == 0, 0.0, pltpu.roll(blocks[0], 1, 1))
        carry_in = jnp.where(lane == 0, blocks[0][:, 127:128], pltpu.roll(blocks[1], 1, 1))
        sums.append((first, blocks[1] - carry_in))
    shifted = (z == 3) | (z == 4)
    zero = jnp.zeros((1, 128), F32)
    for v in range(3):
        s0, s1 = sums[min(v, 1)]
        for b in range(3):
            block = jnp.where(shifted, (zero, s0, s1)[b], (s0, s1, zero)[b])
            if v > 0:
                block = jnp.where(h == v - 1, block, zero)
            arx[0, :, SHELLS * v + 128 * b : SHELLS * v + 128 * b + 128] = block

    for r in FAR8:
        to = (z + r) % SLABS
        copy = remote(arx.at[0], ar1.at[z], ar1_send.at[r], ar1_recv.at[z], {"slab": to})
        copy.start()
        copies.append(copy)

    last_meta.wait()
    for bits in (1, 2, 3):
        s = flip(bits)
        remote(meta_stage.at[s], meta_in.at[s], meta2_send.at[bits], meta2_recv.at[s], {"dom": y * 4 + s}).wait_recv()
    to_smem = pltpu.make_async_copy(meta_in, meta_all, own_sem.at[6])
    to_smem.start()

    numbers = jnp.concatenate([meta_in[c, t] for c in range(4) for t in range(4)], axis=0).astype(F32)

    def field(f):
        return jnp.sum(jnp.where(lane16 == f, numbers, 0.0), axis=1, keepdims=True)

    key = jnp.concatenate(
        [jnp.where(field(8 * e + 4) > 0.5, field(8 * e + 3), -1.0) for e in range(2)], axis=0
    )
    item_lane = lax.broadcasted_iota(I32, (SLOTS, 128), 1)
    item_row = lax.broadcasted_iota(I32, (SLOTS, 128), 0)
    across = jnp.sum(jnp.where(item_lane == item_row, key, 0.0), axis=0, keepdims=True)
    where_f = item_lane.astype(F32)
    last = jnp.max(
        jnp.where((across == item_row.astype(F32)) & (item_lane < SLOTS), where_f, -1.0), axis=1, keepdims=True
    )
    same = (across == key) & (item_lane < item_row) & (key >= 0.0)
    previous = jnp.max(jnp.where(same, where_f, -1.0), axis=1, keepdims=True)
    link_v[...] = jnp.where(item_lane == 0, last, jnp.where(item_lane == 1, previous, 0.0)).astype(I32)
    link_copy = pltpu.make_async_copy(link_v, link, own_sem.at[7])
    link_copy.start()

    ld_tx.wait()
    own_regular.wait()
    own_extra.wait()
    to_smem.wait()
    low_half = lax.broadcasted_iota(I32, (ROWS, BOX), 1) < KX

    def items_of(source, column, e):
        def one_item(t, carry):
            at = 8 * e
            phase_x = tx[meta_all[column, t, 0, at + 1]]
            phase_y = eyb[meta_all[column, t, 0, at + 2]]
            cy = jnp.concatenate([phase_y[0]] * 3, axis=1)
            sy = jnp.concatenate([phase_y[1]] * 3, axis=1)
            cos_t = phase_x[0:1] * cy - phase_x[1:2] * sy
            sin_t = phase_x[3:4] * cy + phase_x[2:3] * sy
            x = source[column, t].astype(F32)
            c = ctf[meta_all[column, t, 0, at]] * meta_all[column, t, 0, at + 4].astype(F32)
            zz = c * (x * cos_t + flip_halves(x) * sin_t)
            contrib[16 * e + 4 * column + t] = zz.astype(BF16)
            m = maps[meta_all[column, t, 0, at + 3]].astype(F32)
            straight = zz * m
            crossed = zz * flip_halves(m)
            n = 2 * (4 * t + column) + e
            vprod[n] = jnp.where(low_half, straight, -crossed) + flip_halves(
                jnp.where(low_half, crossed, straight)
            )
            cm = c * m
            eprod[n] = cm * cm
            return carry

        lax.fori_loop(0, 4, one_item, 0)

    def wait_regular(bits):
        s = flip(bits)
        remote(
            stage.at[s], regular.at[s], img2_send.at[bits], img2_recv.at[s], {"dom": y * 4 + s}
        ).wait_recv()

    def wait_extra(bits):
        s = flip(bits)
        remote(stage.at[4], extra.at[s], ext_send.at[bits], ext_recv.at[s], {"dom": y * 4 + s}).wait_recv()

    items_of(regular, q, 0)
    items_of(extra, q, 1)
    wait_extra(1)
    items_of(extra, flip(1), 1)
    ar1[z] = arx[0]
    for r in NEAR8:
        s = (z + r) % SLABS
        remote(arx.at[0], ar1.at[s], ar1_send.at[r], ar1_recv.at[s], {"slab": s}).wait_recv()
    total = ar1[0]
    for s in range(1, SLABS):
        total = total + ar1[s]
    arx[1] = total
    for r in FAR4:
        to = (y + r) % 4
        copy = remote(arx.at[1], ar2.at[y], ar2_send.at[r], ar2_recv.at[y], {"dom": to * 4 + q})
        copy.start()
        copies.append(copy)
    wait_regular(1)
    items_of(regular, flip(1), 0)
    wait_extra(2)
    copy = remote(
        extra.at[flip(2)], extra.at[flip(2)], ext_send.at[3], ext_recv.at[flip(2)], {"dom": y * 4 + flip(1)}
    )
    copy.start()
    copies.append(copy)
    ar2[y] = total
    for r in NEAR4:
        s = (y + r) % 4
        remote(arx.at[1], ar2.at[s], ar2_send.at[r], ar2_recv.at[s], {"dom": s * 4 + q}).wait_recv()
    total = ar2[0]
    for s in range(1, 4):
        total = total + ar2[s]
    arx[2] = total
    for r in FAR8:
        to = (g + r) % 8
        copy = remote(
            arx.at[2], ar3.at[g], ar3_send.at[r], ar3_recv.at[g], {"half": to // 4, "dom": y * 4 + to % 4}
        )
        copy.start()
        copies.append(copy)
    items_of(extra, flip(2), 1)
    wait_regular(2)
    items_of(regular, flip(2), 0)
    wait_extra(3)
    items_of(extra, flip(3), 1)
    wait_regular(3)
    items_of(regular, flip(3), 0)
    ar3[g] = total
    for r in NEAR8:
        s = (g + r) % 8
        remote(
            arx.at[2], ar3.at[s], ar3_send.at[r], ar3_recv.at[s], {"half": s // 4, "dom": y * 4 + s % 4}
        ).wait_recv()
    total = ar3[0]
    for s in range(1, 8):
        total = total + ar3[s]

    power = total[:, SHELLS : 2 * SHELLS] * total[:, 2 * SHELLS : 3 * SHELLS]
    fsc = total[:, :SHELLS] / jnp.sqrt(power + 1e-06)
    corr_ref[...] = fsc
    floor = jnp.maximum(fsc, 0.1)
    table0 = jnp.where(shifted, floor[:, 128:256], floor[:, 0:128])
    table1 = jnp.where(shifted, floor[:, 256:384], floor[:, 128:256])
    table0 = jnp.broadcast_to(table0, (ROWS, 128))
    table1 = jnp.broadcast_to(table1, (ROWS, 128))
    ld_shell.wait()
    for b in range(3):
        at = shell_of[:, 128 * b : 128 * b + 128]
        low = jnp.take_along_axis(table0, jnp.minimum(at, 127), axis=1)
        high = jnp.take_along_axis(table1, jnp.maximum(at - 128, 0), axis=1)
        weight_ref[:, 128 * b : 128 * b + 128] = jnp.where(at < 128, low, high)
    w = weight_ref[...]

    def weigh(t, carry):
        energies = []
        for k in range(4):
            prod[t, :, BOX * k : BOX * k + BOX] = (vprod[4 * t + k] * w).astype(BF16)
            e = jnp.sum(eprod[4 * t + k] * w, axis=0, keepdims=True)
            energies.append(e[:, 0:128] + e[:, 128:256] + e[:, 256:384])
        energies = jnp.concatenate(energies, axis=0)
        part[t, 32:48, :] = jnp.concatenate(list(split3(energies)) + [jnp.zeros((4, 128), BF16)], axis=0)
        return carry

    lax.fori_loop(0, SLABS, weigh, 0)
    ld_col.wait()
    ld_rowt.wait()
    section = jnp.dot(
        prod[...].reshape(SLABS * ROWS, 4 * BOX), col[...], preferred_element_type=F32
    ).astype(BF16)
    stacked = jnp.concatenate(
        [
            jnp.concatenate(
                [section[ROWS * t : ROWS * t + ROWS, :128], section[ROWS * t : ROWS * t + ROWS, 128:]], axis=0
            )
            for t in range(SLABS)
        ],
        axis=1,
    )
    partial = jnp.dot(rowt[...], stacked, preferred_element_type=F32)
    for t in range(SLABS):
        part[t, 0:32, :] = partial[:, 128 * t : 128 * t + 128].astype(BF16)

    for r in FAR8:
        to = (z + r) % SLABS
        copy = remote(part.at[to], parts_in.at[z], part_send.at[r], part_recv.at[z], {"slab": to})
        copy.start()
        copies.append(copy)

    link_copy.wait()

    def add_item(u, carry):
        e = u // 16
        before = link[u, 1]
        has = jnp.where(before >= 0, 1.0, 0.0)
        from_u = jnp.minimum(jnp.maximum(before, 0), SLOTS - 1)
        column = (u % 16) // 4
        t = u % 4
        c = ctf[meta_all[column, t, 0, 8 * e]]
        valid = meta_all[column, t, 0, 8 * e + 4].astype(F32)
        vprod[u] = contrib[u].astype(F32) + has * vprod[from_u]
        eprod[u] = (c * c) * valid + has * eprod[from_u]
        return carry

    lax.fori_loop(0, SLOTS, add_item, 0)
    whole = part[z].astype(F32)
    for r in NEAR8:
        s = (z + r) % SLABS
        remote(part.at[s], parts_in.at[s], part_send.at[r], part_recv.at[s], {"slab": s}).wait_recv()
        whole = whole + parts_in[s].astype(F32)
    best = jnp.max(whole[0:32], axis=0, keepdims=True)
    answer = jnp.zeros((1, 128), F32)
    for k in range(4):
        top = jnp.max(jnp.where(lane1 // 32 == k, best, -jnp.inf), axis=1, keepdims=True)
        energy = whole[32 + k : 33 + k] + (whole[36 + k : 37 + k] + whole[40 + k : 41 + k])
        energy = jnp.sum(energy, axis=1, keepdims=True)
        answer = jnp.where(lane1 == k, top / jnp.sqrt(energy + 1e-06), answer)
    ret_out[...] = answer

    def score_copy(e, r):
        return remote(
            ret_out, ret.at[d], ret_send.at[8 * e + r], ret_recv.at[d],
            {"dom": 2 * z + e, "slab": (z + r) % SLABS},
        )

    for r in FAR8:
        for e in range(2):
            score_copy(e, r).start()
    for e in range(2):
        pl.when(2 * z + e != d)(score_copy(e, 0).start)

    @pl.when(d // 2 == z)
    def _():
        ret[d] = answer

    def one_slice(r, carry):
        at = link[r, 0]
        has = jnp.where(at >= 0, 1.0, 0.0)
        at = jnp.minimum(jnp.maximum(at, 0), SLOTS - 1)
        inverse = 1.0 / weight_ref[...]
        top = has * vprod[at] + maps[r].astype(F32) * inverse
        new_ref[r] = top / (has * eprod[at] + inverse)
        return carry

    new_copies = []
    for t in range(4):
        lax.fori_loop(8 * t, 8 * t + 8, one_slice, 0)
        block = pl.ds(8 * t, 8)
        copy = pltpu.make_async_copy(new_ref.at[block], new_hbm.at[block], new_sem.at[t])
        copy.start()
        new_copies.append(copy)

    for r in range(DOMS):
        s = (d + r) % DOMS
        copy = remote(ret_out, ret.at[s], ret_send.at[r], ret_recv.at[s], {"dom": s, "slab": d // 2})
        if r == 0:
            pl.when(d // 2 != z)(copy.wait_recv)
        else:
            copy.wait_recv()
    scores = jnp.zeros((1, 128), F32)
    for p in range(PART):
        row = ret[owners[p]]
        value = jnp.sum(jnp.where(lane1 == 2 * (d % 2) + ranks[p], row, 0.0), axis=1, keepdims=True)
        scores = jnp.where(lane1 == p, value, scores)
    score_ref[...] = scores[:, :PART]

    for copy in copies:
        copy.wait_send()
    for e in range(2):
        for r in FAR8:
            score_copy(e, r).wait_send()
        pl.when(2 * z + e != d)(score_copy(e, 0).wait_send)
    for copy in new_copies:
        copy.wait()


DELIVER = 8


def deliver_kernel(score_in, corr_in, new_in, score_out, corr_out, new_out, hold, in_sem, out_sem):
    step = ORI // DELIVER
    reads = []
    writes = []
    for t in range(DELIVER):
        block = pl.ds(step * t, step)
        reads.append(pltpu.make_async_copy(new_in.at[block], hold.at[block], in_sem.at[t]))
        writes.append(pltpu.make_async_copy(hold.at[block], new_out.at[block], out_sem.at[t]))
    for copy in reads:
        copy.start()
    score_out[...] = score_in[...]
    corr_out[...] = corr_in[0, :NSHELL]
    for t in range(DELIVER):
        reads[t].wait()
        writes[t].start()
    for copy in writes:
        copy.wait()


def deliver(scores, fsc, new_maps):
    hbm = pl.BlockSpec(memory_space=pl.ANY)
    vmem = pl.BlockSpec(memory_space=pltpu.VMEM)
    return pl.pallas_call(
        deliver_kernel,
        out_shape=(
            jax.ShapeDtypeStruct((1, PART), F32),
            jax.ShapeDtypeStruct((NSHELL,), F32),
            jax.ShapeDtypeStruct((ORI, ROWS, BOX), F32),
        ),
        in_specs=[vmem, vmem, hbm],
        out_specs=(vmem, vmem, hbm),
        scratch_shapes=[
            pltpu.VMEM((ORI, ROWS, BOX), F32),
            pltpu.SemaphoreType.DMA((DELIVER,)),
            pltpu.SemaphoreType.DMA((DELIVER,)),
        ],
        compiler_params=pltpu.CompilerParams(vmem_limit_bytes=60 * 1024 * 1024),
        name="deliver",
    )(scores, fsc, new_maps)


def run_main(*operands):
    hbm = pl.BlockSpec(memory_space=pltpu.HBM)
    vmem = pl.BlockSpec(memory_space=pltpu.VMEM)
    v = pltpu.VMEM
    smem = pltpu.SMEM
    dma = pltpu.SemaphoreType.DMA
    return pl.pallas_call(
        main_kernel,
        out_shape=(
            jax.ShapeDtypeStruct((1, PART), F32),
            jax.ShapeDtypeStruct((1, SHELLS), F32),
            jax.ShapeDtypeStruct((ORI, ROWS, BOX), F32),
        ),
        in_specs=[hbm] * 15,
        out_specs=(vmem, vmem, pl.BlockSpec(memory_space=pl.ANY)),
        scratch_shapes=[
            smem((PART,), I32), smem((2, PART), I32), smem((PART,), I32), smem((CLASSES,), F32),
            smem((512,), I32),
            v((PART, ROWS, BOX), BF16),
            v((ORI, ROWS, BOX), BF16),
            v((ORI // 2, ROWS, BOX), BF16),
            v((ROWS, BOX), I32),
            v((ROWS, 256), I32),
            v((ROWS, BOX), F32),
            v((33, 8, BOX), F32),
            v((2, ROWS, 128), F32),
            v((4 * BOX, 256), BF16),
            v((SHIFTS, 2 * ROWS), BF16),
            v((BOX, 256), BF16),
            v((ROWS, BOX), F32),
            v((4, 5, ROWS, BOX), BF16),
            v((5, 4, ROWS, BOX), BF16),
            v((4, 4, ROWS, BOX), BF16),
            v((4, 4, ROWS, BOX), BF16),
            v((SLOTS, ROWS, BOX), BF16),
            v((SLOTS, ROWS, BOX), F32),
            v((SLOTS, ROWS, BOX), F32),
            v((CLASSES, ROWS, BOX), F32),
            v((33, 2, ROWS, 128), F32),
            v((4, 4, 1, 128), I32),
            v((4, 4, 1, 128), I32),
            v((4, 4, 1, 128), I32),
            smem((4, 4, 1, 128), I32),
            smem((4, 4, 1, 128), I32),
            v((SLOTS, 128), I32),
            smem((SLOTS, 128), I32),
            v((ORI, ROWS, BOX), F32),
            v((8, 1, 3 * SHELLS), F32),
            v((4, 1, 3 * SHELLS), F32),
            v((8, 1, 3 * SHELLS), F32),
            v((3, 1, 3 * SHELLS), F32),
            v((SLABS, ROWS, 4 * BOX), BF16),
            v((SLABS, 48, 128), BF16),
            v((SLABS, 48, 128), BF16),
            v((DOMS, 1, 128), F32),
            v((1, 128), F32),
            dma((15,)),
            dma((8,)),
            pltpu.SemaphoreType.REGULAR((3,)),
            dma((NCHUNK,)), dma((NCHUNK,)),
            dma((4,)), dma((4,)),
            dma((4,)), dma((4,)),
            dma((4,)), dma((4,)),
            dma((4,)), dma((4,)),
            dma((4,)), dma((4,)),
            dma((8,)), dma((8,)),
            dma((4,)), dma((4,)),
            dma((8,)), dma((8,)),
            dma((8,)), dma((8,)),
            dma((16,)), dma((16,)),
            dma((4,)),
        ],
        compiler_params=pltpu.CompilerParams(
            collective_id=0, has_side_effects=True, vmem_limit_bytes=60 * 1024 * 1024
        ),
        name="refine",
    )(*operands)


def on_device(consts, images, orientation, offsets, defocus_class, defocus, ori_slot, half_maps):
    scores, fsc, new_maps = run_main(
        orientation[0], offsets[0].T, defocus_class[0], defocus, ori_slot, images[0], half_maps[0], *consts
    )
    scores, fsc, new_maps = deliver(scores, fsc, new_maps)
    return scores, new_maps[None], fsc


def solution(mesh):
    in_specs = (
        P("half", "dom", "slab", None),
        P("half", "dom"),
        P("half", "dom", None),
        P("half", "dom"),
        P(),
        P(),
        P("half", "dom", "slab", None),
    )
    out_specs = (P("half", "dom"), P("half", "dom", "slab", None), P())
    return jax.shard_map(
        functools.partial(on_device, tables()),
        mesh=mesh, in_specs=in_specs, out_specs=out_specs, check_vma=False,
    )
```

```python
import functools
import math

import jax
import jax.numpy as jnp
import ml_dtypes
import numpy as np
from jax import lax
from jax.experimental import pallas as pl
from jax.experimental.pallas import tpu as pltpu
from jax.sharding import PartitionSpec as P

BOX = 384
KX = 192
SHIFTS = 32
NSHELL = 267
ROWS = 48
SLABS = 8
DOMS = 16
PART = 8
ORI = 32
CLASSES = 16
SLOTS = 32
SHELLS = 384
CHUNK = 4
NCHUNK = 4
F32 = jnp.float32
BF16 = jnp.bfloat16
I32 = jnp.int32
MESH = pl.DeviceIdType.MESH
FAR8 = (4, 3, 5, 2, 6, 1, 7)
NEAR8 = FAR8[::-1]
FAR4 = (2, 1, 3)
NEAR4 = FAR4[::-1]


def tables():
    row = np.arange(BOX)
    ky = np.where(row < KX, row, row - BOX)
    kx = np.arange(KX)
    q = ky[:, None] ** 2 + kx[None, :] ** 2
    radius = np.floor(np.sqrt(q.astype(np.float64))).astype(np.int64)
    radius -= radius * radius > q
    radius += (radius + 1) * (radius + 1) <= q
    shell = np.clip(radius - 1, 0, NSHELL - 1)
    base = np.array([0, 0, 0, 128, 128, 0, 0, 0])
    local = shell.reshape(SLABS, ROWS, KX) - base[:, None, None]
    assert local.min() >= 0 and local.max() < 256
    shell_of = np.concatenate([local, local], axis=-1).astype(np.int32)
    ends = np.zeros((SLABS, ROWS, 256), np.int32)
    for s in range(256):
        ends[:, :, s] = (local <= s).sum(-1)
    freq = np.concatenate([q, q], axis=-1).reshape(SLABS, ROWS, BOX).astype(np.float32)
    freq = freq / np.float32(BOX * BOX)
    unit = np.float32(2.0 * math.pi / BOX)

    def trig(index):
        angle = (np.mod(index, BOX).astype(np.float32) * unit).astype(np.float32)
        return np.cos(angle).astype(np.float32), np.sin(angle).astype(np.float32)

    shift = np.arange(33) - 16
    cx, sx = trig(shift[:, None] * kx[None, :])
    tx = np.zeros((33, 8, BOX), np.float32)
    tx[:, 0] = np.concatenate([cx, cx], -1)
    tx[:, 1] = np.concatenate([sx, sx], -1)
    tx[:, 2] = np.concatenate([cx, -cx], -1)
    tx[:, 3] = np.concatenate([sx, -sx], -1)
    cy, sy = trig(ky[:, None] * shift[None, :])
    ty = np.zeros((SLABS, 2, ROWS, 128), np.float32)
    ty[:, 0, :, :33] = cy.reshape(SLABS, ROWS, 33)
    ty[:, 1, :, :33] = sy.reshape(SLABS, ROWS, 33)

    window = np.arange(SHIFTS) - SHIFTS // 2
    wcx, wsx = trig(kx[:, None] * window[None, :])
    wcy, wsy = trig(ky[:, None] * window[None, :])
    col_re = np.concatenate([wcx, -wsx], axis=0)
    col_im = np.concatenate([wsx, wcx], axis=0)
    col = np.zeros((4 * BOX, 256), np.float32)
    for k in range(4):
        col[k * BOX : (k + 1) * BOX, 32 * k : 32 * k + 32] = col_re
        col[k * BOX : (k + 1) * BOX, 128 + 32 * k : 160 + 32 * k] = col_im
    wcy = wcy.reshape(SLABS, ROWS, SHIFTS).transpose(0, 2, 1)
    wsy = wsy.reshape(SLABS, ROWS, SHIFTS).transpose(0, 2, 1)
    rowt = np.concatenate([wcy, -wsy], axis=-1)
    tri = (np.arange(BOX)[:, None] % KX <= np.arange(256)[None, :]).astype(np.float32)
    bf = ml_dtypes.bfloat16
    return (
        shell_of, ends, freq, tx, ty, col.astype(bf), rowt.astype(bf), tri.astype(bf),
    )


def flip_halves(x):
    return pltpu.roll(x, KX, 1)


def ctf_rows(freq, defocus):
    g = defocus * freq
    phi = math.atan2(0.1, 0.995)
    m = jnp.floor((g + phi) * (1.0 / math.pi) + 0.5)
    t = ((g - m * 3.140625) - m * 9.67653589793e-4) + phi
    odd = m - 2.0 * jnp.floor(m * 0.5)
    t2 = t * t
    p = -1.0 / 39916800.0
    for c in (1.0 / 362880.0, -1.0 / 5040.0, 1.0 / 120.0, -1.0 / 6.0, 1.0):
        p = p * t2 + c
    scale = math.sqrt(0.995 * 0.995 + 0.01)
    return (p * t) * ((2.0 * odd - 1.0) * scale)


def split3(x):
    hi = x.astype(BF16)
    rest = x - hi.astype(F32)
    mid = rest.astype(BF16)
    low = (rest - mid.astype(F32)).astype(BF16)
    return hi, mid, low


def main_kernel(
    ori_hbm, off_hbm, cls_hbm, defocus_hbm, slot_hbm, img_hbm, map_hbm,
    shell_hbm, ends_hbm, freq_hbm, tx_hbm, ty_hbm, col_hbm, rowt_hbm, tri_hbm,
    score_ref, corr_ref, new_ref,
    ori_ref, off_ref, cls_ref, defocus_ref, slot_ref,
    img, maps, other, shell_of, ends, freq, tx, ty, col, rowt, tri, weight_ref,
    packed, stage, regular, extra, contrib, vprod, eprod, ctf, eyb,
    meta_out, meta_stage, meta_in, meta_own, meta_all, link_v, link,
    ar1, ar2, ar3, arx, prod, part, parts_in, ret, ret_out,
    load_sem, own_sem, ring_sem, map_send, map_recv,
    img1_send, img1_recv, img2_send, img2_recv, ext_send, ext_recv,
    meta1_send, meta1_recv, meta2_send, meta2_recv,
    ar1_send, ar1_recv, ar2_send, ar2_recv, ar3_send, ar3_recv,
    part_send, part_recv, ret_send, ret_recv,
):
    h = lax.axis_index("half")
    d = lax.axis_index("dom")
    z = lax.axis_index("slab")
    y = d // 4
    q = d % 4
    g = h * 4 + q

    def flip(bits):
        hi = (q // 2 + bits // 2) % 2
        lo = (q % 2 + bits % 2) % 2
        return hi * 2 + lo

    def remote(src, dst, send, recv, where):
        return pltpu.make_async_remote_copy(
            src_ref=src, dst_ref=dst, send_sem=send, recv_sem=recv,
            device_id=where, device_id_type=MESH,
        )

    def signal(sem, where):
        pl.semaphore_signal(sem, inc=1, device_id=where, device_id_type=MESH)

    barrier = pltpu.get_barrier_semaphore()
    for r in FAR8:
        to = (g + r) % 8
        signal(barrier, {"half": to // 4, "dom": y * 4 + to % 4})
    for r in FAR4:
        signal(barrier, {"dom": (y + r) % 4 * 4 + q})
    for r in (1, SLABS - 1):
        signal(barrier, {"slab": (z + r) % SLABS})

    loads = [
        (ori_hbm, ori_ref), (off_hbm, off_ref), (cls_hbm, cls_ref), (slot_hbm, slot_ref),
        (defocus_hbm, defocus_ref), (img_hbm, img), (freq_hbm.at[z], freq), (ty_hbm.at[z], ty),
        (map_hbm, maps), (tri_hbm, tri), (ends_hbm.at[z], ends), (tx_hbm, tx),
        (shell_hbm.at[z], shell_of), (col_hbm, col), (rowt_hbm.at[z], rowt),
    ]
    loads = [pltpu.make_async_copy(a, b, load_sem.at[i]) for i, (a, b) in enumerate(loads)]
    for c in loads:
        c.start()
    ld_small = loads[:4]
    (ld_defocus, ld_img, ld_freq, ld_ty, ld_map, ld_tri, ld_ends, ld_tx, ld_shell, ld_col, ld_rowt) = loads[4:]

    for c in ld_small:
        c.wait()
    lane1 = lax.broadcasted_iota(I32, (1, 128), 1)
    owner_row = lax.broadcasted_iota(I32, (DOMS, 128), 0)
    lane16 = lax.broadcasted_iota(I32, (DOMS, 128), 1)
    owners = []
    ranks = []
    second = jnp.int32(0)
    message = jnp.zeros((DOMS, 128), I32)
    for p in range(PART):
        place = slot_ref[ori_ref[p]]
        owner = place // ORI
        rank = jnp.int32(0)
        for before in owners:
            rank = rank + jnp.where(before == owner, 1, 0)
        owners.append(owner)
        ranks.append(rank)
        second = jnp.where(rank == 1, p, second)
        fields = (cls_ref[p], off_ref[0, p] + 16, off_ref[1, p] + 16, place % ORI, jnp.int32(1), jnp.int32(p))
        at = lane16 - 8 * rank
        for f, value in enumerate(fields):
            message = jnp.where((owner_row == owner) & (at == f), value, message)
    for o in range(DOMS):
        meta_out[o // 4, o % 4] = message[o : o + 1]
    own_copy = pltpu.make_async_copy(meta_out, meta_own, own_sem.at[0])
    own_copy.start()

    pl.semaphore_wait(barrier, 7 + 3 + 2)

    map_copies = []
    for c in range(NCHUNK):
        source = map_hbm.at[pl.ds((1 - h) * (ORI // 2) + c * CHUNK, CHUNK)]
        copy = remote(
            source, other.at[pl.ds(c * CHUNK, CHUNK)], map_send.at[c], map_recv.at[c], {"half": 1 - h}
        )
        copy.start()
        map_copies.append(copy)
    copies = list(map_copies)

    def ring(k):
        for r in (1, SLABS - 1):
            signal(ring_sem.at[k], {"slab": (z + r) % SLABS})

    ring(0)

    for r in FAR4:
        to = (y + r) % 4
        copy = remote(
            meta_out.at[to], meta_stage.at[:, y], meta1_send.at[r], meta1_recv.at[y], {"dom": to * 4 + q}
        )
        copy.start()
        copies.append(copy)
    own_copy.wait()
    ld_img.wait()

    def pack(o, carry):
        packed[o // 4, o % 4] = img[meta_own[o // 4, o % 4, 0, 5]]
        return carry

    lax.fori_loop(0, DOMS, pack, 0)
    for t in range(4):
        packed[t, 4] = img[second]
    for r in FAR4:
        to = (y + r) % 4
        copy = remote(packed.at[to], stage.at[:, y], img1_send.at[r], img1_recv.at[y], {"dom": to * 4 + q})
        copy.start()
        copies.append(copy)
    own_img = pltpu.make_async_copy(packed.at[y], stage.at[:, y], own_sem.at[1])
    own_img.start()
    own_meta = pltpu.make_async_copy(meta_out.at[y], meta_stage.at[:, y], own_sem.at[2])
    own_meta.start()
    pl.semaphore_wait(ring_sem.at[0], 2)
    ring(1)

    ld_freq.wait()
    ld_defocus.wait()

    def one_class(k, carry):
        ctf[k] = ctf_rows(freq[...], defocus_ref[k])
        return carry

    lax.fori_loop(0, CLASSES, one_class, 0)
    pl.semaphore_wait(ring_sem.at[1], 2)
    ring(2)
    ld_ty.wait()
    for part_of in range(2):
        for s in range(33):
            eyb[s, part_of] = jnp.broadcast_to(ty[part_of, :, s : s + 1], (ROWS, 128))

    for r in FAR4:
        s = (y + r) % 4
        remote(meta_out.at[s], meta_stage.at[:, s], meta1_send.at[r], meta1_recv.at[s], {"dom": s * 4 + q}).wait_recv()
    own_meta.wait()
    for bits in (3, 2, 1):
        to = flip(bits)
        copy = remote(
            meta_stage.at[to], meta_in.at[q], meta2_send.at[bits], meta2_recv.at[q], {"dom": y * 4 + to}
        )
        copy.start()
        copies.append(copy)
    last_meta = pltpu.make_async_copy(meta_stage.at[q], meta_in.at[q], own_sem.at[3])
    last_meta.start()

    ld_map.wait()

    def own_power(i, total):
        m = maps[i].astype(F32)
        return total + m * m

    own_sq = lax.fori_loop(0, ORI, own_power, jnp.zeros((ROWS, BOX), F32))
    pl.semaphore_wait(ring_sem.at[2], 2)
    cross = jnp.zeros((ROWS, BOX), F32)
    for c in range(NCHUNK):
        if c == NCHUNK - 1:
            for r in FAR4:
                s = (y + r) % 4
                remote(
                    packed.at[s], stage.at[:, s], img1_send.at[r], img1_recv.at[s], {"dom": s * 4 + q}
                ).wait_recv()
            own_img.wait()
            for kind, (src, dst, send, recv) in enumerate(
                ((stage.at[4], extra, ext_send, ext_recv), (stage.at[flip(1)], regular, img2_send, img2_recv))
            ):
                copy = remote(src, dst.at[q], send.at[1], recv.at[q], {"dom": y * 4 + flip(1)})
                copy.start()
                copies.append(copy)
            own_regular = pltpu.make_async_copy(stage.at[q], regular.at[q], own_sem.at[4])
            own_regular.start()
            own_extra = pltpu.make_async_copy(stage.at[4], extra.at[q], own_sem.at[5])
            own_extra.start()
        map_copies[c].wait_recv()

        def cross_term(i, total):
            mine = maps[h * (ORI // 2) + c * CHUNK + i].astype(F32)
            return total + mine * other[c * CHUNK + i].astype(F32)

        cross = lax.fori_loop(0, CHUNK, cross_term, cross)

    copy = remote(stage.at[4], extra.at[q], ext_send.at[2], ext_recv.at[q], {"dom": y * 4 + flip(2)})
    copy.start()
    copies.append(copy)
    for bits in (2, 3):
        to = flip(bits)
        copy = remote(stage.at[to], regular.at[q], img2_send.at[bits], img2_recv.at[q], {"dom": y * 4 + to})
        copy.start()
        copies.append(copy)

    ld_tri.wait()
    ld_ends.wait()
    pieces = jnp.concatenate(list(split3(cross)) + list(split3(own_sq)), axis=0)
    running = jnp.dot(pieces, tri[...], preferred_element_type=F32)
    lane = lax.broadcasted_iota(I32, (1, 128), 1)
    sums = []
    for v in range(2):
        o = 3 * ROWS * v
        c = running[o : o + ROWS] + (running[o + ROWS : o + 2 * ROWS] + running[o + 2 * ROWS : o + 3 * ROWS])
        blocks = []
        for b in range(2):
            e = ends[:, 128 * b : 128 * b + 128]
            low = jnp.take_along_axis(c[:, :128], jnp.clip(e - 1, 0, 127), axis=1)
            high = jnp.take_along_axis(c[:, 128:], jnp.clip(e - 129, 0, 127), axis=1)
            got = jnp.where(e > 128, high, jnp.where(e > 0, low, 0.0))
            blocks.append(jnp.sum(got, axis=0, keepdims=True))
        first = blocks[0] - jnp.where(lane == 0, 0.0, pltpu.roll(blocks[0], 1, 1))
        carry_in = jnp.where(lane == 0, blocks[0][:, 127:128], pltpu.roll(blocks[1], 1, 1))
        sums.append((first, blocks[1] - carry_in))
    shifted = (z == 3) | (z == 4)
    zero = jnp.zeros((1, 128), F32)
    for v in range(3):
        s0, s1 = sums[min(v, 1)]
        for b in range(3):
            block = jnp.where(shifted, (zero, s0, s1)[b], (s0, s1, zero)[b])
            if v > 0:
                block = jnp.where(h == v - 1, block, zero)
            arx[0, :, SHELLS * v + 128 * b : SHELLS * v + 128 * b + 128] = block

    for r in FAR8:
        to = (z + r) % SLABS
        copy = remote(arx.at[0], ar1.at[z], ar1_send.at[r], ar1_recv.at[z], {"slab": to})
        copy.start()
        copies.append(copy)

    last_meta.wait()
    for bits in (1, 2, 3):
        s = flip(bits)
        remote(meta_stage.at[s], meta_in.at[s], meta2_send.at[bits], meta2_recv.at[s], {"dom": y * 4 + s}).wait_recv()
    to_smem = pltpu.make_async_copy(meta_in, meta_all, own_sem.at[6])
    to_smem.start()

    numbers = jnp.concatenate([meta_in[c, t] for c in range(4) for t in range(4)], axis=0).astype(F32)

    def field(f):
        return jnp.sum(jnp.where(lane16 == f, numbers, 0.0), axis=1, keepdims=True)

    key = jnp.concatenate(
        [jnp.where(field(8 * e + 4) > 0.5, field(8 * e + 3), -1.0) for e in range(2)], axis=0
    )
    item_lane = lax.broadcasted_iota(I32, (SLOTS, 128), 1)
    item_row = lax.broadcasted_iota(I32, (SLOTS, 128), 0)
    across = jnp.sum(jnp.where(item_lane == item_row, key, 0.0), axis=0, keepdims=True)
    where_f = item_lane.astype(F32)
    last = jnp.max(
        jnp.where((across == item_row.astype(F32)) & (item_lane < SLOTS), where_f, -1.0), axis=1, keepdims=True
    )
    same = (across == key) & (item_lane < item_row) & (key >= 0.0)
    previous = jnp.max(jnp.where(same, where_f, -1.0), axis=1, keepdims=True)
    link_v[...] = jnp.where(item_lane == 0, last, jnp.where(item_lane == 1, previous, 0.0)).astype(I32)
    link_copy = pltpu.make_async_copy(link_v, link, own_sem.at[7])
    link_copy.start()

    ld_tx.wait()
    own_regular.wait()
    own_extra.wait()
    to_smem.wait()
    low_half = lax.broadcasted_iota(I32, (ROWS, BOX), 1) < KX

    def items_of(source, column, e):
        def one_item(t, carry):
            at = 8 * e
            phase_x = tx[meta_all[column, t, 0, at + 1]]
            phase_y = eyb[meta_all[column, t, 0, at + 2]]
            cy = jnp.concatenate([phase_y[0]] * 3, axis=1)
            sy = jnp.concatenate([phase_y[1]] * 3, axis=1)
            cos_t = phase_x[0:1] * cy - phase_x[1:2] * sy
            sin_t = phase_x[3:4] * cy + phase_x[2:3] * sy
            x = source[column, t].astype(F32)
            c = ctf[meta_all[column, t, 0, at]] * meta_all[column, t, 0, at + 4].astype(F32)
            zz = c * (x * cos_t + flip_halves(x) * sin_t)
            contrib[16 * e + 4 * column + t] = zz.astype(BF16)
            m = maps[meta_all[column, t, 0, at + 3]].astype(F32)
            straight = zz * m
            crossed = zz * flip_halves(m)
            n = 2 * (4 * t + column) + e
            vprod[n] = jnp.where(low_half, straight, -crossed) + flip_halves(
                jnp.where(low_half, crossed, straight)
            )
            cm = c * m
            eprod[n] = cm * cm
            return carry

        lax.fori_loop(0, 4, one_item, 0)

    def wait_regular(bits):
        s = flip(bits)
        remote(
            stage.at[s], regular.at[s], img2_send.at[bits], img2_recv.at[s], {"dom": y * 4 + s}
        ).wait_recv()

    def wait_extra(bits):
        s = flip(bits)
        remote(stage.at[4], extra.at[s], ext_send.at[bits], ext_recv.at[s], {"dom": y * 4 + s}).wait_recv()

    items_of(regular, q, 0)
    items_of(extra, q, 1)
    wait_extra(1)
    items_of(extra, flip(1), 1)
    ar1[z] = arx[0]
    for r in NEAR8:
        s = (z + r) % SLABS
        remote(arx.at[0], ar1.at[s], ar1_send.at[r], ar1_recv.at[s], {"slab": s}).wait_recv()
    total = ar1[0]
    for s in range(1, SLABS):
        total = total + ar1[s]
    arx[1] = total
    for r in FAR4:
        to = (y + r) % 4
        copy = remote(arx.at[1], ar2.at[y], ar2_send.at[r], ar2_recv.at[y], {"dom": to * 4 + q})
        copy.start()
        copies.append(copy)
    wait_regular(1)
    items_of(regular, flip(1), 0)
    wait_extra(2)
    copy = remote(
        extra.at[flip(2)], extra.at[flip(2)], ext_send.at[3], ext_recv.at[flip(2)], {"dom": y * 4 + flip(1)}
    )
    copy.start()
    copies.append(copy)
    ar2[y] = total
    for r in NEAR4:
        s = (y + r) % 4
        remote(arx.at[1], ar2.at[s], ar2_send.at[r], ar2_recv.at[s], {"dom": s * 4 + q}).wait_recv()
    total = ar2[0]
    for s in range(1, 4):
        total = total + ar2[s]
    arx[2] = total
    for r in FAR8:
        to = (g + r) % 8
        copy = remote(
            arx.at[2], ar3.at[g], ar3_send.at[r], ar3_recv.at[g], {"half": to // 4, "dom": y * 4 + to % 4}
        )
        copy.start()
        copies.append(copy)
    items_of(extra, flip(2), 1)
    wait_regular(2)
    items_of(regular, flip(2), 0)
    wait_extra(3)
    items_of(extra, flip(3), 1)
    wait_regular(3)
    items_of(regular, flip(3), 0)
    ar3[g] = total
    for r in NEAR8:
        s = (g + r) % 8
        remote(
            arx.at[2], ar3.at[s], ar3_send.at[r], ar3_recv.at[s], {"half": s // 4, "dom": y * 4 + s % 4}
        ).wait_recv()
    total = ar3[0]
    for s in range(1, 8):
        total = total + ar3[s]

    power = total[:, SHELLS : 2 * SHELLS] * total[:, 2 * SHELLS : 3 * SHELLS]
    fsc = total[:, :SHELLS] / jnp.sqrt(power + 1e-06)
    corr_ref[...] = fsc
    floor = jnp.maximum(fsc, 0.1)
    table0 = jnp.where(shifted, floor[:, 128:256], floor[:, 0:128])
    table1 = jnp.where(shifted, floor[:, 256:384], floor[:, 128:256])
    table0 = jnp.broadcast_to(table0, (ROWS, 128))
    table1 = jnp.broadcast_to(table1, (ROWS, 128))
    ld_shell.wait()
    for b in range(3):
        at = shell_of[:, 128 * b : 128 * b + 128]
        low = jnp.take_along_axis(table0, jnp.minimum(at, 127), axis=1)
        high = jnp.take_along_axis(table1, jnp.maximum(at - 128, 0), axis=1)
        weight_ref[:, 128 * b : 128 * b + 128] = jnp.where(at < 128, low, high)
    w = weight_ref[...]

    def weigh(t, carry):
        energies = []
        for k in range(4):
            prod[t, :, BOX * k : BOX * k + BOX] = (vprod[4 * t + k] * w).astype(BF16)
            e = jnp.sum(eprod[4 * t + k] * w, axis=0, keepdims=True)
            energies.append(e[:, 0:128] + e[:, 128:256] + e[:, 256:384])
        energies = jnp.concatenate(energies, axis=0)
        part[t, 32:48, :] = jnp.concatenate(list(split3(energies)) + [jnp.zeros((4, 128), BF16)], axis=0)
        return carry

    lax.fori_loop(0, SLABS, weigh, 0)
    ld_col.wait()
    ld_rowt.wait()
    section = jnp.dot(
        prod[...].reshape(SLABS * ROWS, 4 * BOX), col[...], preferred_element_type=F32
    ).astype(BF16)
    stacked = jnp.concatenate(
        [
            jnp.concatenate(
                [section[ROWS * t : ROWS * t + ROWS, :128], section[ROWS * t : ROWS * t + ROWS, 128:]], axis=0
            )
            for t in range(SLABS)
        ],
        axis=1,
    )
    partial = jnp.dot(rowt[...], stacked, preferred_element_type=F32)
    for t in range(SLABS):
        part[t, 0:32, :] = partial[:, 128 * t : 128 * t + 128].astype(BF16)

    for r in FAR8:
        to = (z + r) % SLABS
        copy = remote(part.at[to], parts_in.at[z], part_send.at[r], part_recv.at[z], {"slab": to})
        copy.start()
        copies.append(copy)

    link_copy.wait()

    def add_item(u, carry):
        e = u // 16
        before = link[u, 1]
        has = jnp.where(before >= 0, 1.0, 0.0)
        from_u = jnp.minimum(jnp.maximum(before, 0), SLOTS - 1)
        column = (u % 16) // 4
        t = u % 4
        c = ctf[meta_all[column, t, 0, 8 * e]]
        valid = meta_all[column, t, 0, 8 * e + 4].astype(F32)
        vprod[u] = contrib[u].astype(F32) + has * vprod[from_u]
        eprod[u] = (c * c) * valid + has * eprod[from_u]
        return carry

    lax.fori_loop(0, SLOTS, add_item, 0)
    whole = part[z].astype(F32)
    for r in NEAR8:
        s = (z + r) % SLABS
        remote(part.at[s], parts_in.at[s], part_send.at[r], part_recv.at[s], {"slab": s}).wait_recv()
        whole = whole + parts_in[s].astype(F32)
    best = jnp.max(whole[0:32], axis=0, keepdims=True)
    answer = jnp.zeros((1, 128), F32)
    for k in range(4):
        top = jnp.max(jnp.where(lane1 // 32 == k, best, -jnp.inf), axis=1, keepdims=True)
        energy = whole[32 + k : 33 + k] + (whole[36 + k : 37 + k] + whole[40 + k : 41 + k])
        energy = jnp.sum(energy, axis=1, keepdims=True)
        answer = jnp.where(lane1 == k, top / jnp.sqrt(energy + 1e-06), answer)
    ret_out[...] = answer

    def score_copy(e, r):
        return remote(
            ret_out, ret.at[d], ret_send.at[8 * e + r], ret_recv.at[d],
            {"dom": 2 * z + e, "slab": (z + r) % SLABS},
        )

    for r in FAR8:
        for e in range(2):
            score_copy(e, r).start()
    for e in range(2):
        pl.when(2 * z + e != d)(score_copy(e, 0).start)

    @pl.when(d // 2 == z)
    def _():
        ret[d] = answer

    def one_slice(r, carry):
        at = link[r, 0]
        has = jnp.where(at >= 0, 1.0, 0.0)
        at = jnp.minimum(jnp.maximum(at, 0), SLOTS - 1)
        inverse = 1.0 / weight_ref[...]
        top = has * vprod[at] + maps[r].astype(F32) * inverse
        new_ref[r] = top / (has * eprod[at] + inverse)
        return carry

    lax.fori_loop(0, ORI, one_slice, 0)

    for r in range(DOMS):
        s = (d + r) % DOMS
        copy = remote(ret_out, ret.at[s], ret_send.at[r], ret_recv.at[s], {"dom": s, "slab": d // 2})
        if r == 0:
            pl.when(d // 2 != z)(copy.wait_recv)
        else:
            copy.wait_recv()
    scores = jnp.zeros((1, 128), F32)
    for p in range(PART):
        row = ret[owners[p]]
        value = jnp.sum(jnp.where(lane1 == 2 * (d % 2) + ranks[p], row, 0.0), axis=1, keepdims=True)
        scores = jnp.where(lane1 == p, value, scores)
    score_ref[...] = scores[:, :PART]

    for copy in copies:
        copy.wait_send()
    for e in range(2):
        for r in FAR8:
            score_copy(e, r).wait_send()
        pl.when(2 * z + e != d)(score_copy(e, 0).wait_send)


DELIVER = 8


def deliver_kernel(score_in, corr_in, new_in, score_out, corr_out, new_out, sem):
    step = ORI // DELIVER
    writes = []
    for t in range(DELIVER):
        block = pl.ds(step * t, step)
        writes.append(pltpu.make_async_copy(new_in.at[block], new_out.at[block], sem.at[t]))
    for copy in writes:
        copy.start()
    score_out[...] = score_in[...]
    corr_out[...] = corr_in[0, :NSHELL]
    for copy in writes:
        copy.wait()


def deliver(scores, fsc, new_maps):
    hbm = pl.BlockSpec(memory_space=pl.ANY)
    vmem = pl.BlockSpec(memory_space=pltpu.VMEM)
    return pl.pallas_call(
        deliver_kernel,
        out_shape=(
            jax.ShapeDtypeStruct((1, PART), F32),
            jax.ShapeDtypeStruct((NSHELL,), F32),
            jax.ShapeDtypeStruct((ORI, ROWS, BOX), F32),
        ),
        in_specs=[vmem, vmem, vmem],
        out_specs=(vmem, vmem, hbm),
        scratch_shapes=[
            pltpu.SemaphoreType.DMA((DELIVER,)),
        ],
        compiler_params=pltpu.CompilerParams(vmem_limit_bytes=16 * 1024 * 1024),
        name="deliver",
    )(scores, fsc, new_maps)


def run_main(*operands):
    hbm = pl.BlockSpec(memory_space=pltpu.HBM)
    vmem = pl.BlockSpec(memory_space=pltpu.VMEM)
    v = pltpu.VMEM
    smem = pltpu.SMEM
    dma = pltpu.SemaphoreType.DMA
    return pl.pallas_call(
        main_kernel,
        out_shape=(
            pltpu.VMEM((1, PART), F32),
            pltpu.VMEM((1, SHELLS), F32),
            pltpu.VMEM((ORI, ROWS, BOX), F32),
        ),
        in_specs=[hbm] * 15,
        out_specs=(vmem, vmem, vmem),
        scratch_shapes=[
            smem((PART,), I32), smem((2, PART), I32), smem((PART,), I32), smem((CLASSES,), F32),
            smem((512,), I32),
            v((PART, ROWS, BOX), BF16),
            v((ORI, ROWS, BOX), BF16),
            v((ORI // 2, ROWS, BOX), BF16),
            v((ROWS, BOX), I32),
            v((ROWS, 256), I32),
            v((ROWS, BOX), F32),
            v((33, 8, BOX), F32),
            v((2, ROWS, 128), F32),
            v((4 * BOX, 256), BF16),
            v((SHIFTS, 2 * ROWS), BF16),
            v((BOX, 256), BF16),
            v((ROWS, BOX), F32),
            v((4, 5, ROWS, BOX), BF16),
            v((5, 4, ROWS, BOX), BF16),
            v((4, 4, ROWS, BOX), BF16),
            v((4, 4, ROWS, BOX), BF16),
            v((SLOTS, ROWS, BOX), BF16),
            v((SLOTS, ROWS, BOX), F32),
            v((SLOTS, ROWS, BOX), F32),
            v((CLASSES, ROWS, BOX), F32),
            v((33, 2, ROWS, 128), F32),
            v((4, 4, 1, 128), I32),
            v((4, 4, 1, 128), I32),
            v((4, 4, 1, 128), I32),
            smem((4, 4, 1, 128), I32),
            smem((4, 4, 1, 128), I32),
            v((SLOTS, 128), I32),
            smem((SLOTS, 128), I32),
            v((8, 1, 3 * SHELLS), F32),
            v((4, 1, 3 * SHELLS), F32),
            v((8, 1, 3 * SHELLS), F32),
            v((3, 1, 3 * SHELLS), F32),
            v((SLABS, ROWS, 4 * BOX), BF16),
            v((SLABS, 48, 128), BF16),
            v((SLABS, 48, 128), BF16),
            v((DOMS, 1, 128), F32),
            v((1, 128), F32),
            dma((15,)),
            dma((8,)),
            pltpu.SemaphoreType.REGULAR((3,)),
            dma((NCHUNK,)), dma((NCHUNK,)),
            dma((4,)), dma((4,)),
            dma((4,)), dma((4,)),
            dma((4,)), dma((4,)),
            dma((4,)), dma((4,)),
            dma((4,)), dma((4,)),
            dma((8,)), dma((8,)),
            dma((4,)), dma((4,)),
            dma((8,)), dma((8,)),
            dma((8,)), dma((8,)),
            dma((16,)), dma((16,)),
        ],
        compiler_params=pltpu.CompilerParams(
            collective_id=0, has_side_effects=True, vmem_limit_bytes=44 * 1024 * 1024
        ),
        name="refine",
    )(*[pltpu.with_memory_space_constraint(x, pltpu.HBM) for x in operands])


def on_device(consts, images, orientation, offsets, defocus_class, defocus, ori_slot, half_maps):
    scores, fsc, new_maps = run_main(
        orientation[0], offsets[0].T, defocus_class[0], defocus, ori_slot, images[0], half_maps[0], *consts
    )
    scores, fsc, new_maps = deliver(scores, fsc, new_maps)
    return scores, new_maps[None], fsc


def solution(mesh):
    in_specs = (
        P("half", "dom", "slab", None),
        P("half", "dom"),
        P("half", "dom", None),
        P("half", "dom"),
        P(),
        P(),
        P("half", "dom", "slab", None),
    )
    out_specs = (P("half", "dom"), P("half", "dom", "slab", None), P())
    return jax.shard_map(
        functools.partial(on_device, tables()),
        mesh=mesh, in_specs=in_specs, out_specs=out_specs, check_vma=False,
    )
```

```python
import functools
import math

import jax
import jax.numpy as jnp
import ml_dtypes
import numpy as np
from jax import lax
from jax.experimental import pallas as pl
from jax.experimental.pallas import tpu as pltpu
from jax.sharding import PartitionSpec as P

BOX = 384
KX = 192
SHIFTS = 32
NSHELL = 267
ROWS = 48
SLABS = 8
DOMS = 16
PART = 8
ORI = 32
CLASSES = 16
SLOTS = 32
SHELLS = 384
CHUNK = 4
NCHUNK = 4
F32 = jnp.float32
BF16 = jnp.bfloat16
I32 = jnp.int32
MESH = pl.DeviceIdType.MESH
FAR8 = (4, 3, 5, 2, 6, 1, 7)
NEAR8 = FAR8[::-1]
FAR4 = (2, 1, 3)
NEAR4 = FAR4[::-1]


def tables():
    row = np.arange(BOX)
    ky = np.where(row < KX, row, row - BOX)
    kx = np.arange(KX)
    q = ky[:, None] ** 2 + kx[None, :] ** 2
    radius = np.floor(np.sqrt(q.astype(np.float64))).astype(np.int64)
    radius -= radius * radius > q
    radius += (radius + 1) * (radius + 1) <= q
    shell = np.clip(radius - 1, 0, NSHELL - 1)
    base = np.array([0, 0, 0, 128, 128, 0, 0, 0])
    local = shell.reshape(SLABS, ROWS, KX) - base[:, None, None]
    assert local.min() >= 0 and local.max() < 256
    shell_of = np.concatenate([local, local], axis=-1).astype(np.int32)
    ends = np.zeros((SLABS, ROWS, 256), np.int32)
    for s in range(256):
        ends[:, :, s] = (local <= s).sum(-1)
    freq = np.concatenate([q, q], axis=-1).reshape(SLABS, ROWS, BOX).astype(np.float32)
    freq = freq / np.float32(BOX * BOX)
    unit = np.float32(2.0 * math.pi / BOX)

    def trig(index):
        angle = (np.mod(index, BOX).astype(np.float32) * unit).astype(np.float32)
        return np.cos(angle).astype(np.float32), np.sin(angle).astype(np.float32)

    shift = np.arange(33) - 16
    cx, sx = trig(shift[:, None] * kx[None, :])
    tx = np.zeros((33, 8, BOX), np.float32)
    tx[:, 0] = np.concatenate([cx, cx], -1)
    tx[:, 1] = np.concatenate([sx, sx], -1)
    tx[:, 2] = np.concatenate([cx, -cx], -1)
    tx[:, 3] = np.concatenate([sx, -sx], -1)
    cy, sy = trig(ky[:, None] * shift[None, :])
    ty = np.zeros((SLABS, 2, ROWS, 128), np.float32)
    ty[:, 0, :, :33] = cy.reshape(SLABS, ROWS, 33)
    ty[:, 1, :, :33] = sy.reshape(SLABS, ROWS, 33)

    window = np.arange(SHIFTS) - SHIFTS // 2
    wcx, wsx = trig(kx[:, None] * window[None, :])
    wcy, wsy = trig(ky[:, None] * window[None, :])
    col_re = np.concatenate([wcx, -wsx], axis=0)
    col_im = np.concatenate([wsx, wcx], axis=0)
    col = np.zeros((4 * BOX, 256), np.float32)
    for k in range(4):
        col[k * BOX : (k + 1) * BOX, 32 * k : 32 * k + 32] = col_re
        col[k * BOX : (k + 1) * BOX, 128 + 32 * k : 160 + 32 * k] = col_im
    wcy = wcy.reshape(SLABS, ROWS, SHIFTS).transpose(0, 2, 1)
    wsy = wsy.reshape(SLABS, ROWS, SHIFTS).transpose(0, 2, 1)
    rowt = np.concatenate([wcy, -wsy], axis=-1)
    tri = (np.arange(BOX)[:, None] % KX <= np.arange(256)[None, :]).astype(np.float32)
    bf = ml_dtypes.bfloat16
    return (
        shell_of, ends, freq, tx, ty, col.astype(bf), rowt.astype(bf), tri.astype(bf),
    )


def flip_halves(x):
    return pltpu.roll(x, KX, 1)


def ctf_rows(freq, defocus):
    g = defocus * freq
    phi = math.atan2(0.1, 0.995)
    m = jnp.floor((g + phi) * (1.0 / math.pi) + 0.5)
    t = ((g - m * 3.140625) - m * 9.67653589793e-4) + phi
    odd = m - 2.0 * jnp.floor(m * 0.5)
    t2 = t * t
    p = -1.0 / 39916800.0
    for c in (1.0 / 362880.0, -1.0 / 5040.0, 1.0 / 120.0, -1.0 / 6.0, 1.0):
        p = p * t2 + c
    scale = math.sqrt(0.995 * 0.995 + 0.01)
    return (p * t) * ((2.0 * odd - 1.0) * scale)


def split3(x):
    hi = x.astype(BF16)
    rest = x - hi.astype(F32)
    mid = rest.astype(BF16)
    low = (rest - mid.astype(F32)).astype(BF16)
    return hi, mid, low


def main_kernel(
    ori_hbm, off_hbm, cls_hbm, defocus_hbm, slot_hbm, img_hbm, map_hbm,
    shell_hbm, ends_hbm, freq_hbm, tx_hbm, ty_hbm, col_hbm, rowt_hbm, tri_hbm,
    score_ref, corr_ref, new_ref,
    ori_ref, off_ref, cls_ref, defocus_ref, slot_ref,
    img, maps, other, shell_of, ends, freq, tx, ty, col, rowt, tri, weight_ref,
    packed, stage, regular, extra, contrib, vprod, eprod, ctf, eyb,
    meta_out, meta_stage, meta_in, meta_own, meta_all, link_v, link,
    ar1, ar2, ar3, arx, prod, part, parts_in, ret, ret_out,
    load_sem, own_sem, ring_sem, map_send, map_recv,
    img1_send, img1_recv, img2_send, img2_recv, ext_send, ext_recv,
    meta1_send, meta1_recv, meta2_send, meta2_recv,
    ar1_send, ar1_recv, ar2_send, ar2_recv, ar3_send, ar3_recv,
    part_send, part_recv, ret_send, ret_recv,
):
    h = lax.axis_index("half")
    d = lax.axis_index("dom")
    z = lax.axis_index("slab")
    y = d // 4
    q = d % 4
    g = h * 4 + q

    def flip(bits):
        hi = (q // 2 + bits // 2) % 2
        lo = (q % 2 + bits % 2) % 2
        return hi * 2 + lo

    def remote(src, dst, send, recv, where):
        return pltpu.make_async_remote_copy(
            src_ref=src, dst_ref=dst, send_sem=send, recv_sem=recv,
            device_id=where, device_id_type=MESH,
        )

    def signal(sem, where):
        pl.semaphore_signal(sem, inc=1, device_id=where, device_id_type=MESH)

    neighbours = (
        {"half": 1 - h}, {"half": 1 - h, "dom": y * 4 + flip(2)}, {"dom": y * 4 + flip(1)},
        {"dom": (y + 1) % 4 * 4 + q}, {"dom": (y + 3) % 4 * 4 + q},
        {"slab": (z + 1) % SLABS}, {"slab": (z + 7) % SLABS},
    )
    barrier = pltpu.get_barrier_semaphore()
    for where in neighbours:
        signal(barrier, where)

    loads = [
        (ori_hbm, ori_ref), (off_hbm, off_ref), (cls_hbm, cls_ref), (slot_hbm, slot_ref),
        (defocus_hbm, defocus_ref), (img_hbm, img), (freq_hbm.at[z], freq), (ty_hbm.at[z], ty),
        (map_hbm, maps), (tri_hbm, tri), (ends_hbm.at[z], ends), (tx_hbm, tx),
        (shell_hbm.at[z], shell_of), (col_hbm, col), (rowt_hbm.at[z], rowt),
    ]
    loads = [pltpu.make_async_copy(a, b, load_sem.at[i]) for i, (a, b) in enumerate(loads)]
    for c in loads:
        c.start()
    ld_small = loads[:4]
    (ld_defocus, ld_img, ld_freq, ld_ty, ld_map, ld_tri, ld_ends, ld_tx, ld_shell, ld_col, ld_rowt) = loads[4:]

    for c in ld_small:
        c.wait()
    lane1 = lax.broadcasted_iota(I32, (1, 128), 1)
    owner_row = lax.broadcasted_iota(I32, (DOMS, 128), 0)
    lane16 = lax.broadcasted_iota(I32, (DOMS, 128), 1)
    owners = []
    ranks = []
    second = jnp.int32(0)
    message = jnp.zeros((DOMS, 128), I32)
    for p in range(PART):
        place = slot_ref[ori_ref[p]]
        owner = place // ORI
        rank = jnp.int32(0)
        for before in owners:
            rank = rank + jnp.where(before == owner, 1, 0)
        owners.append(owner)
        ranks.append(rank)
        second = jnp.where(rank == 1, p, second)
        fields = (cls_ref[p], off_ref[0, p] + 16, off_ref[1, p] + 16, place % ORI, jnp.int32(1), jnp.int32(p))
        at = lane16 - 8 * rank
        for f, value in enumerate(fields):
            message = jnp.where((owner_row == owner) & (at == f), value, message)
    for o in range(DOMS):
        meta_out[o // 4, o % 4] = message[o : o + 1]
    own_copy = pltpu.make_async_copy(meta_out, meta_own, own_sem.at[0])
    own_copy.start()

    pl.semaphore_wait(barrier, len(neighbours))

    map_copies = []
    for c in range(NCHUNK):
        source = map_hbm.at[pl.ds((1 - h) * (ORI // 2) + c * CHUNK, CHUNK)]
        copy = remote(
            source, other.at[pl.ds(c * CHUNK, CHUNK)], map_send.at[c], map_recv.at[c], {"half": 1 - h}
        )
        copy.start()
        map_copies.append(copy)
    copies = list(map_copies)

    def ring(k):
        for where in neighbours:
            signal(ring_sem.at[k], where)

    ring(0)

    own_copy.wait()
    ld_img.wait()

    def pack(o, carry):
        packed[o // 4, o % 4] = img[meta_own[o // 4, o % 4, 0, 5]]
        return carry

    lax.fori_loop(0, DOMS, pack, 0)
    for t in range(4):
        packed[t, 4] = img[second]
    pl.semaphore_wait(ring_sem.at[0], len(neighbours))
    ring(1)

    for r in FAR4:
        to = (y + r) % 4
        copy = remote(
            meta_out.at[to], meta_stage.at[:, y], meta1_send.at[r], meta1_recv.at[y], {"dom": to * 4 + q}
        )
        copy.start()
        copies.append(copy)
    for r in FAR4:
        to = (y + r) % 4
        copy = remote(packed.at[to], stage.at[:, y], img1_send.at[r], img1_recv.at[y], {"dom": to * 4 + q})
        copy.start()
        copies.append(copy)
    own_img = pltpu.make_async_copy(packed.at[y], stage.at[:, y], own_sem.at[1])
    own_img.start()
    own_meta = pltpu.make_async_copy(meta_out.at[y], meta_stage.at[:, y], own_sem.at[2])
    own_meta.start()

    ld_freq.wait()
    ld_defocus.wait()

    def one_class(k, carry):
        ctf[k] = ctf_rows(freq[...], defocus_ref[k])
        return carry

    lax.fori_loop(0, CLASSES, one_class, 0)
    pl.semaphore_wait(ring_sem.at[1], len(neighbours))
    ring(2)
    ld_ty.wait()
    for part_of in range(2):
        for s in range(33):
            eyb[s, part_of] = jnp.broadcast_to(ty[part_of, :, s : s + 1], (ROWS, 128))

    for r in FAR4:
        s = (y + r) % 4
        remote(meta_out.at[s], meta_stage.at[:, s], meta1_send.at[r], meta1_recv.at[s], {"dom": s * 4 + q}).wait_recv()
    own_meta.wait()
    for bits in (3, 2, 1):
        to = flip(bits)
        copy = remote(
            meta_stage.at[to], meta_in.at[q], meta2_send.at[bits], meta2_recv.at[q], {"dom": y * 4 + to}
        )
        copy.start()
        copies.append(copy)
    last_meta = pltpu.make_async_copy(meta_stage.at[q], meta_in.at[q], own_sem.at[3])
    last_meta.start()

    ld_map.wait()

    def own_power(i, total):
        m = maps[i].astype(F32)
        return total + m * m

    own_sq = lax.fori_loop(0, ORI, own_power, jnp.zeros((ROWS, BOX), F32))
    pl.semaphore_wait(ring_sem.at[2], len(neighbours))
    ld_tri.wait()
    ld_ends.wait()

    def shell_sums(values):
        running = jnp.dot(jnp.concatenate(split3(values), axis=0), tri[...], preferred_element_type=F32)
        c = running[:ROWS] + (running[ROWS : 2 * ROWS] + running[2 * ROWS :])
        blocks = []
        for b in range(2):
            e = ends[:, 128 * b : 128 * b + 128]
            low = jnp.take_along_axis(c[:, :128], jnp.clip(e - 1, 0, 127), axis=1)
            high = jnp.take_along_axis(c[:, 128:], jnp.clip(e - 129, 0, 127), axis=1)
            got = jnp.where(e > 128, high, jnp.where(e > 0, low, 0.0))
            blocks.append(jnp.sum(got, axis=0, keepdims=True))
        first = blocks[0] - jnp.where(lane1 == 0, 0.0, pltpu.roll(blocks[0], 1, 1))
        carry_in = jnp.where(lane1 == 0, blocks[0][:, 127:128], pltpu.roll(blocks[1], 1, 1))
        return first, blocks[1] - carry_in

    power_sums = shell_sums(own_sq)
    cross = jnp.zeros((ROWS, BOX), F32)
    for c in range(NCHUNK):
        if c == NCHUNK - 1:
            for r in FAR4:
                s = (y + r) % 4
                remote(
                    packed.at[s], stage.at[:, s], img1_send.at[r], img1_recv.at[s], {"dom": s * 4 + q}
                ).wait_recv()
            own_img.wait()
            for kind, (src, dst, send, recv) in enumerate(
                ((stage.at[4], extra, ext_send, ext_recv), (stage.at[flip(1)], regular, img2_send, img2_recv))
            ):
                copy = remote(src, dst.at[q], send.at[1], recv.at[q], {"dom": y * 4 + flip(1)})
                copy.start()
                copies.append(copy)
            own_regular = pltpu.make_async_copy(stage.at[q], regular.at[q], own_sem.at[4])
            own_regular.start()
            own_extra = pltpu.make_async_copy(stage.at[4], extra.at[q], own_sem.at[5])
            own_extra.start()
        map_copies[c].wait_recv()

        def cross_term(i, total):
            mine = maps[h * (ORI // 2) + c * CHUNK + i].astype(F32)
            return total + mine * other[c * CHUNK + i].astype(F32)

        cross = lax.fori_loop(0, CHUNK, cross_term, cross)

    copy = remote(stage.at[4], extra.at[q], ext_send.at[2], ext_recv.at[q], {"dom": y * 4 + flip(2)})
    copy.start()
    copies.append(copy)
    for bits in (2, 3):
        to = flip(bits)
        copy = remote(stage.at[to], regular.at[q], img2_send.at[bits], img2_recv.at[q], {"dom": y * 4 + to})
        copy.start()
        copies.append(copy)

    sums = (shell_sums(cross), power_sums)
    shifted = (z == 3) | (z == 4)
    zero = jnp.zeros((1, 128), F32)
    for v in range(3):
        s0, s1 = sums[min(v, 1)]
        for b in range(3):
            block = jnp.where(shifted, (zero, s0, s1)[b], (s0, s1, zero)[b])
            if v > 0:
                block = jnp.where(h == v - 1, block, zero)
            arx[0, :, SHELLS * v + 128 * b : SHELLS * v + 128 * b + 128] = block

    for r in FAR8:
        to = (z + r) % SLABS
        copy = remote(arx.at[0], ar1.at[z], ar1_send.at[r], ar1_recv.at[z], {"slab": to})
        copy.start()
        copies.append(copy)

    last_meta.wait()
    for bits in (1, 2, 3):
        s = flip(bits)
        remote(meta_stage.at[s], meta_in.at[s], meta2_send.at[bits], meta2_recv.at[s], {"dom": y * 4 + s}).wait_recv()
    to_smem = pltpu.make_async_copy(meta_in, meta_all, own_sem.at[6])
    to_smem.start()

    numbers = jnp.concatenate([meta_in[c, t] for c in range(4) for t in range(4)], axis=0).astype(F32)

    def field(f):
        return jnp.sum(jnp.where(lane16 == f, numbers, 0.0), axis=1, keepdims=True)

    key = jnp.concatenate(
        [jnp.where(field(8 * e + 4) > 0.5, field(8 * e + 3), -1.0) for e in range(2)], axis=0
    )
    item_lane = lax.broadcasted_iota(I32, (SLOTS, 128), 1)
    item_row = lax.broadcasted_iota(I32, (SLOTS, 128), 0)
    across = jnp.sum(jnp.where(item_lane == item_row, key, 0.0), axis=0, keepdims=True)
    where_f = item_lane.astype(F32)
    last = jnp.max(
        jnp.where((across == item_row.astype(F32)) & (item_lane < SLOTS), where_f, -1.0), axis=1, keepdims=True
    )
    same = (across == key) & (item_lane < item_row) & (key >= 0.0)
    previous = jnp.max(jnp.where(same, where_f, -1.0), axis=1, keepdims=True)
    link_v[...] = jnp.where(item_lane == 0, last, jnp.where(item_lane == 1, previous, 0.0)).astype(I32)
    link_copy = pltpu.make_async_copy(link_v, link, own_sem.at[7])
    link_copy.start()

    ld_tx.wait()
    own_regular.wait()
    own_extra.wait()
    to_smem.wait()
    low_half = lax.broadcasted_iota(I32, (ROWS, BOX), 1) < KX

    def items_of(source, column, e):
        def one_item(t, carry):
            at = 8 * e
            phase_x = tx[meta_all[column, t, 0, at + 1]]
            phase_y = eyb[meta_all[column, t, 0, at + 2]]
            cy = jnp.concatenate([phase_y[0]] * 3, axis=1)
            sy = jnp.concatenate([phase_y[1]] * 3, axis=1)
            cos_t = phase_x[0:1] * cy - phase_x[1:2] * sy
            sin_t = phase_x[3:4] * cy + phase_x[2:3] * sy
            x = source[column, t].astype(F32)
            c = ctf[meta_all[column, t, 0, at]] * meta_all[column, t, 0, at + 4].astype(F32)
            zz = c * (x * cos_t + flip_halves(x) * sin_t)
            contrib[16 * e + 4 * column + t] = zz.astype(BF16)
            m = maps[meta_all[column, t, 0, at + 3]].astype(F32)
            straight = zz * m
            crossed = zz * flip_halves(m)
            n = 2 * (4 * t + column) + e
            vprod[n] = jnp.where(low_half, straight, -crossed) + flip_halves(
                jnp.where(low_half, crossed, straight)
            )
            cm = c * m
            eprod[n] = cm * cm
            return carry

        lax.fori_loop(0, 4, one_item, 0)

    def wait_regular(bits):
        s = flip(bits)
        remote(
            stage.at[s], regular.at[s], img2_send.at[bits], img2_recv.at[s], {"dom": y * 4 + s}
        ).wait_recv()

    def wait_extra(bits):
        s = flip(bits)
        remote(stage.at[4], extra.at[s], ext_send.at[bits], ext_recv.at[s], {"dom": y * 4 + s}).wait_recv()

    items_of(regular, q, 0)
    items_of(extra, q, 1)
    wait_extra(1)
    items_of(extra, flip(1), 1)
    ar1[z] = arx[0]
    for r in NEAR8:
        s = (z + r) % SLABS
        remote(arx.at[0], ar1.at[s], ar1_send.at[r], ar1_recv.at[s], {"slab": s}).wait_recv()
    total = ar1[0]
    for s in range(1, SLABS):
        total = total + ar1[s]
    arx[1] = total
    for r in FAR4:
        to = (y + r) % 4
        copy = remote(arx.at[1], ar2.at[y], ar2_send.at[r], ar2_recv.at[y], {"dom": to * 4 + q})
        copy.start()
        copies.append(copy)
    wait_regular(1)
    items_of(regular, flip(1), 0)
    wait_extra(2)
    copy = remote(
        extra.at[flip(2)], extra.at[flip(2)], ext_send.at[3], ext_recv.at[flip(2)], {"dom": y * 4 + flip(1)}
    )
    copy.start()
    copies.append(copy)
    ar2[y] = total
    for r in NEAR4:
        s = (y + r) % 4
        remote(arx.at[1], ar2.at[s], ar2_send.at[r], ar2_recv.at[s], {"dom": s * 4 + q}).wait_recv()
    total = ar2[0]
    for s in range(1, 4):
        total = total + ar2[s]
    arx[2] = total
    for r in FAR8:
        to = (g + r) % 8
        copy = remote(
            arx.at[2], ar3.at[g], ar3_send.at[r], ar3_recv.at[g], {"half": to // 4, "dom": y * 4 + to % 4}
        )
        copy.start()
        copies.append(copy)
    items_of(extra, flip(2), 1)
    wait_regular(2)
    items_of(regular, flip(2), 0)
    wait_extra(3)
    items_of(extra, flip(3), 1)
    wait_regular(3)
    items_of(regular, flip(3), 0)
    ar3[g] = total
    for r in NEAR8:
        s = (g + r) % 8
        remote(
            arx.at[2], ar3.at[s], ar3_send.at[r], ar3_recv.at[s], {"half": s // 4, "dom": y * 4 + s % 4}
        ).wait_recv()
    total = ar3[0]
    for s in range(1, 8):
        total = total + ar3[s]

    power = total[:, SHELLS : 2 * SHELLS] * total[:, 2 * SHELLS : 3 * SHELLS]
    fsc = total[:, :SHELLS] / jnp.sqrt(power + 1e-06)
    corr_ref[...] = fsc
    floor = jnp.maximum(fsc, 0.1)
    table0 = jnp.where(shifted, floor[:, 128:256], floor[:, 0:128])
    table1 = jnp.where(shifted, floor[:, 256:384], floor[:, 128:256])
    table0 = jnp.broadcast_to(table0, (ROWS, 128))
    table1 = jnp.broadcast_to(table1, (ROWS, 128))
    ld_shell.wait()
    for b in range(3):
        at = shell_of[:, 128 * b : 128 * b + 128]
        low = jnp.take_along_axis(table0, jnp.minimum(at, 127), axis=1)
        high = jnp.take_along_axis(table1, jnp.maximum(at - 128, 0), axis=1)
        weight_ref[:, 128 * b : 128 * b + 128] = jnp.where(at < 128, low, high)
    w = weight_ref[...]

    ld_col.wait()
    ld_rowt.wait()
    for half, start in enumerate((3, 7)):

        def weigh(j, carry):
            t = (z + start + j) % SLABS
            energies = []
            for k in range(4):
                prod[4 * half + j, :, BOX * k : BOX * k + BOX] = (vprod[4 * t + k] * w).astype(BF16)
                e = jnp.sum(eprod[4 * t + k] * w, axis=0, keepdims=True)
                energies.append(e[:, 0:128] + e[:, 128:256] + e[:, 256:384])
            energies = jnp.concatenate(energies, axis=0)
            part[t, 32:48, :] = jnp.concatenate(list(split3(energies)) + [jnp.zeros((4, 128), BF16)], axis=0)
            return carry

        lax.fori_loop(0, 4, weigh, 0)
        section = jnp.dot(
            prod[4 * half : 4 * half + 4].reshape(4 * ROWS, 4 * BOX), col[...], preferred_element_type=F32
        ).astype(BF16)
        stacked = jnp.concatenate(
            [
                jnp.concatenate(
                    [section[ROWS * j : ROWS * j + ROWS, :128], section[ROWS * j : ROWS * j + ROWS, 128:]],
                    axis=0,
                )
                for j in range(4)
            ],
            axis=1,
        )
        partial = jnp.dot(rowt[...], stacked, preferred_element_type=F32).astype(BF16)
        for j in range(4):
            part[(z + start + j) % SLABS, 0:32, :] = partial[:, 128 * j : 128 * j + 128]
        for j in (1, 2, 0, 3):
            r = (start + j) % SLABS
            if r == 0:
                continue
            to = (z + r) % SLABS
            copy = remote(part.at[to], parts_in.at[z], part_send.at[r], part_recv.at[z], {"slab": to})
            copy.start()
            copies.append(copy)

    link_copy.wait()

    def add_item(u, carry):
        e = u // 16
        before = link[u, 1]
        has = jnp.where(before >= 0, 1.0, 0.0)
        from_u = jnp.minimum(jnp.maximum(before, 0), SLOTS - 1)
        column = (u % 16) // 4
        t = u % 4
        c = ctf[meta_all[column, t, 0, 8 * e]]
        valid = meta_all[column, t, 0, 8 * e + 4].astype(F32)
        vprod[u] = contrib[u].astype(F32) + has * vprod[from_u]
        eprod[u] = (c * c) * valid + has * eprod[from_u]
        return carry

    lax.fori_loop(0, SLOTS, add_item, 0)
    whole = part[z].astype(F32)
    for r in NEAR8:
        s = (z + r) % SLABS
        remote(part.at[s], parts_in.at[s], part_send.at[r], part_recv.at[s], {"slab": s}).wait_recv()
        whole = whole + parts_in[s].astype(F32)
    best = jnp.max(whole[0:32], axis=0, keepdims=True)
    lane4 = lax.broadcasted_iota(I32, (4, 128), 1)
    row4 = lax.broadcasted_iota(I32, (4, 128), 0)
    top = jnp.max(jnp.where(lane4 // 32 == row4, best, -jnp.inf), axis=1, keepdims=True)
    energy = jnp.sum(whole[32:36] + (whole[36:40] + whole[40:44]), axis=1, keepdims=True)
    value = top / jnp.sqrt(energy + 1e-06)
    answer = jnp.sum(jnp.where(lane4 == row4, value, 0.0), axis=0, keepdims=True)
    ret_out[...] = answer

    def score_copy(e, r):
        return remote(
            ret_out, ret.at[d], ret_send.at[8 * e + r], ret_recv.at[d],
            {"dom": 2 * z + e, "slab": (z + r) % SLABS},
        )

    for r in FAR8:
        for e in range(2):
            score_copy(e, r).start()
    for e in range(2):
        pl.when(2 * z + e != d)(score_copy(e, 0).start)

    @pl.when(d // 2 == z)
    def _():
        ret[d] = answer

    def one_slice(r, carry):
        at = link[r, 0]
        has = jnp.where(at >= 0, 1.0, 0.0)
        at = jnp.minimum(jnp.maximum(at, 0), SLOTS - 1)
        inverse = 1.0 / weight_ref[...]
        top = has * vprod[at] + maps[r].astype(F32) * inverse
        new_ref[r] = top / (has * eprod[at] + inverse)
        return carry

    lax.fori_loop(0, ORI, one_slice, 0)

    for copy in copies:
        copy.wait_send()
    for e in range(2):
        for r in FAR8:
            score_copy(e, r).wait_send()
        pl.when(2 * z + e != d)(score_copy(e, 0).wait_send)
    for r in range(DOMS):
        s = (d + r) % DOMS
        copy = remote(ret_out, ret.at[s], ret_send.at[r], ret_recv.at[s], {"dom": s, "slab": d // 2})
        if r == 0:
            pl.when(d // 2 != z)(copy.wait_recv)
        else:
            copy.wait_recv()
    picked = [jnp.where(lane1 == 2 * (d % 2) + ranks[p], ret[owners[p]], 0.0) for p in range(PART)]
    picked = jnp.sum(jnp.concatenate(picked, axis=0), axis=1, keepdims=True)
    lane8 = lax.broadcasted_iota(I32, (PART, 128), 1)
    row8 = lax.broadcasted_iota(I32, (PART, 128), 0)
    scores = jnp.sum(jnp.where(lane8 == row8, picked, 0.0), axis=0, keepdims=True)
    score_ref[...] = scores[:, :PART]


DELIVER = 8


def deliver_kernel(score_in, corr_in, new_in, score_out, corr_out, new_out, sem):
    step = ORI // DELIVER
    writes = []
    for t in range(DELIVER):
        block = pl.ds(step * t, step)
        writes.append(pltpu.make_async_copy(new_in.at[block], new_out.at[block], sem.at[t]))
    for copy in writes:
        copy.start()
    score_out[...] = score_in[...]
    corr_out[...] = corr_in[0, :NSHELL]
    for copy in writes:
        copy.wait()


def deliver(scores, fsc, new_maps):
    hbm = pl.BlockSpec(memory_space=pl.ANY)
    vmem = pl.BlockSpec(memory_space=pltpu.VMEM)
    return pl.pallas_call(
        deliver_kernel,
        out_shape=(
            jax.ShapeDtypeStruct((1, PART), F32),
            jax.ShapeDtypeStruct((NSHELL,), F32),
            jax.ShapeDtypeStruct((ORI, ROWS, BOX), F32),
        ),
        in_specs=[vmem, vmem, vmem],
        out_specs=(vmem, vmem, hbm),
        scratch_shapes=[
            pltpu.SemaphoreType.DMA((DELIVER,)),
        ],
        compiler_params=pltpu.CompilerParams(vmem_limit_bytes=16 * 1024 * 1024),
        name="deliver",
    )(scores, fsc, new_maps)


def run_main(*operands):
    hbm = pl.BlockSpec(memory_space=pltpu.HBM)
    vmem = pl.BlockSpec(memory_space=pltpu.VMEM)
    v = pltpu.VMEM
    smem = pltpu.SMEM
    dma = pltpu.SemaphoreType.DMA
    return pl.pallas_call(
        main_kernel,
        out_shape=(
            pltpu.VMEM((1, PART), F32),
            pltpu.VMEM((1, SHELLS), F32),
            pltpu.VMEM((ORI, ROWS, BOX), F32),
        ),
        in_specs=[hbm] * 15,
        out_specs=(vmem, vmem, vmem),
        scratch_shapes=[
            smem((PART,), I32), smem((2, PART), I32), smem((PART,), I32), smem((CLASSES,), F32),
            smem((512,), I32),
            v((PART, ROWS, BOX), BF16),
            v((ORI, ROWS, BOX), BF16),
            v((ORI // 2, ROWS, BOX), BF16),
            v((ROWS, BOX), I32),
            v((ROWS, 256), I32),
            v((ROWS, BOX), F32),
            v((33, 8, BOX), F32),
            v((2, ROWS, 128), F32),
            v((4 * BOX, 256), BF16),
            v((SHIFTS, 2 * ROWS), BF16),
            v((BOX, 256), BF16),
            v((ROWS, BOX), F32),
            v((4, 5, ROWS, BOX), BF16),
            v((5, 4, ROWS, BOX), BF16),
            v((4, 4, ROWS, BOX), BF16),
            v((4, 4, ROWS, BOX), BF16),
            v((SLOTS, ROWS, BOX), BF16),
            v((SLOTS, ROWS, BOX), F32),
            v((SLOTS, ROWS, BOX), F32),
            v((CLASSES, ROWS, BOX), F32),
            v((33, 2, ROWS, 128), F32),
            v((4, 4, 1, 128), I32),
            v((4, 4, 1, 128), I32),
            v((4, 4, 1, 128), I32),
            smem((4, 4, 1, 128), I32),
            smem((4, 4, 1, 128), I32),
            v((SLOTS, 128), I32),
            smem((SLOTS, 128), I32),
            v((8, 1, 3 * SHELLS), F32),
            v((4, 1, 3 * SHELLS), F32),
            v((8, 1, 3 * SHELLS), F32),
            v((3, 1, 3 * SHELLS), F32),
            v((SLABS, ROWS, 4 * BOX), BF16),
            v((SLABS, 48, 128), BF16),
            v((SLABS, 48, 128), BF16),
            v((DOMS, 1, 128), F32),
            v((1, 128), F32),
            dma((15,)),
            dma((8,)),
            pltpu.SemaphoreType.REGULAR((3,)),
            dma((NCHUNK,)), dma((NCHUNK,)),
            dma((4,)), dma((4,)),
            dma((4,)), dma((4,)),
            dma((4,)), dma((4,)),
            dma((4,)), dma((4,)),
            dma((4,)), dma((4,)),
            dma((8,)), dma((8,)),
            dma((4,)), dma((4,)),
            dma((8,)), dma((8,)),
            dma((8,)), dma((8,)),
            dma((16,)), dma((16,)),
        ],
        compiler_params=pltpu.CompilerParams(
            collective_id=0, has_side_effects=True, vmem_limit_bytes=44 * 1024 * 1024
        ),
        name="refine",
    )(*[pltpu.with_memory_space_constraint(x, pltpu.HBM) for x in operands])


def on_device(consts, images, orientation, offsets, defocus_class, defocus, ori_slot, half_maps):
    scores, fsc, new_maps = run_main(
        orientation[0], offsets[0].T, defocus_class[0], defocus, ori_slot, images[0], half_maps[0], *consts
    )
    scores, fsc, new_maps = deliver(scores, fsc, new_maps)
    return scores, new_maps[None], fsc


def solution(mesh):
    in_specs = (
        P("half", "dom", "slab", None),
        P("half", "dom"),
        P("half", "dom", None),
        P("half", "dom"),
        P(),
        P(),
        P("half", "dom", "slab", None),
    )
    out_specs = (P("half", "dom"), P("half", "dom", "slab", None), P())
    return jax.shard_map(
        functools.partial(on_device, tables()),
        mesh=mesh, in_specs=in_specs, out_specs=out_specs, check_vma=False,
    )
```

```python
import functools
import math

import jax
import jax.numpy as jnp
import ml_dtypes
import numpy as np
from jax import lax
from jax.experimental import pallas as pl
from jax.experimental.pallas import tpu as pltpu
from jax.sharding import PartitionSpec as P

BOX = 384
KX = 192
SHIFTS = 32
NSHELL = 267
ROWS = 48
SLABS = 8
DOMS = 16
PART = 8
ORI = 32
CLASSES = 16
SLOTS = 32
SHELLS = 384
CHUNK = 4
NCHUNK = 4
F32 = jnp.float32
BF16 = jnp.bfloat16
I32 = jnp.int32
MESH = pl.DeviceIdType.MESH
FAR8 = (4, 3, 5, 2, 6, 1, 7)
NEAR8 = FAR8[::-1]
FAR4 = (2, 1, 3)
NEAR4 = FAR4[::-1]


def tables():
    row = np.arange(BOX)
    ky = np.where(row < KX, row, row - BOX)
    kx = np.arange(KX)
    q = ky[:, None] ** 2 + kx[None, :] ** 2
    radius = np.floor(np.sqrt(q.astype(np.float64))).astype(np.int64)
    radius -= radius * radius > q
    radius += (radius + 1) * (radius + 1) <= q
    shell = np.clip(radius - 1, 0, NSHELL - 1)
    base = np.array([0, 0, 0, 128, 128, 0, 0, 0])
    local = shell.reshape(SLABS, ROWS, KX) - base[:, None, None]
    assert local.min() >= 0 and local.max() < 256
    shell_of = np.concatenate([local, local], axis=-1).astype(np.int32)
    ends = np.zeros((SLABS, ROWS, 256), np.int32)
    for s in range(256):
        ends[:, :, s] = (local <= s).sum(-1)
    freq = np.concatenate([q, q], axis=-1).reshape(SLABS, ROWS, BOX).astype(np.float32)
    freq = freq / np.float32(BOX * BOX)
    unit = np.float32(2.0 * math.pi / BOX)

    def trig(index):
        angle = (np.mod(index, BOX).astype(np.float32) * unit).astype(np.float32)
        return np.cos(angle).astype(np.float32), np.sin(angle).astype(np.float32)

    shift = np.arange(33) - 16
    cx, sx = trig(shift[:, None] * kx[None, :])
    tx = np.zeros((33, 8, BOX), np.float32)
    tx[:, 0] = np.concatenate([cx, cx], -1)
    tx[:, 1] = np.concatenate([sx, sx], -1)
    tx[:, 2] = np.concatenate([cx, -cx], -1)
    tx[:, 3] = np.concatenate([sx, -sx], -1)
    cy, sy = trig(ky[:, None] * shift[None, :])
    ty = np.zeros((SLABS, 2, ROWS, 128), np.float32)
    ty[:, 0, :, :33] = cy.reshape(SLABS, ROWS, 33)
    ty[:, 1, :, :33] = sy.reshape(SLABS, ROWS, 33)

    window = np.arange(SHIFTS) - SHIFTS // 2
    wcx, wsx = trig(kx[:, None] * window[None, :])
    wcy, wsy = trig(ky[:, None] * window[None, :])
    col_re = np.concatenate([wcx, -wsx], axis=0)
    col_im = np.concatenate([wsx, wcx], axis=0)
    col = np.zeros((4 * BOX, 256), np.float32)
    for k in range(4):
        col[k * BOX : (k + 1) * BOX, 32 * k : 32 * k + 32] = col_re
        col[k * BOX : (k + 1) * BOX, 128 + 32 * k : 160 + 32 * k] = col_im
    wcy = wcy.reshape(SLABS, ROWS, SHIFTS).transpose(0, 2, 1)
    wsy = wsy.reshape(SLABS, ROWS, SHIFTS).transpose(0, 2, 1)
    rowt = np.concatenate([wcy, -wsy], axis=-1)
    tri = (np.arange(BOX)[:, None] % KX <= np.arange(256)[None, :]).astype(np.float32)
    bf = ml_dtypes.bfloat16
    return (
        shell_of, ends, freq, tx, ty, col.astype(bf), rowt.astype(bf), tri.astype(bf),
    )


def flip_halves(x):
    return pltpu.roll(x, KX, 1)


def ctf_rows(freq, defocus):
    g = defocus * freq
    phi = math.atan2(0.1, 0.995)
    m = jnp.floor((g + phi) * (1.0 / math.pi) + 0.5)
    t = ((g - m * 3.140625) - m * 9.67653589793e-4) + phi
    odd = m - 2.0 * jnp.floor(m * 0.5)
    t2 = t * t
    p = -1.0 / 39916800.0
    for c in (1.0 / 362880.0, -1.0 / 5040.0, 1.0 / 120.0, -1.0 / 6.0, 1.0):
        p = p * t2 + c
    scale = math.sqrt(0.995 * 0.995 + 0.01)
    return (p * t) * ((2.0 * odd - 1.0) * scale)


def split3(x):
    hi = x.astype(BF16)
    rest = x - hi.astype(F32)
    mid = rest.astype(BF16)
    low = (rest - mid.astype(F32)).astype(BF16)
    return hi, mid, low


def main_kernel(
    ori_hbm, off_hbm, cls_hbm, defocus_hbm, slot_hbm, img_hbm, map_hbm,
    shell_hbm, ends_hbm, freq_hbm, tx_hbm, ty_hbm, col_hbm, rowt_hbm, tri_hbm,
    score_ref, corr_ref, new_ref,
    ori_ref, off_ref, cls_ref, defocus_ref, slot_ref,
    img, maps, other, shell_of, ends, freq, tx, ty, col, rowt, tri, weight_ref,
    packed, stage, regular, extra, contrib, vprod, eprod, ctf, eyb,
    meta_out, meta_stage, meta_in, meta_own, meta_all, link_v, link,
    ar1, ar2, arx, prod, part, parts_in, ret, ret_out,
    load_sem, own_sem, ring_sem, map_send, map_recv,
    img1_send, img1_recv, img2_send, img2_recv, ext_send, ext_recv,
    meta1_send, meta1_recv, meta2_send, meta2_recv,
    ar1_send, ar1_recv, ar2_send, ar2_recv,
    part_send, part_recv, ret_send, ret_recv,
):
    h = lax.axis_index("half")
    d = lax.axis_index("dom")
    z = lax.axis_index("slab")
    y = d // 4
    q = d % 4

    def flip(bits):
        hi = (q // 2 + bits // 2) % 2
        lo = (q % 2 + bits % 2) % 2
        return hi * 2 + lo

    def remote(src, dst, send, recv, where):
        return pltpu.make_async_remote_copy(
            src_ref=src, dst_ref=dst, send_sem=send, recv_sem=recv,
            device_id=where, device_id_type=MESH,
        )

    def signal(sem, where):
        pl.semaphore_signal(sem, inc=1, device_id=where, device_id_type=MESH)

    neighbours = (
        {"half": 1 - h}, {"half": 1 - h, "dom": y * 4 + flip(2)}, {"dom": y * 4 + flip(1)},
        {"dom": (y + 1) % 4 * 4 + q}, {"dom": (y + 3) % 4 * 4 + q},
        {"slab": (z + 1) % SLABS}, {"slab": (z + 7) % SLABS},
    )
    core = q % 2
    place_x = q // 2 * 2 + h
    along_z = []
    for r in (4, 3, 5, 2, 6, 1, 7, 0):
        for c in (1, 0):
            if r or c:
                to_z, to_core = (z + r) % SLABS, (core + c) % 2
                where = {"slab": to_z, "dom": y * 4 + q // 2 * 2 + to_core}
                along_z.append((where, z * 2 + core, to_z * 2 + to_core))
    in_plane = []
    for r in (2, 1, 3, 0):
        for c in (2, 1, 3, 0):
            if r or c:
                to_y, to_x = (y + r) % 4, (place_x + c) % 4
                where = {"half": to_x % 2, "dom": to_y * 4 + to_x // 2 * 2 + core}
                in_plane.append((where, y * 4 + place_x, to_y * 4 + to_x))

    def spread(source, peers, landing, sends, receives):
        for i, (where, mine, _) in enumerate(peers):
            copy = remote(source, landing.at[mine], sends.at[i], receives.at[mine], where)
            copy.start()
            copies.append(copy)

    def gather(source, peers, landing, sends, receives):
        for i, (where, _, theirs) in reversed(list(enumerate(peers))):
            remote(source, landing.at[theirs], sends.at[i], receives.at[theirs], where).wait_recv()
        total = landing[0]
        for i in range(1, 16):
            total = total + landing[i]
        return total

    barrier = pltpu.get_barrier_semaphore()
    for where in neighbours:
        signal(barrier, where)

    loads = [
        (ori_hbm, ori_ref), (off_hbm, off_ref), (cls_hbm, cls_ref), (slot_hbm, slot_ref),
        (defocus_hbm, defocus_ref), (img_hbm, img), (freq_hbm.at[z], freq), (ty_hbm.at[z], ty),
        (map_hbm, maps), (tri_hbm, tri), (ends_hbm.at[z], ends), (tx_hbm, tx),
        (shell_hbm.at[z], shell_of), (col_hbm, col), (rowt_hbm.at[z], rowt),
    ]
    loads = [pltpu.make_async_copy(a, b, load_sem.at[i]) for i, (a, b) in enumerate(loads)]
    for c in loads:
        c.start()
    ld_small = loads[:4]
    (ld_defocus, ld_img, ld_freq, ld_ty, ld_map, ld_tri, ld_ends, ld_tx, ld_shell, ld_col, ld_rowt) = loads[4:]

    for c in ld_small:
        c.wait()
    lane1 = lax.broadcasted_iota(I32, (1, 128), 1)
    owner_row = lax.broadcasted_iota(I32, (DOMS, 128), 0)
    lane16 = lax.broadcasted_iota(I32, (DOMS, 128), 1)
    owners = []
    ranks = []
    second = jnp.int32(0)
    message = jnp.zeros((DOMS, 128), I32)
    for p in range(PART):
        place = slot_ref[ori_ref[p]]
        owner = place // ORI
        rank = jnp.int32(0)
        for before in owners:
            rank = rank + jnp.where(before == owner, 1, 0)
        owners.append(owner)
        ranks.append(rank)
        second = jnp.where(rank == 1, p, second)
        fields = (cls_ref[p], off_ref[0, p] + 16, off_ref[1, p] + 16, place % ORI, jnp.int32(1), jnp.int32(p))
        at = lane16 - 8 * rank
        for f, value in enumerate(fields):
            message = jnp.where((owner_row == owner) & (at == f), value, message)
    for o in range(DOMS):
        meta_out[o // 4, o % 4] = message[o : o + 1]
    own_copy = pltpu.make_async_copy(meta_out, meta_own, own_sem.at[0])
    own_copy.start()

    pl.semaphore_wait(barrier, len(neighbours))

    map_copies = []
    for c in range(NCHUNK):
        source = map_hbm.at[pl.ds((1 - h) * (ORI // 2) + c * CHUNK, CHUNK)]
        copy = remote(
            source, other.at[pl.ds(c * CHUNK, CHUNK)], map_send.at[c], map_recv.at[c], {"half": 1 - h}
        )
        copy.start()
        map_copies.append(copy)
    copies = list(map_copies)

    def ring(k):
        for where in neighbours:
            signal(ring_sem.at[k], where)

    ring(0)

    own_copy.wait()
    ld_img.wait()

    def pack(o, carry):
        packed[o // 4, o % 4] = img[meta_own[o // 4, o % 4, 0, 5]]
        return carry

    lax.fori_loop(0, DOMS, pack, 0)
    for t in range(4):
        packed[t, 4] = img[second]
    pl.semaphore_wait(ring_sem.at[0], len(neighbours))
    ring(1)

    for r in FAR4:
        to = (y + r) % 4
        copy = remote(
            meta_out.at[to], meta_stage.at[:, y], meta1_send.at[r], meta1_recv.at[y], {"dom": to * 4 + q}
        )
        copy.start()
        copies.append(copy)
    for r in FAR4:
        to = (y + r) % 4
        copy = remote(packed.at[to], stage.at[:, y], img1_send.at[r], img1_recv.at[y], {"dom": to * 4 + q})
        copy.start()
        copies.append(copy)
    own_img = pltpu.make_async_copy(packed.at[y], stage.at[:, y], own_sem.at[1])
    own_img.start()
    own_meta = pltpu.make_async_copy(meta_out.at[y], meta_stage.at[:, y], own_sem.at[2])
    own_meta.start()

    ld_freq.wait()
    ld_defocus.wait()

    def one_class(k, carry):
        ctf[k] = ctf_rows(freq[...], defocus_ref[k])
        return carry

    lax.fori_loop(0, CLASSES, one_class, 0)
    pl.semaphore_wait(ring_sem.at[1], len(neighbours))
    ring(2)
    ld_ty.wait()
    for part_of in range(2):
        for s in range(33):
            eyb[s, part_of] = jnp.broadcast_to(ty[part_of, :, s : s + 1], (ROWS, 128))

    for r in FAR4:
        s = (y + r) % 4
        remote(meta_out.at[s], meta_stage.at[:, s], meta1_send.at[r], meta1_recv.at[s], {"dom": s * 4 + q}).wait_recv()
    own_meta.wait()
    for bits in (3, 2, 1):
        to = flip(bits)
        copy = remote(
            meta_stage.at[to], meta_in.at[q], meta2_send.at[bits], meta2_recv.at[q], {"dom": y * 4 + to}
        )
        copy.start()
        copies.append(copy)
    last_meta = pltpu.make_async_copy(meta_stage.at[q], meta_in.at[q], own_sem.at[3])
    last_meta.start()

    ld_map.wait()

    def own_power(i, total):
        m = maps[i].astype(F32)
        return total + m * m

    own_sq = lax.fori_loop(0, ORI, own_power, jnp.zeros((ROWS, BOX), F32))
    pl.semaphore_wait(ring_sem.at[2], len(neighbours))
    ring(3)
    ld_tri.wait()
    ld_ends.wait()

    def shell_sums(values):
        running = jnp.dot(jnp.concatenate(split3(values), axis=0), tri[...], preferred_element_type=F32)
        c = running[:ROWS] + (running[ROWS : 2 * ROWS] + running[2 * ROWS :])
        blocks = []
        for b in range(2):
            e = ends[:, 128 * b : 128 * b + 128]
            low = jnp.take_along_axis(c[:, :128], jnp.clip(e - 1, 0, 127), axis=1)
            high = jnp.take_along_axis(c[:, 128:], jnp.clip(e - 129, 0, 127), axis=1)
            got = jnp.where(e > 128, high, jnp.where(e > 0, low, 0.0))
            blocks.append(jnp.sum(got, axis=0, keepdims=True))
        first = blocks[0] - jnp.where(lane1 == 0, 0.0, pltpu.roll(blocks[0], 1, 1))
        carry_in = jnp.where(lane1 == 0, blocks[0][:, 127:128], pltpu.roll(blocks[1], 1, 1))
        return first, blocks[1] - carry_in

    power_sums = shell_sums(own_sq)
    cross = jnp.zeros((ROWS, BOX), F32)
    for c in range(NCHUNK):
        if c == NCHUNK - 1:
            for r in FAR4:
                s = (y + r) % 4
                remote(
                    packed.at[s], stage.at[:, s], img1_send.at[r], img1_recv.at[s], {"dom": s * 4 + q}
                ).wait_recv()
            own_img.wait()
            for kind, (src, dst, send, recv) in enumerate(
                ((stage.at[4], extra, ext_send, ext_recv), (stage.at[flip(1)], regular, img2_send, img2_recv))
            ):
                copy = remote(src, dst.at[q], send.at[1], recv.at[q], {"dom": y * 4 + flip(1)})
                copy.start()
                copies.append(copy)
            own_regular = pltpu.make_async_copy(stage.at[q], regular.at[q], own_sem.at[4])
            own_regular.start()
            own_extra = pltpu.make_async_copy(stage.at[4], extra.at[q], own_sem.at[5])
            own_extra.start()
        map_copies[c].wait_recv()

        def cross_term(i, total):
            mine = maps[h * (ORI // 2) + c * CHUNK + i].astype(F32)
            return total + mine * other[c * CHUNK + i].astype(F32)

        cross = lax.fori_loop(0, CHUNK, cross_term, cross)

    copy = remote(stage.at[4], extra.at[q], ext_send.at[2], ext_recv.at[q], {"dom": y * 4 + flip(2)})
    copy.start()
    copies.append(copy)
    for bits in (2, 3):
        to = flip(bits)
        copy = remote(stage.at[to], regular.at[q], img2_send.at[bits], img2_recv.at[q], {"dom": y * 4 + to})
        copy.start()
        copies.append(copy)

    pl.semaphore_wait(ring_sem.at[3], len(neighbours))

    sums = (shell_sums(cross), power_sums)
    shifted = (z == 3) | (z == 4)
    zero = jnp.zeros((1, 128), F32)
    for v in range(3):
        s0, s1 = sums[min(v, 1)]
        for b in range(3):
            block = jnp.where(shifted, (zero, s0, s1)[b], (s0, s1, zero)[b])
            if v > 0:
                block = jnp.where(h == v - 1, block, zero)
            arx[0, :, SHELLS * v + 128 * b : SHELLS * v + 128 * b + 128] = block

    spread(arx.at[0], along_z, ar1, ar1_send, ar1_recv)
    ar1[z * 2 + core] = arx[0]

    last_meta.wait()
    for bits in (1, 2, 3):
        s = flip(bits)
        remote(meta_stage.at[s], meta_in.at[s], meta2_send.at[bits], meta2_recv.at[s], {"dom": y * 4 + s}).wait_recv()
    to_smem = pltpu.make_async_copy(meta_in, meta_all, own_sem.at[6])
    to_smem.start()

    numbers = jnp.concatenate([meta_in[c, t] for c in range(4) for t in range(4)], axis=0).astype(F32)

    def field(f):
        return jnp.sum(jnp.where(lane16 == f, numbers, 0.0), axis=1, keepdims=True)

    key = jnp.concatenate(
        [jnp.where(field(8 * e + 4) > 0.5, field(8 * e + 3), -1.0) for e in range(2)], axis=0
    )
    item_lane = lax.broadcasted_iota(I32, (SLOTS, 128), 1)
    item_row = lax.broadcasted_iota(I32, (SLOTS, 128), 0)
    across = jnp.sum(jnp.where(item_lane == item_row, key, 0.0), axis=0, keepdims=True)
    where_f = item_lane.astype(F32)
    last = jnp.max(
        jnp.where((across == item_row.astype(F32)) & (item_lane < SLOTS), where_f, -1.0), axis=1, keepdims=True
    )
    same = (across == key) & (item_lane < item_row) & (key >= 0.0)
    previous = jnp.max(jnp.where(same, where_f, -1.0), axis=1, keepdims=True)
    link_v[...] = jnp.where(item_lane == 0, last, jnp.where(item_lane == 1, previous, 0.0)).astype(I32)
    link_copy = pltpu.make_async_copy(link_v, link, own_sem.at[7])
    link_copy.start()

    ld_tx.wait()
    own_regular.wait()
    own_extra.wait()
    to_smem.wait()
    low_half = lax.broadcasted_iota(I32, (ROWS, BOX), 1) < KX

    def items_of(source, column, e):
        def one_item(t, carry):
            at = 8 * e
            phase_x = tx[meta_all[column, t, 0, at + 1]]
            phase_y = eyb[meta_all[column, t, 0, at + 2]]
            cy = jnp.concatenate([phase_y[0]] * 3, axis=1)
            sy = jnp.concatenate([phase_y[1]] * 3, axis=1)
            cos_t = phase_x[0:1] * cy - phase_x[1:2] * sy
            sin_t = phase_x[3:4] * cy + phase_x[2:3] * sy
            x = source[column, t].astype(F32)
            c = ctf[meta_all[column, t, 0, at]] * meta_all[column, t, 0, at + 4].astype(F32)
            zz = c * (x * cos_t + flip_halves(x) * sin_t)
            contrib[16 * e + 4 * column + t] = zz.astype(BF16)
            m = maps[meta_all[column, t, 0, at + 3]].astype(F32)
            straight = zz * m
            crossed = zz * flip_halves(m)
            n = 2 * (4 * t + column) + e
            vprod[n] = jnp.where(low_half, straight, -crossed) + flip_halves(
                jnp.where(low_half, crossed, straight)
            )
            cm = c * m
            eprod[n] = cm * cm
            return carry

        lax.fori_loop(0, 4, one_item, 0)

    def wait_regular(bits):
        s = flip(bits)
        remote(
            stage.at[s], regular.at[s], img2_send.at[bits], img2_recv.at[s], {"dom": y * 4 + s}
        ).wait_recv()

    def wait_extra(bits):
        s = flip(bits)
        remote(stage.at[4], extra.at[s], ext_send.at[bits], ext_recv.at[s], {"dom": y * 4 + s}).wait_recv()

    items_of(regular, q, 0)
    items_of(extra, q, 1)
    wait_extra(1)
    items_of(extra, flip(1), 1)
    wait_regular(1)
    items_of(regular, flip(1), 0)
    total = gather(arx.at[0], along_z, ar1, ar1_send, ar1_recv)
    arx[1] = total
    spread(arx.at[1], in_plane, ar2, ar2_send, ar2_recv)
    ar2[y * 4 + place_x] = total
    wait_extra(2)
    copy = remote(
        extra.at[flip(2)], extra.at[flip(2)], ext_send.at[3], ext_recv.at[flip(2)], {"dom": y * 4 + flip(1)}
    )
    copy.start()
    copies.append(copy)
    items_of(extra, flip(2), 1)
    wait_regular(2)
    items_of(regular, flip(2), 0)
    wait_extra(3)
    items_of(extra, flip(3), 1)
    wait_regular(3)
    items_of(regular, flip(3), 0)
    total = gather(arx.at[1], in_plane, ar2, ar2_send, ar2_recv)

    power = total[:, SHELLS : 2 * SHELLS] * total[:, 2 * SHELLS : 3 * SHELLS]
    fsc = total[:, :SHELLS] / jnp.sqrt(power + 1e-06)
    corr_ref[...] = fsc[0, :NSHELL]
    floor = jnp.maximum(fsc, 0.1)
    table0 = jnp.where(shifted, floor[:, 128:256], floor[:, 0:128])
    table1 = jnp.where(shifted, floor[:, 256:384], floor[:, 128:256])
    table0 = jnp.broadcast_to(table0, (ROWS, 128))
    table1 = jnp.broadcast_to(table1, (ROWS, 128))
    ld_shell.wait()
    for b in range(3):
        at = shell_of[:, 128 * b : 128 * b + 128]
        low = jnp.take_along_axis(table0, jnp.minimum(at, 127), axis=1)
        high = jnp.take_along_axis(table1, jnp.maximum(at - 128, 0), axis=1)
        weight_ref[:, 128 * b : 128 * b + 128] = jnp.where(at < 128, low, high)
    w = weight_ref[...]

    ld_col.wait()
    ld_rowt.wait()
    for half, start in enumerate((3, 7)):

        def weigh(j, carry):
            t = (z + start + j) % SLABS
            energies = []
            for k in range(4):
                prod[4 * half + j, :, BOX * k : BOX * k + BOX] = (vprod[4 * t + k] * w).astype(BF16)
                e = jnp.sum(eprod[4 * t + k] * w, axis=0, keepdims=True)
                energies.append(e[:, 0:128] + e[:, 128:256] + e[:, 256:384])
            energies = jnp.concatenate(energies, axis=0)
            part[t, 32:48, :] = jnp.concatenate(list(split3(energies)) + [jnp.zeros((4, 128), BF16)], axis=0)
            return carry

        lax.fori_loop(0, 4, weigh, 0)
        section = jnp.dot(
            prod[4 * half : 4 * half + 4].reshape(4 * ROWS, 4 * BOX), col[...], preferred_element_type=F32
        ).astype(BF16)
        stacked = jnp.concatenate(
            [
                jnp.concatenate(
                    [section[ROWS * j : ROWS * j + ROWS, :128], section[ROWS * j : ROWS * j + ROWS, 128:]],
                    axis=0,
                )
                for j in range(4)
            ],
            axis=1,
        )
        partial = jnp.dot(rowt[...], stacked, preferred_element_type=F32).astype(BF16)
        for j in range(4):
            part[(z + start + j) % SLABS, 0:32, :] = partial[:, 128 * j : 128 * j + 128]
        for j in (1, 2, 0, 3):
            r = (start + j) % SLABS
            if r == 0:
                continue
            to = (z + r) % SLABS
            copy = remote(part.at[to], parts_in.at[z], part_send.at[r], part_recv.at[z], {"slab": to})
            copy.start()
            copies.append(copy)

    link_copy.wait()

    def add_item(u, carry):
        e = u // 16
        before = link[u, 1]
        has = jnp.where(before >= 0, 1.0, 0.0)
        from_u = jnp.minimum(jnp.maximum(before, 0), SLOTS - 1)
        column = (u % 16) // 4
        t = u % 4
        c = ctf[meta_all[column, t, 0, 8 * e]]
        valid = meta_all[column, t, 0, 8 * e + 4].astype(F32)
        vprod[u] = contrib[u].astype(F32) + has * vprod[from_u]
        eprod[u] = (c * c) * valid + has * eprod[from_u]
        return carry

    lax.fori_loop(0, SLOTS, add_item, 0)
    whole = part[z].astype(F32)
    for r in NEAR8:
        s = (z + r) % SLABS
        remote(part.at[s], parts_in.at[s], part_send.at[r], part_recv.at[s], {"slab": s}).wait_recv()
        whole = whole + parts_in[s].astype(F32)
    best = jnp.max(whole[0:32], axis=0, keepdims=True)
    lane4 = lax.broadcasted_iota(I32, (4, 128), 1)
    row4 = lax.broadcasted_iota(I32, (4, 128), 0)
    top = jnp.max(jnp.where(lane4 // 32 == row4, best, -jnp.inf), axis=1, keepdims=True)
    energy = jnp.sum(whole[32:36] + (whole[36:40] + whole[40:44]), axis=1, keepdims=True)
    value = top / jnp.sqrt(energy + 1e-06)
    answer = jnp.sum(jnp.where(lane4 == row4, value, 0.0), axis=0, keepdims=True)
    ret_out[...] = answer

    def score_copy(e, r):
        return remote(
            ret_out, ret.at[d], ret_send.at[8 * e + r], ret_recv.at[d],
            {"dom": 2 * z + e, "slab": (z + r) % SLABS},
        )

    for r in FAR8:
        for e in range(2):
            score_copy(e, r).start()
    for e in range(2):
        pl.when(2 * z + e != d)(score_copy(e, 0).start)

    @pl.when(d // 2 == z)
    def _():
        ret[d] = answer

    def one_slice(r, carry):
        at = link[r, 0]
        has = jnp.where(at >= 0, 1.0, 0.0)
        at = jnp.minimum(jnp.maximum(at, 0), SLOTS - 1)
        inverse = 1.0 / weight_ref[...]
        top = has * vprod[at] + maps[r].astype(F32) * inverse
        new_ref[r] = top / (has * eprod[at] + inverse)
        return carry

    lax.fori_loop(0, ORI, one_slice, 0)

    for copy in copies:
        copy.wait_send()
    for e in range(2):
        for r in FAR8:
            score_copy(e, r).wait_send()
        pl.when(2 * z + e != d)(score_copy(e, 0).wait_send)
    for r in range(DOMS):
        s = (d + r) % DOMS
        copy = remote(ret_out, ret.at[s], ret_send.at[r], ret_recv.at[s], {"dom": s, "slab": d // 2})
        if r == 0:
            pl.when(d // 2 != z)(copy.wait_recv)
        else:
            copy.wait_recv()
    picked = [jnp.where(lane1 == 2 * (d % 2) + ranks[p], ret[owners[p]], 0.0) for p in range(PART)]
    picked = jnp.sum(jnp.concatenate(picked, axis=0), axis=1, keepdims=True)
    lane8 = lax.broadcasted_iota(I32, (PART, 128), 1)
    row8 = lax.broadcasted_iota(I32, (PART, 128), 0)
    scores = jnp.sum(jnp.where(lane8 == row8, picked, 0.0), axis=0, keepdims=True)
    score_ref[...] = scores[:, :PART]


DELIVER = 8


def deliver_kernel(score_in, corr_in, new_in, score_out, corr_out, new_out, sem):
    step = ORI // DELIVER
    writes = []
    for t in range(DELIVER):
        block = pl.ds(step * t, step)
        writes.append(pltpu.make_async_copy(new_in.at[block], new_out.at[block], sem.at[t]))
    writes.append(pltpu.make_async_copy(score_in, score_out, sem.at[DELIVER]))
    writes.append(pltpu.make_async_copy(corr_in, corr_out, sem.at[DELIVER + 1]))
    for copy in writes:
        copy.start()
    for copy in writes:
        copy.wait()


def deliver(scores, fsc, new_maps):
    hbm = pl.BlockSpec(memory_space=pl.ANY)
    vmem = pl.BlockSpec(memory_space=pltpu.VMEM)
    return pl.pallas_call(
        deliver_kernel,
        out_shape=(
            jax.ShapeDtypeStruct((1, PART), F32),
            jax.ShapeDtypeStruct((NSHELL,), F32),
            jax.ShapeDtypeStruct((ORI, ROWS, BOX), F32),
        ),
        in_specs=[vmem, vmem, vmem],
        out_specs=(hbm, hbm, hbm),
        scratch_shapes=[
            pltpu.SemaphoreType.DMA((DELIVER + 2,)),
        ],
        compiler_params=pltpu.CompilerParams(vmem_limit_bytes=16 * 1024 * 1024),
        name="deliver",
    )(scores, fsc, new_maps)


def run_main(*operands):
    hbm = pl.BlockSpec(memory_space=pltpu.HBM)
    vmem = pl.BlockSpec(memory_space=pltpu.VMEM)
    v = pltpu.VMEM
    smem = pltpu.SMEM
    dma = pltpu.SemaphoreType.DMA
    return pl.pallas_call(
        main_kernel,
        out_shape=(
            pltpu.VMEM((1, PART), F32),
            pltpu.VMEM((NSHELL,), F32),
            pltpu.VMEM((ORI, ROWS, BOX), F32),
        ),
        in_specs=[hbm] * 15,
        out_specs=(vmem, vmem, vmem),
        scratch_shapes=[
            smem((PART,), I32), smem((2, PART), I32), smem((PART,), I32), smem((CLASSES,), F32),
            smem((512,), I32),
            v((PART, ROWS, BOX), BF16),
            v((ORI, ROWS, BOX), BF16),
            v((ORI // 2, ROWS, BOX), BF16),
            v((ROWS, BOX), I32),
            v((ROWS, 256), I32),
            v((ROWS, BOX), F32),
            v((33, 8, BOX), F32),
            v((2, ROWS, 128), F32),
            v((4 * BOX, 256), BF16),
            v((SHIFTS, 2 * ROWS), BF16),
            v((BOX, 256), BF16),
            v((ROWS, BOX), F32),
            v((4, 5, ROWS, BOX), BF16),
            v((5, 4, ROWS, BOX), BF16),
            v((4, 4, ROWS, BOX), BF16),
            v((4, 4, ROWS, BOX), BF16),
            v((SLOTS, ROWS, BOX), BF16),
            v((SLOTS, ROWS, BOX), F32),
            v((SLOTS, ROWS, BOX), F32),
            v((CLASSES, ROWS, BOX), F32),
            v((33, 2, ROWS, 128), F32),
            v((4, 4, 1, 128), I32),
            v((4, 4, 1, 128), I32),
            v((4, 4, 1, 128), I32),
            smem((4, 4, 1, 128), I32),
            smem((4, 4, 1, 128), I32),
            v((SLOTS, 128), I32),
            smem((SLOTS, 128), I32),
            v((16, 1, 3 * SHELLS), F32),
            v((16, 1, 3 * SHELLS), F32),
            v((2, 1, 3 * SHELLS), F32),
            v((SLABS, ROWS, 4 * BOX), BF16),
            v((SLABS, 48, 128), BF16),
            v((SLABS, 48, 128), BF16),
            v((DOMS, 1, 128), F32),
            v((1, 128), F32),
            dma((15,)),
            dma((8,)),
            pltpu.SemaphoreType.REGULAR((4,)),
            dma((NCHUNK,)), dma((NCHUNK,)),
            dma((4,)), dma((4,)),
            dma((4,)), dma((4,)),
            dma((4,)), dma((4,)),
            dma((4,)), dma((4,)),
            dma((4,)), dma((4,)),
            dma((16,)), dma((16,)),
            dma((16,)), dma((16,)),
            dma((8,)), dma((8,)),
            dma((16,)), dma((16,)),
        ],
        compiler_params=pltpu.CompilerParams(
            collective_id=0, has_side_effects=True, vmem_limit_bytes=44 * 1024 * 1024
        ),
        name="refine",
    )(*[pltpu.with_memory_space_constraint(x, pltpu.HBM) for x in operands])


def on_device(consts, images, orientation, offsets, defocus_class, defocus, ori_slot, half_maps):
    scores, fsc, new_maps = run_main(
        orientation[0], offsets[0].T, defocus_class[0], defocus, ori_slot, images[0], half_maps[0], *consts
    )
    scores, fsc, new_maps = deliver(scores, fsc, new_maps)
    return scores, new_maps[None], fsc


def solution(mesh):
    in_specs = (
        P("half", "dom", "slab", None),
        P("half", "dom"),
        P("half", "dom", None),
        P("half", "dom"),
        P(),
        P(),
        P("half", "dom", "slab", None),
    )
    out_specs = (P("half", "dom"), P("half", "dom", "slab", None), P())
    return jax.shard_map(
        functools.partial(on_device, tables()),
        mesh=mesh, in_specs=in_specs, out_specs=out_specs, check_vma=False,
    )
```

```python
import functools
import math

import jax
import jax.numpy as jnp
import ml_dtypes
import numpy as np
from jax import lax
from jax.experimental import pallas as pl
from jax.experimental.pallas import tpu as pltpu
from jax.sharding import PartitionSpec as P

BOX = 384
KX = 192
SHIFTS = 32
NSHELL = 267
ROWS = 48
SLABS = 8
DOMS = 16
PART = 8
ORI = 32
CLASSES = 16
SLOTS = 32
SHELLS = 384
CHUNK = 4
NCHUNK = 4
F32 = jnp.float32
BF16 = jnp.bfloat16
I32 = jnp.int32
MESH = pl.DeviceIdType.MESH
FAR8 = (4, 3, 5, 2, 6, 1, 7)
NEAR8 = FAR8[::-1]
FAR4 = (2, 1, 3)
NEAR4 = FAR4[::-1]


def tables():
    row = np.arange(BOX)
    ky = np.where(row < KX, row, row - BOX)
    kx = np.arange(KX)
    q = ky[:, None] ** 2 + kx[None, :] ** 2
    radius = np.floor(np.sqrt(q.astype(np.float64))).astype(np.int64)
    radius -= radius * radius > q
    radius += (radius + 1) * (radius + 1) <= q
    shell = np.clip(radius - 1, 0, NSHELL - 1)
    base = np.array([0, 0, 0, 128, 128, 0, 0, 0])
    local = shell.reshape(SLABS, ROWS, KX) - base[:, None, None]
    assert local.min() >= 0 and local.max() < 256
    shell_of = np.concatenate([local, local], axis=-1).astype(np.int32)
    ends = np.zeros((SLABS, ROWS, 256), np.int32)
    for s in range(256):
        ends[:, :, s] = (local <= s).sum(-1)
    freq = np.concatenate([q, q], axis=-1).reshape(SLABS, ROWS, BOX).astype(np.float32)
    freq = freq / np.float32(BOX * BOX)
    unit = np.float32(2.0 * math.pi / BOX)

    def trig(index):
        angle = (np.mod(index, BOX).astype(np.float32) * unit).astype(np.float32)
        return np.cos(angle).astype(np.float32), np.sin(angle).astype(np.float32)

    shift = np.arange(33) - 16
    cx, sx = trig(shift[:, None] * kx[None, :])
    tx = np.zeros((33, 8, BOX), np.float32)
    tx[:, 0] = np.concatenate([cx, cx], -1)
    tx[:, 1] = np.concatenate([sx, sx], -1)
    tx[:, 2] = np.concatenate([cx, -cx], -1)
    tx[:, 3] = np.concatenate([sx, -sx], -1)
    cy, sy = trig(ky[:, None] * shift[None, :])
    ty = np.zeros((SLABS, 2, ROWS, 128), np.float32)
    ty[:, 0, :, :33] = cy.reshape(SLABS, ROWS, 33)
    ty[:, 1, :, :33] = sy.reshape(SLABS, ROWS, 33)

    window = np.arange(SHIFTS) - SHIFTS // 2
    wcx, wsx = trig(kx[:, None] * window[None, :])
    wcy, wsy = trig(ky[:, None] * window[None, :])
    col_re = np.concatenate([wcx, -wsx], axis=0)
    col_im = np.concatenate([wsx, wcx], axis=0)
    col = np.zeros((4 * BOX, 256), np.float32)
    for k in range(4):
        col[k * BOX : (k + 1) * BOX, 32 * k : 32 * k + 32] = col_re
        col[k * BOX : (k + 1) * BOX, 128 + 32 * k : 160 + 32 * k] = col_im
    wcy = wcy.reshape(SLABS, ROWS, SHIFTS).transpose(0, 2, 1)
    wsy = wsy.reshape(SLABS, ROWS, SHIFTS).transpose(0, 2, 1)
    rowt = np.concatenate([wcy, -wsy], axis=-1)
    tri = (np.arange(BOX)[:, None] % KX <= np.arange(256)[None, :]).astype(np.float32)
    bf = ml_dtypes.bfloat16
    return (
        shell_of, ends, freq, tx, ty, col.astype(bf), rowt.astype(bf), tri.astype(bf),
    )


def flip_halves(x):
    return pltpu.roll(x, KX, 1)


def ctf_rows(freq, defocus):
    g = defocus * freq
    phi = math.atan2(0.1, 0.995)
    m = jnp.floor((g + phi) * (1.0 / math.pi) + 0.5)
    t = ((g - m * 3.140625) - m * 9.67653589793e-4) + phi
    odd = m - 2.0 * jnp.floor(m * 0.5)
    t2 = t * t
    p = -1.0 / 39916800.0
    for c in (1.0 / 362880.0, -1.0 / 5040.0, 1.0 / 120.0, -1.0 / 6.0, 1.0):
        p = p * t2 + c
    scale = math.sqrt(0.995 * 0.995 + 0.01)
    return (p * t) * ((2.0 * odd - 1.0) * scale)


def split3(x):
    hi = x.astype(BF16)
    rest = x - hi.astype(F32)
    mid = rest.astype(BF16)
    low = (rest - mid.astype(F32)).astype(BF16)
    return hi, mid, low


def main_kernel(
    ori_hbm, off_hbm, cls_hbm, defocus_hbm, slot_hbm, img_hbm, map_hbm,
    shell_hbm, ends_hbm, freq_hbm, tx_hbm, ty_hbm, col_hbm, rowt_hbm, tri_hbm,
    score_ref, corr_ref, new_ref,
    ori_ref, off_ref, cls_ref, defocus_ref, slot_ref,
    img, maps, other, shell_of, ends, freq, tx, ty, col, rowt, tri, weight_ref,
    packed, stage, regular, extra, contrib, vprod, eprod, ctf, eyb,
    meta_out, meta_stage, meta_in, meta_own, meta_all, link_v, link,
    ar1, ar2, arx, prod, part, parts_in, ret, ret_out,
    load_sem, own_sem, ring_sem, map_send, map_recv,
    img1_send, img1_recv, img2_send, img2_recv, ext_send, ext_recv,
    meta1_send, meta1_recv, meta2_send, meta2_recv,
    ar1_send, ar1_recv, ar2_send, ar2_recv,
    part_send, part_recv, ret_send, ret_recv,
):
    h = lax.axis_index("half")
    d = lax.axis_index("dom")
    z = lax.axis_index("slab")
    y = d // 4
    q = d % 4

    def flip(bits):
        hi = (q // 2 + bits // 2) % 2
        lo = (q % 2 + bits % 2) % 2
        return hi * 2 + lo

    def remote(src, dst, send, recv, where):
        return pltpu.make_async_remote_copy(
            src_ref=src, dst_ref=dst, send_sem=send, recv_sem=recv,
            device_id=where, device_id_type=MESH,
        )

    def signal(sem, where):
        pl.semaphore_signal(sem, inc=1, device_id=where, device_id_type=MESH)

    neighbours = (
        {"half": 1 - h}, {"half": 1 - h, "dom": y * 4 + flip(2)}, {"dom": y * 4 + flip(1)},
        {"dom": (y + 1) % 4 * 4 + q}, {"dom": (y + 3) % 4 * 4 + q},
        {"slab": (z + 1) % SLABS}, {"slab": (z + 7) % SLABS},
    )
    core = q % 2
    place_x = q // 2 * 2 + h
    along_z = []
    for r in (4, 3, 5, 2, 6, 1, 7, 0):
        for c in (1, 0):
            if r or c:
                to_z, to_core = (z + r) % SLABS, (core + c) % 2
                where = {"slab": to_z, "dom": y * 4 + q // 2 * 2 + to_core}
                along_z.append((where, z * 2 + core, to_z * 2 + to_core))
    in_plane = []
    for r in (2, 1, 3, 0):
        for c in (2, 1, 3, 0):
            if r or c:
                to_y, to_x = (y + r) % 4, (place_x + c) % 4
                where = {"half": to_x % 2, "dom": to_y * 4 + to_x // 2 * 2 + core}
                in_plane.append((where, y * 4 + place_x, to_y * 4 + to_x))

    def spread(source, peers, landing, sends, receives):
        for i, (where, mine, _) in enumerate(peers):
            copy = remote(source, landing.at[mine], sends.at[i], receives.at[mine], where)
            copy.start()
            copies.append(copy)

    def gather(source, peers, landing, sends, receives):
        for i, (where, _, theirs) in reversed(list(enumerate(peers))):
            remote(source, landing.at[theirs], sends.at[i], receives.at[theirs], where).wait_recv()
        total = landing[0]
        for i in range(1, 16):
            total = total + landing[i]
        return total

    barrier = pltpu.get_barrier_semaphore()
    for where in neighbours:
        signal(barrier, where)

    loads = [
        (ori_hbm, ori_ref), (off_hbm, off_ref), (cls_hbm, cls_ref), (slot_hbm, slot_ref),
        (defocus_hbm, defocus_ref), (img_hbm, img), (freq_hbm.at[z], freq), (ty_hbm.at[z], ty),
        (map_hbm, maps), (tri_hbm, tri), (ends_hbm.at[z], ends), (tx_hbm, tx),
        (shell_hbm.at[z], shell_of), (col_hbm, col), (rowt_hbm.at[z], rowt),
    ]
    loads = [pltpu.make_async_copy(a, b, load_sem.at[i]) for i, (a, b) in enumerate(loads)]
    for c in loads:
        c.start()
    ld_small = loads[:4]
    (ld_defocus, ld_img, ld_freq, ld_ty, ld_map, ld_tri, ld_ends, ld_tx, ld_shell, ld_col, ld_rowt) = loads[4:]

    for c in ld_small:
        c.wait()
    lane1 = lax.broadcasted_iota(I32, (1, 128), 1)
    owner_row = lax.broadcasted_iota(I32, (DOMS, 128), 0)
    lane16 = lax.broadcasted_iota(I32, (DOMS, 128), 1)
    owners = []
    ranks = []
    second = jnp.int32(0)
    message = jnp.zeros((DOMS, 128), I32)
    for p in range(PART):
        place = slot_ref[ori_ref[p]]
        owner = place // ORI
        rank = jnp.int32(0)
        for before in owners:
            rank = rank + jnp.where(before == owner, 1, 0)
        owners.append(owner)
        ranks.append(rank)
        second = jnp.where(rank == 1, p, second)
        fields = (cls_ref[p], off_ref[0, p] + 16, off_ref[1, p] + 16, place % ORI, jnp.int32(1), jnp.int32(p))
        at = lane16 - 8 * rank
        for f, value in enumerate(fields):
            message = jnp.where((owner_row == owner) & (at == f), value, message)
    for o in range(DOMS):
        meta_out[o // 4, o % 4] = message[o : o + 1]
    own_copy = pltpu.make_async_copy(meta_out, meta_own, own_sem.at[0])
    own_copy.start()

    pl.semaphore_wait(barrier, len(neighbours))

    map_copies = []
    for c in range(NCHUNK):
        source = map_hbm.at[pl.ds((1 - h) * (ORI // 2) + c * CHUNK, CHUNK)]
        copy = remote(
            source, other.at[pl.ds(c * CHUNK, CHUNK)], map_send.at[c], map_recv.at[c], {"half": 1 - h}
        )
        copy.start()
        map_copies.append(copy)
    copies = list(map_copies)

    def ring(k):
        for where in neighbours:
            signal(ring_sem.at[k], where)

    ring(0)

    own_copy.wait()
    ld_img.wait()

    def pack(o, carry):
        packed[o // 4, o % 4] = img[meta_own[o // 4, o % 4, 0, 5]]
        return carry

    lax.fori_loop(0, DOMS, pack, 0)
    for t in range(4):
        packed[t, 4] = img[second]
    pl.semaphore_wait(ring_sem.at[0], len(neighbours))
    ring(1)

    for r in FAR4:
        to = (y + r) % 4
        copy = remote(
            meta_out.at[to], meta_stage.at[:, y], meta1_send.at[r], meta1_recv.at[y], {"dom": to * 4 + q}
        )
        copy.start()
        copies.append(copy)
    for r in FAR4:
        to = (y + r) % 4
        copy = remote(packed.at[to], stage.at[:, y], img1_send.at[r], img1_recv.at[y], {"dom": to * 4 + q})
        copy.start()
        copies.append(copy)
    own_img = pltpu.make_async_copy(packed.at[y], stage.at[:, y], own_sem.at[1])
    own_img.start()
    own_meta = pltpu.make_async_copy(meta_out.at[y], meta_stage.at[:, y], own_sem.at[2])
    own_meta.start()

    ld_freq.wait()
    ld_defocus.wait()

    def one_class(k, carry):
        ctf[k] = ctf_rows(freq[...], defocus_ref[k])
        return carry

    lax.fori_loop(0, CLASSES, one_class, 0)
    pl.semaphore_wait(ring_sem.at[1], len(neighbours))
    ring(2)
    ld_ty.wait()
    for part_of in range(2):
        for s in range(33):
            eyb[s, part_of] = jnp.broadcast_to(ty[part_of, :, s : s + 1], (ROWS, 128))

    for r in FAR4:
        s = (y + r) % 4
        remote(meta_out.at[s], meta_stage.at[:, s], meta1_send.at[r], meta1_recv.at[s], {"dom": s * 4 + q}).wait_recv()
    own_meta.wait()
    for bits in (3, 2, 1):
        to = flip(bits)
        copy = remote(
            meta_stage.at[to], meta_in.at[q], meta2_send.at[bits], meta2_recv.at[q], {"dom": y * 4 + to}
        )
        copy.start()
        copies.append(copy)
    last_meta = pltpu.make_async_copy(meta_stage.at[q], meta_in.at[q], own_sem.at[3])
    last_meta.start()

    ld_map.wait()

    def own_power(i, total):
        m = maps[i].astype(F32)
        return total + m * m

    own_sq = lax.fori_loop(0, ORI, own_power, jnp.zeros((ROWS, BOX), F32))
    pl.semaphore_wait(ring_sem.at[2], len(neighbours))
    ring(3)
    ld_tri.wait()
    ld_ends.wait()

    def shell_sums(values):
        running = jnp.dot(jnp.concatenate(split3(values), axis=0), tri[...], preferred_element_type=F32)
        c = running[:ROWS] + (running[ROWS : 2 * ROWS] + running[2 * ROWS :])
        blocks = []
        for b in range(2):
            e = ends[:, 128 * b : 128 * b + 128]
            low = jnp.take_along_axis(c[:, :128], jnp.clip(e - 1, 0, 127), axis=1)
            high = jnp.take_along_axis(c[:, 128:], jnp.clip(e - 129, 0, 127), axis=1)
            got = jnp.where(e > 128, high, jnp.where(e > 0, low, 0.0))
            blocks.append(jnp.sum(got, axis=0, keepdims=True))
        first = blocks[0] - jnp.where(lane1 == 0, 0.0, pltpu.roll(blocks[0], 1, 1))
        carry_in = jnp.where(lane1 == 0, blocks[0][:, 127:128], pltpu.roll(blocks[1], 1, 1))
        return first, blocks[1] - carry_in

    power_sums = shell_sums(own_sq)
    cross = jnp.zeros((ROWS, BOX), F32)
    for c in range(NCHUNK):
        if c == NCHUNK - 1:
            for r in FAR4:
                s = (y + r) % 4
                remote(
                    packed.at[s], stage.at[:, s], img1_send.at[r], img1_recv.at[s], {"dom": s * 4 + q}
                ).wait_recv()
            own_img.wait()
            for kind, (src, dst, send, recv) in enumerate(
                ((stage.at[4], extra, ext_send, ext_recv), (stage.at[flip(1)], regular, img2_send, img2_recv))
            ):
                copy = remote(src, dst.at[q], send.at[1], recv.at[q], {"dom": y * 4 + flip(1)})
                copy.start()
                copies.append(copy)
            own_regular = pltpu.make_async_copy(stage.at[q], regular.at[q], own_sem.at[4])
            own_regular.start()
            own_extra = pltpu.make_async_copy(stage.at[4], extra.at[q], own_sem.at[5])
            own_extra.start()
        map_copies[c].wait_recv()

        def cross_term(i, total):
            mine = maps[h * (ORI // 2) + c * CHUNK + i].astype(F32)
            return total + mine * other[c * CHUNK + i].astype(F32)

        cross = lax.fori_loop(0, CHUNK, cross_term, cross)

    copy = remote(stage.at[4], extra.at[q], ext_send.at[2], ext_recv.at[q], {"dom": y * 4 + flip(2)})
    copy.start()
    copies.append(copy)

    def send_regular(bits):
        to = flip(bits)
        copy = remote(stage.at[to], regular.at[q], img2_send.at[bits], img2_recv.at[q], {"dom": y * 4 + to})
        copy.start()
        copies.append(copy)

    send_regular(2)

    pl.semaphore_wait(ring_sem.at[3], len(neighbours))

    sums = (shell_sums(cross), power_sums)
    shifted = (z == 3) | (z == 4)
    zero = jnp.zeros((1, 128), F32)
    for v in range(3):
        s0, s1 = sums[min(v, 1)]
        for b in range(3):
            block = jnp.where(shifted, (zero, s0, s1)[b], (s0, s1, zero)[b])
            if v > 0:
                block = jnp.where(h == v - 1, block, zero)
            arx[0, :, SHELLS * v + 128 * b : SHELLS * v + 128 * b + 128] = block

    spread(arx.at[0], along_z, ar1, ar1_send, ar1_recv)
    ar1[z * 2 + core] = arx[0]

    last_meta.wait()
    for bits in (1, 2, 3):
        s = flip(bits)
        remote(meta_stage.at[s], meta_in.at[s], meta2_send.at[bits], meta2_recv.at[s], {"dom": y * 4 + s}).wait_recv()
    to_smem = pltpu.make_async_copy(meta_in, meta_all, own_sem.at[6])
    to_smem.start()

    numbers = jnp.concatenate([meta_in[c, t] for c in range(4) for t in range(4)], axis=0).astype(F32)

    def field(f):
        return jnp.sum(jnp.where(lane16 == f, numbers, 0.0), axis=1, keepdims=True)

    key = jnp.concatenate(
        [jnp.where(field(8 * e + 4) > 0.5, field(8 * e + 3), -1.0) for e in range(2)], axis=0
    )
    item_lane = lax.broadcasted_iota(I32, (SLOTS, 128), 1)
    item_row = lax.broadcasted_iota(I32, (SLOTS, 128), 0)
    across = jnp.sum(jnp.where(item_lane == item_row, key, 0.0), axis=0, keepdims=True)
    where_f = item_lane.astype(F32)
    last = jnp.max(
        jnp.where((across == item_row.astype(F32)) & (item_lane < SLOTS), where_f, -1.0), axis=1, keepdims=True
    )
    same = (across == key) & (item_lane < item_row) & (key >= 0.0)
    previous = jnp.max(jnp.where(same, where_f, -1.0), axis=1, keepdims=True)
    link_v[...] = jnp.where(item_lane == 0, last, jnp.where(item_lane == 1, previous, 0.0)).astype(I32)
    link_copy = pltpu.make_async_copy(link_v, link, own_sem.at[7])
    link_copy.start()

    ld_tx.wait()
    own_regular.wait()
    own_extra.wait()
    to_smem.wait()
    low_half = lax.broadcasted_iota(I32, (ROWS, BOX), 1) < KX

    def items_of(source, column, e):
        def one_item(t, carry):
            at = 8 * e
            phase_x = tx[meta_all[column, t, 0, at + 1]]
            phase_y = eyb[meta_all[column, t, 0, at + 2]]
            cy = jnp.concatenate([phase_y[0]] * 3, axis=1)
            sy = jnp.concatenate([phase_y[1]] * 3, axis=1)
            cos_t = phase_x[0:1] * cy - phase_x[1:2] * sy
            sin_t = phase_x[3:4] * cy + phase_x[2:3] * sy
            x = source[column, t].astype(F32)
            c = ctf[meta_all[column, t, 0, at]] * meta_all[column, t, 0, at + 4].astype(F32)
            zz = c * (x * cos_t + flip_halves(x) * sin_t)
            contrib[16 * e + 4 * column + t] = zz.astype(BF16)
            m = maps[meta_all[column, t, 0, at + 3]].astype(F32)
            straight = zz * m
            crossed = zz * flip_halves(m)
            n = 2 * (4 * t + column) + e
            vprod[n] = jnp.where(low_half, straight, -crossed) + flip_halves(
                jnp.where(low_half, crossed, straight)
            )
            cm = c * m
            eprod[n] = cm * cm
            return carry

        lax.fori_loop(0, 4, one_item, 0)

    def wait_regular(bits):
        s = flip(bits)
        remote(
            stage.at[s], regular.at[s], img2_send.at[bits], img2_recv.at[s], {"dom": y * 4 + s}
        ).wait_recv()

    def wait_extra(bits):
        s = flip(bits)
        remote(stage.at[4], extra.at[s], ext_send.at[bits], ext_recv.at[s], {"dom": y * 4 + s}).wait_recv()

    items_of(regular, q, 0)
    items_of(extra, q, 1)
    wait_extra(1)
    items_of(extra, flip(1), 1)
    wait_regular(1)
    items_of(regular, flip(1), 0)
    total = gather(arx.at[0], along_z, ar1, ar1_send, ar1_recv)
    arx[1] = total
    spread(arx.at[1], in_plane, ar2, ar2_send, ar2_recv)
    send_regular(3)
    ar2[y * 4 + place_x] = total
    wait_extra(2)
    copy = remote(
        extra.at[flip(2)], extra.at[flip(2)], ext_send.at[3], ext_recv.at[flip(2)], {"dom": y * 4 + flip(1)}
    )
    copy.start()
    copies.append(copy)
    items_of(extra, flip(2), 1)
    wait_regular(2)
    items_of(regular, flip(2), 0)
    wait_extra(3)
    items_of(extra, flip(3), 1)
    total = gather(arx.at[1], in_plane, ar2, ar2_send, ar2_recv)

    power = total[:, SHELLS : 2 * SHELLS] * total[:, 2 * SHELLS : 3 * SHELLS]
    fsc = total[:, :SHELLS] / jnp.sqrt(power + 1e-06)
    corr_ref[...] = fsc[0, :NSHELL]
    floor = jnp.maximum(fsc, 0.1)
    table0 = jnp.where(shifted, floor[:, 128:256], floor[:, 0:128])
    table1 = jnp.where(shifted, floor[:, 256:384], floor[:, 128:256])
    table0 = jnp.broadcast_to(table0, (ROWS, 128))
    table1 = jnp.broadcast_to(table1, (ROWS, 128))
    ld_shell.wait()
    for b in range(3):
        at = shell_of[:, 128 * b : 128 * b + 128]
        low = jnp.take_along_axis(table0, jnp.minimum(at, 127), axis=1)
        high = jnp.take_along_axis(table1, jnp.maximum(at - 128, 0), axis=1)
        weight_ref[:, 128 * b : 128 * b + 128] = jnp.where(at < 128, low, high)
    w = weight_ref[...]

    guarded = []
    ld_col.wait()
    ld_rowt.wait()
    for half in range(2):
        from_x = (q // 2 + half) % 2
        if half == 1:
            wait_regular(3)
            items_of(regular, flip(3), 0)

        def weigh(j, carry):
            t = 2 * j + from_x
            energies = []
            for k in range(4):
                prod[4 * half + j, :, BOX * k : BOX * k + BOX] = (vprod[4 * t + k] * w).astype(BF16)
                e = jnp.sum(eprod[4 * t + k] * w, axis=0, keepdims=True)
                energies.append(e[:, 0:128] + e[:, 128:256] + e[:, 256:384])
            energies = jnp.concatenate(energies, axis=0)
            part[t, 32:48, :] = jnp.concatenate(list(split3(energies)) + [jnp.zeros((4, 128), BF16)], axis=0)
            return carry

        lax.fori_loop(0, 4, weigh, 0)
        section = jnp.dot(
            prod[4 * half : 4 * half + 4].reshape(4 * ROWS, 4 * BOX), col[...], preferred_element_type=F32
        ).astype(BF16)
        stacked = jnp.concatenate(
            [
                jnp.concatenate(
                    [section[ROWS * j : ROWS * j + ROWS, :128], section[ROWS * j : ROWS * j + ROWS, 128:]],
                    axis=0,
                )
                for j in range(4)
            ],
            axis=1,
        )
        partial = jnp.dot(rowt[...], stacked, preferred_element_type=F32).astype(BF16)
        for j in range(4):
            part[2 * j + from_x, 0:32, :] = partial[:, 128 * j : 128 * j + 128]
        for r in (2, 1, 3, 0):
            to = 2 * ((z // 2 + r) % 4) + from_x
            copy = remote(part.at[to], parts_in.at[z], part_send.at[to], part_recv.at[z], {"slab": to})
            if r == 0:
                pl.when(to != z)(copy.start)
                guarded.append((to != z, copy))
            else:
                copy.start()
                copies.append(copy)

    link_copy.wait()

    def add_item(u, carry):
        e = u // 16
        before = link[u, 1]
        has = jnp.where(before >= 0, 1.0, 0.0)
        from_u = jnp.minimum(jnp.maximum(before, 0), SLOTS - 1)
        column = (u % 16) // 4
        t = u % 4
        c = ctf[meta_all[column, t, 0, 8 * e]]
        valid = meta_all[column, t, 0, 8 * e + 4].astype(F32)
        vprod[u] = contrib[u].astype(F32) + has * vprod[from_u]
        eprod[u] = (c * c) * valid + has * eprod[from_u]
        return carry

    lax.fori_loop(0, SLOTS, add_item, 0)
    whole = part[z].astype(F32)
    for r in NEAR8:
        s = (z + r) % SLABS
        remote(part.at[s], parts_in.at[s], part_send.at[r], part_recv.at[s], {"slab": s}).wait_recv()
        whole = whole + parts_in[s].astype(F32)
    best = jnp.max(whole[0:32], axis=0, keepdims=True)
    lane4 = lax.broadcasted_iota(I32, (4, 128), 1)
    row4 = lax.broadcasted_iota(I32, (4, 128), 0)
    top = jnp.max(jnp.where(lane4 // 32 == row4, best, -jnp.inf), axis=1, keepdims=True)
    energy = jnp.sum(whole[32:36] + (whole[36:40] + whole[40:44]), axis=1, keepdims=True)
    value = top / jnp.sqrt(energy + 1e-06)
    answer = jnp.sum(jnp.where(lane4 == row4, value, 0.0), axis=0, keepdims=True)
    ret_out[...] = answer

    def score_copy(e, r):
        return remote(
            ret_out, ret.at[d], ret_send.at[8 * e + r], ret_recv.at[d],
            {"dom": 2 * z + e, "slab": (z + r) % SLABS},
        )

    for r in FAR8:
        for e in range(2):
            score_copy(e, r).start()
    for e in range(2):
        pl.when(2 * z + e != d)(score_copy(e, 0).start)

    @pl.when(d // 2 == z)
    def _():
        ret[d] = answer

    def one_slice(r, carry):
        at = link[r, 0]
        has = jnp.where(at >= 0, 1.0, 0.0)
        at = jnp.minimum(jnp.maximum(at, 0), SLOTS - 1)
        inverse = 1.0 / weight_ref[...]
        top = has * vprod[at] + maps[r].astype(F32) * inverse
        new_ref[r] = top / (has * eprod[at] + inverse)
        return carry

    lax.fori_loop(0, ORI, one_slice, 0)

    for copy in copies:
        copy.wait_send()
    for sent, copy in guarded:
        pl.when(sent)(copy.wait_send)
    for e in range(2):
        for r in FAR8:
            score_copy(e, r).wait_send()
        pl.when(2 * z + e != d)(score_copy(e, 0).wait_send)
    for r in range(DOMS):
        s = (d + r) % DOMS
        copy = remote(ret_out, ret.at[s], ret_send.at[r], ret_recv.at[s], {"dom": s, "slab": d // 2})
        if r == 0:
            pl.when(d // 2 != z)(copy.wait_recv)
        else:
            copy.wait_recv()
    picked = [jnp.where(lane1 == 2 * (d % 2) + ranks[p], ret[owners[p]], 0.0) for p in range(PART)]
    picked = jnp.sum(jnp.concatenate(picked, axis=0), axis=1, keepdims=True)
    lane8 = lax.broadcasted_iota(I32, (PART, 128), 1)
    row8 = lax.broadcasted_iota(I32, (PART, 128), 0)
    scores = jnp.sum(jnp.where(lane8 == row8, picked, 0.0), axis=0, keepdims=True)
    score_ref[...] = scores[:, :PART]


DELIVER = 8


def deliver_kernel(score_in, corr_in, new_in, score_out, corr_out, new_out, sem):
    step = ORI // DELIVER
    writes = []
    for t in range(DELIVER):
        block = pl.ds(step * t, step)
        writes.append(pltpu.make_async_copy(new_in.at[block], new_out.at[block], sem.at[t]))
    writes.append(pltpu.make_async_copy(score_in, score_out, sem.at[DELIVER]))
    writes.append(pltpu.make_async_copy(corr_in, corr_out, sem.at[DELIVER + 1]))
    for copy in writes:
        copy.start()
    for copy in writes:
        copy.wait()


def deliver(scores, fsc, new_maps):
    hbm = pl.BlockSpec(memory_space=pl.ANY)
    vmem = pl.BlockSpec(memory_space=pltpu.VMEM)
    return pl.pallas_call(
        deliver_kernel,
        out_shape=(
            jax.ShapeDtypeStruct((1, PART), F32),
            jax.ShapeDtypeStruct((NSHELL,), F32),
            jax.ShapeDtypeStruct((ORI, ROWS, BOX), F32),
        ),
        in_specs=[vmem, vmem, vmem],
        out_specs=(hbm, hbm, hbm),
        scratch_shapes=[
            pltpu.SemaphoreType.DMA((DELIVER + 2,)),
        ],
        compiler_params=pltpu.CompilerParams(vmem_limit_bytes=16 * 1024 * 1024),
        name="deliver",
    )(scores, fsc, new_maps)


def run_main(*operands):
    hbm = pl.BlockSpec(memory_space=pltpu.HBM)
    vmem = pl.BlockSpec(memory_space=pltpu.VMEM)
    v = pltpu.VMEM
    smem = pltpu.SMEM
    dma = pltpu.SemaphoreType.DMA
    return pl.pallas_call(
        main_kernel,
        out_shape=(
            pltpu.VMEM((1, PART), F32),
            pltpu.VMEM((NSHELL,), F32),
            pltpu.VMEM((ORI, ROWS, BOX), F32),
        ),
        in_specs=[hbm] * 15,
        out_specs=(vmem, vmem, vmem),
        scratch_shapes=[
            smem((PART,), I32), smem((2, PART), I32), smem((PART,), I32), smem((CLASSES,), F32),
            smem((512,), I32),
            v((PART, ROWS, BOX), BF16),
            v((ORI, ROWS, BOX), BF16),
            v((ORI // 2, ROWS, BOX), BF16),
            v((ROWS, BOX), I32),
            v((ROWS, 256), I32),
            v((ROWS, BOX), F32),
            v((33, 8, BOX), F32),
            v((2, ROWS, 128), F32),
            v((4 * BOX, 256), BF16),
            v((SHIFTS, 2 * ROWS), BF16),
            v((BOX, 256), BF16),
            v((ROWS, BOX), F32),
            v((4, 5, ROWS, BOX), BF16),
            v((5, 4, ROWS, BOX), BF16),
            v((4, 4, ROWS, BOX), BF16),
            v((4, 4, ROWS, BOX), BF16),
            v((SLOTS, ROWS, BOX), BF16),
            v((SLOTS, ROWS, BOX), F32),
            v((SLOTS, ROWS, BOX), F32),
            v((CLASSES, ROWS, BOX), F32),
            v((33, 2, ROWS, 128), F32),
            v((4, 4, 1, 128), I32),
            v((4, 4, 1, 128), I32),
            v((4, 4, 1, 128), I32),
            smem((4, 4, 1, 128), I32),
            smem((4, 4, 1, 128), I32),
            v((SLOTS, 128), I32),
            smem((SLOTS, 128), I32),
            v((16, 1, 3 * SHELLS), F32),
            v((16, 1, 3 * SHELLS), F32),
            v((2, 1, 3 * SHELLS), F32),
            v((SLABS, ROWS, 4 * BOX), BF16),
            v((SLABS, 48, 128), BF16),
            v((SLABS, 48, 128), BF16),
            v((DOMS, 1, 128), F32),
            v((1, 128), F32),
            dma((15,)),
            dma((8,)),
            pltpu.SemaphoreType.REGULAR((4,)),
            dma((NCHUNK,)), dma((NCHUNK,)),
            dma((4,)), dma((4,)),
            dma((4,)), dma((4,)),
            dma((4,)), dma((4,)),
            dma((4,)), dma((4,)),
            dma((4,)), dma((4,)),
            dma((16,)), dma((16,)),
            dma((16,)), dma((16,)),
            dma((8,)), dma((8,)),
            dma((16,)), dma((16,)),
        ],
        compiler_params=pltpu.CompilerParams(
            collective_id=0, has_side_effects=True, vmem_limit_bytes=44 * 1024 * 1024
        ),
        name="refine",
    )(*[pltpu.with_memory_space_constraint(x, pltpu.HBM) for x in operands])


def on_device(consts, images, orientation, offsets, defocus_class, defocus, ori_slot, half_maps):
    scores, fsc, new_maps = run_main(
        orientation[0], offsets[0].T, defocus_class[0], defocus, ori_slot, images[0], half_maps[0], *consts
    )
    scores, fsc, new_maps = deliver(scores, fsc, new_maps)
    return scores, new_maps[None], fsc


def solution(mesh):
    in_specs = (
        P("half", "dom", "slab", None),
        P("half", "dom"),
        P("half", "dom", None),
        P("half", "dom"),
        P(),
        P(),
        P("half", "dom", "slab", None),
    )
    out_specs = (P("half", "dom"), P("half", "dom", "slab", None), P())
    return jax.shard_map(
        functools.partial(on_device, tables()),
        mesh=mesh, in_specs=in_specs, out_specs=out_specs, check_vma=False,
    )
```

```python
import functools
import math

import jax
import jax.numpy as jnp
import ml_dtypes
import numpy as np
from jax import lax
from jax.experimental import pallas as pl
from jax.experimental.pallas import tpu as pltpu
from jax.sharding import PartitionSpec as P

BOX = 384
KX = 192
SHIFTS = 32
NSHELL = 267
ROWS = 48
SLABS = 8
DOMS = 16
PART = 8
ORI = 32
CLASSES = 16
SLOTS = 32
SHELLS = 384
CHUNK = 4
NCHUNK = 4
F32 = jnp.float32
BF16 = jnp.bfloat16
I32 = jnp.int32
MESH = pl.DeviceIdType.MESH
FAR8 = (4, 3, 5, 2, 6, 1, 7)
NEAR8 = FAR8[::-1]
FAR4 = (2, 1, 3)
NEAR4 = FAR4[::-1]


def tables():
    row = np.arange(BOX)
    ky = np.where(row < KX, row, row - BOX)
    kx = np.arange(KX)
    q = ky[:, None] ** 2 + kx[None, :] ** 2
    radius = np.floor(np.sqrt(q.astype(np.float64))).astype(np.int64)
    radius -= radius * radius > q
    radius += (radius + 1) * (radius + 1) <= q
    shell = np.clip(radius - 1, 0, NSHELL - 1)
    base = np.array([0, 0, 0, 128, 128, 0, 0, 0])
    local = shell.reshape(SLABS, ROWS, KX) - base[:, None, None]
    assert local.min() >= 0 and local.max() < 256
    shell_of = np.concatenate([local, local], axis=-1).astype(np.int32)
    ends = np.zeros((SLABS, ROWS, 256), np.int32)
    for s in range(256):
        ends[:, :, s] = (local <= s).sum(-1)
    freq = np.concatenate([q, q], axis=-1).reshape(SLABS, ROWS, BOX).astype(np.float32)
    freq = freq / np.float32(BOX * BOX)
    unit = np.float32(2.0 * math.pi / BOX)

    def trig(index):
        angle = (np.mod(index, BOX).astype(np.float32) * unit).astype(np.float32)
        return np.cos(angle).astype(np.float32), np.sin(angle).astype(np.float32)

    shift = np.arange(33) - 16
    cx, sx = trig(shift[:, None] * kx[None, :])
    tx = np.zeros((33, 8, BOX), np.float32)
    tx[:, 0] = np.concatenate([cx, cx], -1)
    tx[:, 1] = np.concatenate([sx, sx], -1)
    tx[:, 2] = np.concatenate([cx, -cx], -1)
    tx[:, 3] = np.concatenate([sx, -sx], -1)
    cy, sy = trig(ky[:, None] * shift[None, :])
    ty = np.zeros((SLABS, 2, ROWS, 128), np.float32)
    ty[:, 0, :, :33] = cy.reshape(SLABS, ROWS, 33)
    ty[:, 1, :, :33] = sy.reshape(SLABS, ROWS, 33)

    window = np.arange(SHIFTS) - SHIFTS // 2
    wcx, wsx = trig(kx[:, None] * window[None, :])
    wcy, wsy = trig(ky[:, None] * window[None, :])
    col_re = np.concatenate([wcx, -wsx], axis=0)
    col_im = np.concatenate([wsx, wcx], axis=0)
    col = np.zeros((4 * BOX, 256), np.float32)
    for k in range(4):
        col[k * BOX : (k + 1) * BOX, 32 * k : 32 * k + 32] = col_re
        col[k * BOX : (k + 1) * BOX, 128 + 32 * k : 160 + 32 * k] = col_im
    wcy = wcy.reshape(SLABS, ROWS, SHIFTS).transpose(0, 2, 1)
    wsy = wsy.reshape(SLABS, ROWS, SHIFTS).transpose(0, 2, 1)
    rowt = np.concatenate([wcy, -wsy], axis=-1)
    tri = (np.arange(BOX)[:, None] % KX <= np.arange(256)[None, :]).astype(np.float32)
    bf = ml_dtypes.bfloat16
    return (
        shell_of, ends, freq, tx, ty, col.astype(bf), rowt.astype(bf), tri.astype(bf),
    )


def flip_halves(x):
    return pltpu.roll(x, KX, 1)


def ctf_rows(freq, defocus):
    g = defocus * freq
    phi = math.atan2(0.1, 0.995)
    m = jnp.floor((g + phi) * (1.0 / math.pi) + 0.5)
    t = ((g - m * 3.140625) - m * 9.67653589793e-4) + phi
    odd = m - 2.0 * jnp.floor(m * 0.5)
    t2 = t * t
    p = -1.0 / 39916800.0
    for c in (1.0 / 362880.0, -1.0 / 5040.0, 1.0 / 120.0, -1.0 / 6.0, 1.0):
        p = p * t2 + c
    scale = math.sqrt(0.995 * 0.995 + 0.01)
    return (p * t) * ((2.0 * odd - 1.0) * scale)


def split3(x):
    hi = x.astype(BF16)
    rest = x - hi.astype(F32)
    mid = rest.astype(BF16)
    low = (rest - mid.astype(F32)).astype(BF16)
    return hi, mid, low


def main_kernel(
    ori_hbm, off_hbm, cls_hbm, defocus_hbm, slot_hbm, img_hbm, map_hbm,
    shell_hbm, ends_hbm, freq_hbm, tx_hbm, ty_hbm, col_hbm, rowt_hbm, tri_hbm,
    score_ref, corr_ref, new_ref,
    ori_ref, off_ref, cls_ref, defocus_ref, slot_ref,
    img, maps, other, shell_of, ends, freq, tx, ty, col, rowt, tri, weight_ref,
    packed, stage, regular, extra, contrib, vprod, eprod, ctf, eyb,
    meta_out, meta_stage, meta_in, meta_own, meta_all, link_v, link,
    ar1, ar2, ar3, arx, prod, part, parts_in, ret, ret_out,
    load_sem, own_sem, ring_sem, map_send, map_recv,
    img1_send, img1_recv, img2_send, img2_recv, ext_send, ext_recv,
    meta1_send, meta1_recv, meta2_send, meta2_recv,
    ar1_send, ar1_recv, ar2_send, ar2_recv, ar3_send, ar3_recv,
    part_send, part_recv, ret_send, ret_recv,
):
    h = lax.axis_index("half")
    d = lax.axis_index("dom")
    z = lax.axis_index("slab")
    y = d // 4
    q = d % 4
    g = h * 4 + q

    def flip(bits):
        hi = (q // 2 + bits // 2) % 2
        lo = (q % 2 + bits % 2) % 2
        return hi * 2 + lo

    def remote(src, dst, send, recv, where):
        return pltpu.make_async_remote_copy(
            src_ref=src, dst_ref=dst, send_sem=send, recv_sem=recv,
            device_id=where, device_id_type=MESH,
        )

    def signal(sem, where):
        pl.semaphore_signal(sem, inc=1, device_id=where, device_id_type=MESH)

    neighbours = (
        {"half": 1 - h}, {"half": 1 - h, "dom": y * 4 + flip(2)}, {"dom": y * 4 + flip(1)},
        {"dom": (y + 1) % 4 * 4 + q}, {"dom": (y + 3) % 4 * 4 + q},
        {"slab": (z + 1) % SLABS}, {"slab": (z + 7) % SLABS},
    )
    barrier = pltpu.get_barrier_semaphore()
    for where in neighbours:
        signal(barrier, where)

    loads = [
        (ori_hbm, ori_ref), (off_hbm, off_ref), (cls_hbm, cls_ref), (slot_hbm, slot_ref),
        (defocus_hbm, defocus_ref), (img_hbm, img), (freq_hbm.at[z], freq), (ty_hbm.at[z], ty),
        (map_hbm, maps), (tri_hbm, tri), (ends_hbm.at[z], ends), (tx_hbm, tx),
        (shell_hbm.at[z], shell_of), (col_hbm, col), (rowt_hbm.at[z], rowt),
    ]
    loads = [pltpu.make_async_copy(a, b, load_sem.at[i]) for i, (a, b) in enumerate(loads)]
    for c in loads:
        c.start()
    ld_small = loads[:4]
    (ld_defocus, ld_img, ld_freq, ld_ty, ld_map, ld_tri, ld_ends, ld_tx, ld_shell, ld_col, ld_rowt) = loads[4:]

    for c in ld_small:
        c.wait()
    lane1 = lax.broadcasted_iota(I32, (1, 128), 1)
    owner_row = lax.broadcasted_iota(I32, (DOMS, 128), 0)
    lane16 = lax.broadcasted_iota(I32, (DOMS, 128), 1)
    owners = []
    ranks = []
    second = jnp.int32(0)
    message = jnp.zeros((DOMS, 128), I32)
    for p in range(PART):
        place = slot_ref[ori_ref[p]]
        owner = place // ORI
        rank = jnp.int32(0)
        for before in owners:
            rank = rank + jnp.where(before == owner, 1, 0)
        owners.append(owner)
        ranks.append(rank)
        second = jnp.where(rank == 1, p, second)
        fields = (cls_ref[p], off_ref[0, p] + 16, off_ref[1, p] + 16, place % ORI, jnp.int32(1), jnp.int32(p))
        at = lane16 - 8 * rank
        for f, value in enumerate(fields):
            message = jnp.where((owner_row == owner) & (at == f), value, message)
    for o in range(DOMS):
        meta_out[o // 4, o % 4] = message[o : o + 1]
    own_copy = pltpu.make_async_copy(meta_out, meta_own, own_sem.at[0])
    own_copy.start()

    pl.semaphore_wait(barrier, len(neighbours))

    map_copies = []
    for c in range(NCHUNK):
        source = map_hbm.at[pl.ds((1 - h) * (ORI // 2) + c * CHUNK, CHUNK)]
        copy = remote(
            source, other.at[pl.ds(c * CHUNK, CHUNK)], map_send.at[c], map_recv.at[c], {"half": 1 - h}
        )
        copy.start()
        map_copies.append(copy)
    copies = list(map_copies)

    def ring(k):
        for where in neighbours:
            signal(ring_sem.at[k], where)

    ring(0)

    own_copy.wait()
    ld_img.wait()

    def pack(o, carry):
        packed[o // 4, o % 4] = img[meta_own[o // 4, o % 4, 0, 5]]
        return carry

    lax.fori_loop(0, DOMS, pack, 0)
    for t in range(4):
        packed[t, 4] = img[second]
    pl.semaphore_wait(ring_sem.at[0], len(neighbours))
    ring(1)

    for r in FAR4:
        to = (y + r) % 4
        copy = remote(
            meta_out.at[to], meta_stage.at[:, y], meta1_send.at[r], meta1_recv.at[y], {"dom": to * 4 + q}
        )
        copy.start()
        copies.append(copy)
    for r in FAR4:
        to = (y + r) % 4
        copy = remote(packed.at[to], stage.at[:, y], img1_send.at[r], img1_recv.at[y], {"dom": to * 4 + q})
        copy.start()
        copies.append(copy)
    own_img = pltpu.make_async_copy(packed.at[y], stage.at[:, y], own_sem.at[1])
    own_img.start()
    own_meta = pltpu.make_async_copy(meta_out.at[y], meta_stage.at[:, y], own_sem.at[2])
    own_meta.start()

    ld_freq.wait()
    ld_defocus.wait()

    def one_class(k, carry):
        ctf[k] = ctf_rows(freq[...], defocus_ref[k])
        return carry

    lax.fori_loop(0, CLASSES, one_class, 0)
    pl.semaphore_wait(ring_sem.at[1], len(neighbours))
    ring(2)
    ld_ty.wait()
    for part_of in range(2):
        for s in range(33):
            eyb[s, part_of] = jnp.broadcast_to(ty[part_of, :, s : s + 1], (ROWS, 128))

    for r in FAR4:
        s = (y + r) % 4
        remote(meta_out.at[s], meta_stage.at[:, s], meta1_send.at[r], meta1_recv.at[s], {"dom": s * 4 + q}).wait_recv()
    own_meta.wait()
    for bits in (3, 2, 1):
        to = flip(bits)
        copy = remote(
            meta_stage.at[to], meta_in.at[q], meta2_send.at[bits], meta2_recv.at[q], {"dom": y * 4 + to}
        )
        copy.start()
        copies.append(copy)
    last_meta = pltpu.make_async_copy(meta_stage.at[q], meta_in.at[q], own_sem.at[3])
    last_meta.start()

    ld_map.wait()

    def own_power(i, total):
        m = maps[i].astype(F32)
        return total + m * m

    own_sq = lax.fori_loop(0, ORI, own_power, jnp.zeros((ROWS, BOX), F32))
    pl.semaphore_wait(ring_sem.at[2], len(neighbours))
    ld_tri.wait()
    ld_ends.wait()

    def shell_sums(values):
        running = jnp.dot(jnp.concatenate(split3(values), axis=0), tri[...], preferred_element_type=F32)
        c = running[:ROWS] + (running[ROWS : 2 * ROWS] + running[2 * ROWS :])
        blocks = []
        for b in range(2):
            e = ends[:, 128 * b : 128 * b + 128]
            low = jnp.take_along_axis(c[:, :128], jnp.clip(e - 1, 0, 127), axis=1)
            high = jnp.take_along_axis(c[:, 128:], jnp.clip(e - 129, 0, 127), axis=1)
            got = jnp.where(e > 128, high, jnp.where(e > 0, low, 0.0))
            blocks.append(jnp.sum(got, axis=0, keepdims=True))
        first = blocks[0] - jnp.where(lane1 == 0, 0.0, pltpu.roll(blocks[0], 1, 1))
        carry_in = jnp.where(lane1 == 0, blocks[0][:, 127:128], pltpu.roll(blocks[1], 1, 1))
        return first, blocks[1] - carry_in

    power_sums = shell_sums(own_sq)
    cross = jnp.zeros((ROWS, BOX), F32)
    for c in range(NCHUNK):
        if c == NCHUNK - 1:
            for r in FAR4:
                s = (y + r) % 4
                remote(
                    packed.at[s], stage.at[:, s], img1_send.at[r], img1_recv.at[s], {"dom": s * 4 + q}
                ).wait_recv()
            own_img.wait()
            for kind, (src, dst, send, recv) in enumerate(
                ((stage.at[4], extra, ext_send, ext_recv), (stage.at[flip(1)], regular, img2_send, img2_recv))
            ):
                copy = remote(src, dst.at[q], send.at[1], recv.at[q], {"dom": y * 4 + flip(1)})
                copy.start()
                copies.append(copy)
            own_regular = pltpu.make_async_copy(stage.at[q], regular.at[q], own_sem.at[4])
            own_regular.start()
            own_extra = pltpu.make_async_copy(stage.at[4], extra.at[q], own_sem.at[5])
            own_extra.start()
        map_copies[c].wait_recv()

        def cross_term(i, total):
            mine = maps[h * (ORI // 2) + c * CHUNK + i].astype(F32)
            return total + mine * other[c * CHUNK + i].astype(F32)

        cross = lax.fori_loop(0, CHUNK, cross_term, cross)

    copy = remote(stage.at[4], extra.at[q], ext_send.at[2], ext_recv.at[q], {"dom": y * 4 + flip(2)})
    copy.start()
    copies.append(copy)

    def send_regular(bits):
        to = flip(bits)
        copy = remote(stage.at[to], regular.at[q], img2_send.at[bits], img2_recv.at[q], {"dom": y * 4 + to})
        copy.start()
        copies.append(copy)

    send_regular(2)

    sums = (shell_sums(cross), power_sums)
    shifted = (z == 3) | (z == 4)
    zero = jnp.zeros((1, 128), F32)
    for v in range(3):
        s0, s1 = sums[min(v, 1)]
        for b in range(3):
            block = jnp.where(shifted, (zero, s0, s1)[b], (s0, s1, zero)[b])
            if v > 0:
                block = jnp.where(h == v - 1, block, zero)
            arx[0, :, SHELLS * v + 128 * b : SHELLS * v + 128 * b + 128] = block

    for r in FAR8:
        to = (z + r) % SLABS
        copy = remote(arx.at[0], ar1.at[z], ar1_send.at[r], ar1_recv.at[z], {"slab": to})
        copy.start()
        copies.append(copy)

    last_meta.wait()
    for bits in (1, 2, 3):
        s = flip(bits)
        remote(meta_stage.at[s], meta_in.at[s], meta2_send.at[bits], meta2_recv.at[s], {"dom": y * 4 + s}).wait_recv()
    to_smem = pltpu.make_async_copy(meta_in, meta_all, own_sem.at[6])
    to_smem.start()

    numbers = jnp.concatenate([meta_in[c, t] for c in range(4) for t in range(4)], axis=0).astype(F32)

    def field(f):
        return jnp.sum(jnp.where(lane16 == f, numbers, 0.0), axis=1, keepdims=True)

    key = jnp.concatenate(
        [jnp.where(field(8 * e + 4) > 0.5, field(8 * e + 3), -1.0) for e in range(2)], axis=0
    )
    item_lane = lax.broadcasted_iota(I32, (SLOTS, 128), 1)
    item_row = lax.broadcasted_iota(I32, (SLOTS, 128), 0)
    across = jnp.sum(jnp.where(item_lane == item_row, key, 0.0), axis=0, keepdims=True)
    where_f = item_lane.astype(F32)
    last = jnp.max(
        jnp.where((across == item_row.astype(F32)) & (item_lane < SLOTS), where_f, -1.0), axis=1, keepdims=True
    )
    same = (across == key) & (item_lane < item_row) & (key >= 0.0)
    previous = jnp.max(jnp.where(same, where_f, -1.0), axis=1, keepdims=True)
    link_v[...] = jnp.where(item_lane == 0, last, jnp.where(item_lane == 1, previous, 0.0)).astype(I32)
    link_copy = pltpu.make_async_copy(link_v, link, own_sem.at[7])
    link_copy.start()

    ld_tx.wait()
    own_regular.wait()
    own_extra.wait()
    to_smem.wait()
    low_half = lax.broadcasted_iota(I32, (ROWS, BOX), 1) < KX

    def items_of(source, column, e):
        def one_item(t, carry):
            at = 8 * e
            phase_x = tx[meta_all[column, t, 0, at + 1]]
            phase_y = eyb[meta_all[column, t, 0, at + 2]]
            cy = jnp.concatenate([phase_y[0]] * 3, axis=1)
            sy = jnp.concatenate([phase_y[1]] * 3, axis=1)
            cos_t = phase_x[0:1] * cy - phase_x[1:2] * sy
            sin_t = phase_x[3:4] * cy + phase_x[2:3] * sy
            x = source[column, t].astype(F32)
            c = ctf[meta_all[column, t, 0, at]] * meta_all[column, t, 0, at + 4].astype(F32)
            zz = c * (x * cos_t + flip_halves(x) * sin_t)
            contrib[16 * e + 4 * column + t] = zz.astype(BF16)
            m = maps[meta_all[column, t, 0, at + 3]].astype(F32)
            straight = zz * m
            crossed = zz * flip_halves(m)
            n = 2 * (4 * t + column) + e
            vprod[n] = jnp.where(low_half, straight, -crossed) + flip_halves(
                jnp.where(low_half, crossed, straight)
            )
            cm = c * m
            eprod[n] = cm * cm
            return carry

        lax.fori_loop(0, 4, one_item, 0)

    def wait_regular(bits):
        s = flip(bits)
        remote(
            stage.at[s], regular.at[s], img2_send.at[bits], img2_recv.at[s], {"dom": y * 4 + s}
        ).wait_recv()

    def wait_extra(bits):
        s = flip(bits)
        remote(stage.at[4], extra.at[s], ext_send.at[bits], ext_recv.at[s], {"dom": y * 4 + s}).wait_recv()

    items_of(regular, q, 0)
    items_of(extra, q, 1)
    wait_extra(1)
    items_of(extra, flip(1), 1)
    ar1[z] = arx[0]
    for r in NEAR8:
        s = (z + r) % SLABS
        remote(arx.at[0], ar1.at[s], ar1_send.at[r], ar1_recv.at[s], {"slab": s}).wait_recv()
    total = ar1[0]
    for s in range(1, SLABS):
        total = total + ar1[s]
    arx[1] = total
    for r in FAR4:
        to = (y + r) % 4
        copy = remote(arx.at[1], ar2.at[y], ar2_send.at[r], ar2_recv.at[y], {"dom": to * 4 + q})
        copy.start()
        copies.append(copy)
    wait_regular(1)
    items_of(regular, flip(1), 0)
    wait_extra(2)
    copy = remote(
        extra.at[flip(2)], extra.at[flip(2)], ext_send.at[3], ext_recv.at[flip(2)], {"dom": y * 4 + flip(1)}
    )
    copy.start()
    copies.append(copy)
    ar2[y] = total
    for r in NEAR4:
        s = (y + r) % 4
        remote(arx.at[1], ar2.at[s], ar2_send.at[r], ar2_recv.at[s], {"dom": s * 4 + q}).wait_recv()
    total = ar2[0]
    for s in range(1, 4):
        total = total + ar2[s]
    arx[2] = total
    for r in FAR8:
        to = (g + r) % 8
        copy = remote(
            arx.at[2], ar3.at[g], ar3_send.at[r], ar3_recv.at[g], {"half": to // 4, "dom": y * 4 + to % 4}
        )
        copy.start()
        copies.append(copy)
    send_regular(3)
    items_of(extra, flip(2), 1)
    wait_regular(2)
    items_of(regular, flip(2), 0)
    wait_extra(3)
    items_of(extra, flip(3), 1)
    ar3[g] = total
    for r in NEAR8:
        s = (g + r) % 8
        remote(
            arx.at[2], ar3.at[s], ar3_send.at[r], ar3_recv.at[s], {"half": s // 4, "dom": y * 4 + s % 4}
        ).wait_recv()
    total = ar3[0]
    for s in range(1, 8):
        total = total + ar3[s]

    power = total[:, SHELLS : 2 * SHELLS] * total[:, 2 * SHELLS : 3 * SHELLS]
    fsc = total[:, :SHELLS] / jnp.sqrt(power + 1e-06)
    corr_ref[...] = fsc[0, :NSHELL]
    floor = jnp.maximum(fsc, 0.1)
    table0 = jnp.where(shifted, floor[:, 128:256], floor[:, 0:128])
    table1 = jnp.where(shifted, floor[:, 256:384], floor[:, 128:256])
    table0 = jnp.broadcast_to(table0, (ROWS, 128))
    table1 = jnp.broadcast_to(table1, (ROWS, 128))
    ld_shell.wait()
    for b in range(3):
        at = shell_of[:, 128 * b : 128 * b + 128]
        low = jnp.take_along_axis(table0, jnp.minimum(at, 127), axis=1)
        high = jnp.take_along_axis(table1, jnp.maximum(at - 128, 0), axis=1)
        weight_ref[:, 128 * b : 128 * b + 128] = jnp.where(at < 128, low, high)
    w = weight_ref[...]

    guarded = []
    ld_col.wait()
    ld_rowt.wait()
    for half in range(2):
        from_x = (q // 2 + half) % 2
        if half == 1:
            wait_regular(3)
            items_of(regular, flip(3), 0)

        def weigh(j, carry):
            t = 2 * j + from_x
            energies = []
            for k in range(4):
                prod[4 * half + j, :, BOX * k : BOX * k + BOX] = (vprod[4 * t + k] * w).astype(BF16)
                e = jnp.sum(eprod[4 * t + k] * w, axis=0, keepdims=True)
                energies.append(e[:, 0:128] + e[:, 128:256] + e[:, 256:384])
            energies = jnp.concatenate(energies, axis=0)
            part[t, 32:48, :] = jnp.concatenate(list(split3(energies)) + [jnp.zeros((4, 128), BF16)], axis=0)
            return carry

        lax.fori_loop(0, 4, weigh, 0)
        section = jnp.dot(
            prod[4 * half : 4 * half + 4].reshape(4 * ROWS, 4 * BOX), col[...], preferred_element_type=F32
        ).astype(BF16)
        stacked = jnp.concatenate(
            [
                jnp.concatenate(
                    [section[ROWS * j : ROWS * j + ROWS, :128], section[ROWS * j : ROWS * j + ROWS, 128:]],
                    axis=0,
                )
                for j in range(4)
            ],
            axis=1,
        )
        partial = jnp.dot(rowt[...], stacked, preferred_element_type=F32).astype(BF16)
        for j in range(4):
            part[2 * j + from_x, 0:32, :] = partial[:, 128 * j : 128 * j + 128]
        for r in (2, 1, 3, 0):
            to = 2 * ((z // 2 + r) % 4) + from_x
            copy = remote(part.at[to], parts_in.at[z], part_send.at[to], part_recv.at[z], {"slab": to})
            if r == 0:
                pl.when(to != z)(copy.start)
                guarded.append((to != z, copy))
            else:
                copy.start()
                copies.append(copy)

    link_copy.wait()

    def add_item(u, carry):
        e = u // 16
        before = link[u, 1]
        has = jnp.where(before >= 0, 1.0, 0.0)
        from_u = jnp.minimum(jnp.maximum(before, 0), SLOTS - 1)
        column = (u % 16) // 4
        t = u % 4
        c = ctf[meta_all[column, t, 0, 8 * e]]
        valid = meta_all[column, t, 0, 8 * e + 4].astype(F32)
        vprod[u] = contrib[u].astype(F32) + has * vprod[from_u]
        eprod[u] = (c * c) * valid + has * eprod[from_u]
        return carry

    lax.fori_loop(0, SLOTS, add_item, 0)
    whole = part[z].astype(F32)
    for r in NEAR8:
        s = (z + r) % SLABS
        remote(part.at[s], parts_in.at[s], part_send.at[r], part_recv.at[s], {"slab": s}).wait_recv()
        whole = whole + parts_in[s].astype(F32)
    best = jnp.max(whole[0:32], axis=0, keepdims=True)
    lane4 = lax.broadcasted_iota(I32, (4, 128), 1)
    row4 = lax.broadcasted_iota(I32, (4, 128), 0)
    top = jnp.max(jnp.where(lane4 // 32 == row4, best, -jnp.inf), axis=1, keepdims=True)
    energy = jnp.sum(whole[32:36] + (whole[36:40] + whole[40:44]), axis=1, keepdims=True)
    value = top / jnp.sqrt(energy + 1e-06)
    answer = jnp.sum(jnp.where(lane4 == row4, value, 0.0), axis=0, keepdims=True)
    ret_out[...] = answer

    def score_copy(e, r):
        return remote(
            ret_out, ret.at[d], ret_send.at[8 * e + r], ret_recv.at[d],
            {"dom": 2 * z + e, "slab": (z + r) % SLABS},
        )

    for r in FAR8:
        for e in range(2):
            score_copy(e, r).start()
    for e in range(2):
        pl.when(2 * z + e != d)(score_copy(e, 0).start)

    @pl.when(d // 2 == z)
    def _():
        ret[d] = answer

    def one_slice(r, carry):
        at = link[r, 0]
        has = jnp.where(at >= 0, 1.0, 0.0)
        at = jnp.minimum(jnp.maximum(at, 0), SLOTS - 1)
        inverse = 1.0 / weight_ref[...]
        top = has * vprod[at] + maps[r].astype(F32) * inverse
        new_ref[r] = top / (has * eprod[at] + inverse)
        return carry

    lax.fori_loop(0, ORI, one_slice, 0)

    for copy in copies:
        copy.wait_send()
    for sent, copy in guarded:
        pl.when(sent)(copy.wait_send)
    for e in range(2):
        for r in FAR8:
            score_copy(e, r).wait_send()
        pl.when(2 * z + e != d)(score_copy(e, 0).wait_send)
    for r in range(DOMS):
        s = (d + r) % DOMS
        copy = remote(ret_out, ret.at[s], ret_send.at[r], ret_recv.at[s], {"dom": s, "slab": d // 2})
        if r == 0:
            pl.when(d // 2 != z)(copy.wait_recv)
        else:
            copy.wait_recv()
    picked = [jnp.where(lane1 == 2 * (d % 2) + ranks[p], ret[owners[p]], 0.0) for p in range(PART)]
    picked = jnp.sum(jnp.concatenate(picked, axis=0), axis=1, keepdims=True)
    lane8 = lax.broadcasted_iota(I32, (PART, 128), 1)
    row8 = lax.broadcasted_iota(I32, (PART, 128), 0)
    scores = jnp.sum(jnp.where(lane8 == row8, picked, 0.0), axis=0, keepdims=True)
    score_ref[...] = scores[:, :PART]


DELIVER = 8


def deliver_kernel(score_in, corr_in, new_in, score_out, corr_out, new_out, sem):
    step = ORI // DELIVER
    writes = []
    for t in range(DELIVER):
        block = pl.ds(step * t, step)
        writes.append(pltpu.make_async_copy(new_in.at[block], new_out.at[block], sem.at[t]))
    writes.append(pltpu.make_async_copy(score_in, score_out, sem.at[DELIVER]))
    writes.append(pltpu.make_async_copy(corr_in, corr_out, sem.at[DELIVER + 1]))
    for copy in writes:
        copy.start()
    for copy in writes:
        copy.wait()


def deliver(scores, fsc, new_maps):
    hbm = pl.BlockSpec(memory_space=pl.ANY)
    vmem = pl.BlockSpec(memory_space=pltpu.VMEM)
    return pl.pallas_call(
        deliver_kernel,
        out_shape=(
            jax.ShapeDtypeStruct((1, PART), F32),
            jax.ShapeDtypeStruct((NSHELL,), F32),
            jax.ShapeDtypeStruct((ORI, ROWS, BOX), F32),
        ),
        in_specs=[vmem, vmem, vmem],
        out_specs=(hbm, hbm, hbm),
        scratch_shapes=[
            pltpu.SemaphoreType.DMA((DELIVER + 2,)),
        ],
        compiler_params=pltpu.CompilerParams(vmem_limit_bytes=16 * 1024 * 1024),
        name="deliver",
    )(scores, fsc, new_maps)


def run_main(*operands):
    hbm = pl.BlockSpec(memory_space=pltpu.HBM)
    vmem = pl.BlockSpec(memory_space=pltpu.VMEM)
    v = pltpu.VMEM
    smem = pltpu.SMEM
    dma = pltpu.SemaphoreType.DMA
    return pl.pallas_call(
        main_kernel,
        out_shape=(
            pltpu.VMEM((1, PART), F32),
            pltpu.VMEM((NSHELL,), F32),
            pltpu.VMEM((ORI, ROWS, BOX), F32),
        ),
        in_specs=[hbm] * 15,
        out_specs=(vmem, vmem, vmem),
        scratch_shapes=[
            smem((PART,), I32), smem((2, PART), I32), smem((PART,), I32), smem((CLASSES,), F32),
            smem((512,), I32),
            v((PART, ROWS, BOX), BF16),
            v((ORI, ROWS, BOX), BF16),
            v((ORI // 2, ROWS, BOX), BF16),
            v((ROWS, BOX), I32),
            v((ROWS, 256), I32),
            v((ROWS, BOX), F32),
            v((33, 8, BOX), F32),
            v((2, ROWS, 128), F32),
            v((4 * BOX, 256), BF16),
            v((SHIFTS, 2 * ROWS), BF16),
            v((BOX, 256), BF16),
            v((ROWS, BOX), F32),
            v((4, 5, ROWS, BOX), BF16),
            v((5, 4, ROWS, BOX), BF16),
            v((4, 4, ROWS, BOX), BF16),
            v((4, 4, ROWS, BOX), BF16),
            v((SLOTS, ROWS, BOX), BF16),
            v((SLOTS, ROWS, BOX), F32),
            v((SLOTS, ROWS, BOX), F32),
            v((CLASSES, ROWS, BOX), F32),
            v((33, 2, ROWS, 128), F32),
            v((4, 4, 1, 128), I32),
            v((4, 4, 1, 128), I32),
            v((4, 4, 1, 128), I32),
            smem((4, 4, 1, 128), I32),
            smem((4, 4, 1, 128), I32),
            v((SLOTS, 128), I32),
            smem((SLOTS, 128), I32),
            v((8, 1, 3 * SHELLS), F32),
            v((4, 1, 3 * SHELLS), F32),
            v((8, 1, 3 * SHELLS), F32),
            v((3, 1, 3 * SHELLS), F32),
            v((SLABS, ROWS, 4 * BOX), BF16),
            v((SLABS, 48, 128), BF16),
            v((SLABS, 48, 128), BF16),
            v((DOMS, 1, 128), F32),
            v((1, 128), F32),
            dma((15,)),
            dma((8,)),
            pltpu.SemaphoreType.REGULAR((3,)),
            dma((NCHUNK,)), dma((NCHUNK,)),
            dma((4,)), dma((4,)),
            dma((4,)), dma((4,)),
            dma((4,)), dma((4,)),
            dma((4,)), dma((4,)),
            dma((4,)), dma((4,)),
            dma((8,)), dma((8,)),
            dma((4,)), dma((4,)),
            dma((8,)), dma((8,)),
            dma((8,)), dma((8,)),
            dma((16,)), dma((16,)),
        ],
        compiler_params=pltpu.CompilerParams(
            collective_id=0, has_side_effects=True, vmem_limit_bytes=44 * 1024 * 1024
        ),
        name="refine",
    )(*[pltpu.with_memory_space_constraint(x, pltpu.HBM) for x in operands])


def on_device(consts, images, orientation, offsets, defocus_class, defocus, ori_slot, half_maps):
    scores, fsc, new_maps = run_main(
        orientation[0], offsets[0].T, defocus_class[0], defocus, ori_slot, images[0], half_maps[0], *consts
    )
    scores, fsc, new_maps = deliver(scores, fsc, new_maps)
    return scores, new_maps[None], fsc


def solution(mesh):
    in_specs = (
        P("half", "dom", "slab", None),
        P("half", "dom"),
        P("half", "dom", None),
        P("half", "dom"),
        P(),
        P(),
        P("half", "dom", "slab", None),
    )
    out_specs = (P("half", "dom"), P("half", "dom", "slab", None), P())
    return jax.shard_map(
        functools.partial(on_device, tables()),
        mesh=mesh, in_specs=in_specs, out_specs=out_specs, check_vma=False,
    )
```

```python
import functools
import math

import jax
import jax.numpy as jnp
import ml_dtypes
import numpy as np
from jax import lax
from jax.experimental import pallas as pl
from jax.experimental.pallas import tpu as pltpu
from jax.sharding import PartitionSpec as P

BOX = 384
KX = 192
SHIFTS = 32
NSHELL = 267
ROWS = 48
SLABS = 8
DOMS = 16
PART = 8
ORI = 32
CLASSES = 16
SLOTS = 32
SHELLS = 384
CHUNK = 4
NCHUNK = 4
F32 = jnp.float32
BF16 = jnp.bfloat16
I32 = jnp.int32
MESH = pl.DeviceIdType.MESH
FAR8 = (4, 3, 5, 2, 6, 1, 7)
NEAR8 = FAR8[::-1]
FAR4 = (2, 1, 3)
NEAR4 = FAR4[::-1]


def tables():
    row = np.arange(BOX)
    ky = np.where(row < KX, row, row - BOX)
    kx = np.arange(KX)
    q = ky[:, None] ** 2 + kx[None, :] ** 2
    radius = np.floor(np.sqrt(q.astype(np.float64))).astype(np.int64)
    radius -= radius * radius > q
    radius += (radius + 1) * (radius + 1) <= q
    shell = np.clip(radius - 1, 0, NSHELL - 1)
    base = np.array([0, 0, 0, 128, 128, 0, 0, 0])
    local = shell.reshape(SLABS, ROWS, KX) - base[:, None, None]
    assert local.min() >= 0 and local.max() < 256
    shell_of = np.concatenate([local, local], axis=-1).astype(np.int32)
    ends = np.zeros((SLABS, ROWS, 256), np.int32)
    for s in range(256):
        ends[:, :, s] = (local <= s).sum(-1)
    freq = np.concatenate([q, q], axis=-1).reshape(SLABS, ROWS, BOX).astype(np.float32)
    freq = freq / np.float32(BOX * BOX)
    unit = np.float32(2.0 * math.pi / BOX)

    def trig(index):
        angle = (np.mod(index, BOX).astype(np.float32) * unit).astype(np.float32)
        return np.cos(angle).astype(np.float32), np.sin(angle).astype(np.float32)

    shift = np.arange(33) - 16
    cx, sx = trig(shift[:, None] * kx[None, :])
    tx = np.zeros((33, 8, BOX), np.float32)
    tx[:, 0] = np.concatenate([cx, cx], -1)
    tx[:, 1] = np.concatenate([sx, sx], -1)
    tx[:, 2] = np.concatenate([cx, -cx], -1)
    tx[:, 3] = np.concatenate([sx, -sx], -1)
    cy, sy = trig(ky[:, None] * shift[None, :])
    ty = np.zeros((SLABS, 2, ROWS, 128), np.float32)
    ty[:, 0, :, :33] = cy.reshape(SLABS, ROWS, 33)
    ty[:, 1, :, :33] = sy.reshape(SLABS, ROWS, 33)

    window = np.arange(SHIFTS) - SHIFTS // 2
    wcx, wsx = trig(kx[:, None] * window[None, :])
    wcy, wsy = trig(ky[:, None] * window[None, :])
    col_re = np.concatenate([wcx, -wsx], axis=0)
    col_im = np.concatenate([wsx, wcx], axis=0)
    col = np.zeros((4 * BOX, 256), np.float32)
    for k in range(4):
        col[k * BOX : (k + 1) * BOX, 32 * k : 32 * k + 32] = col_re
        col[k * BOX : (k + 1) * BOX, 128 + 32 * k : 160 + 32 * k] = col_im
    wcy = wcy.reshape(SLABS, ROWS, SHIFTS).transpose(0, 2, 1)
    wsy = wsy.reshape(SLABS, ROWS, SHIFTS).transpose(0, 2, 1)
    rowt = np.concatenate([wcy, -wsy], axis=-1)
    tri = (np.arange(BOX)[:, None] % KX <= np.arange(256)[None, :]).astype(np.float32)
    bf = ml_dtypes.bfloat16
    return (
        shell_of, ends, freq, tx, ty, col.astype(bf), rowt.astype(bf), tri.astype(bf),
    )


def flip_halves(x):
    return pltpu.roll(x, KX, 1)


def ctf_rows(freq, defocus):
    g = defocus * freq
    phi = math.atan2(0.1, 0.995)
    m = jnp.floor((g + phi) * (1.0 / math.pi) + 0.5)
    t = ((g - m * 3.140625) - m * 9.67653589793e-4) + phi
    odd = m - 2.0 * jnp.floor(m * 0.5)
    t2 = t * t
    p = -1.0 / 39916800.0
    for c in (1.0 / 362880.0, -1.0 / 5040.0, 1.0 / 120.0, -1.0 / 6.0, 1.0):
        p = p * t2 + c
    scale = math.sqrt(0.995 * 0.995 + 0.01)
    return (p * t) * ((2.0 * odd - 1.0) * scale)


def split3(x):
    hi = x.astype(BF16)
    rest = x - hi.astype(F32)
    mid = rest.astype(BF16)
    low = (rest - mid.astype(F32)).astype(BF16)
    return hi, mid, low


def main_kernel(
    ori_hbm, off_hbm, cls_hbm, defocus_hbm, slot_hbm, img_hbm, map_hbm,
    shell_hbm, ends_hbm, freq_hbm, tx_hbm, ty_hbm, col_hbm, rowt_hbm, tri_hbm,
    score_ref, corr_ref, new_ref,
    ori_ref, off_ref, cls_ref, defocus_ref, slot_ref,
    img, maps, other, shell_of, ends, freq, tx, ty, col, rowt, tri, weight_ref,
    packed, stage, regular, extra, contrib, vprod, eprod, ctf, eyb,
    meta_out, meta_stage, meta_in, meta_own, meta_all, link_v, link,
    ar1, ar2, ar3, arx, prod, part, parts_in, ret, ret_out,
    load_sem, own_sem, ring_sem, map_send, map_recv,
    img1_send, img1_recv, img2_send, img2_recv, ext_send, ext_recv,
    meta1_send, meta1_recv, meta2_send, meta2_recv,
    ar1_send, ar1_recv, ar2_send, ar2_recv, ar3_send, ar3_recv,
    part_send, part_recv, ret_send, ret_recv,
):
    h = lax.axis_index("half")
    d = lax.axis_index("dom")
    z = lax.axis_index("slab")
    y = d // 4
    q = d % 4
    g = h * 4 + q

    def flip(bits):
        hi = (q // 2 + bits // 2) % 2
        lo = (q % 2 + bits % 2) % 2
        return hi * 2 + lo

    def remote(src, dst, send, recv, where):
        return pltpu.make_async_remote_copy(
            src_ref=src, dst_ref=dst, send_sem=send, recv_sem=recv,
            device_id=where, device_id_type=MESH,
        )

    def signal(sem, where):
        pl.semaphore_signal(sem, inc=1, device_id=where, device_id_type=MESH)

    neighbours = (
        {"half": 1 - h}, {"half": 1 - h, "dom": y * 4 + flip(2)}, {"dom": y * 4 + flip(1)},
        {"dom": (y + 1) % 4 * 4 + q}, {"dom": (y + 3) % 4 * 4 + q},
        {"slab": (z + 1) % SLABS}, {"slab": (z + 7) % SLABS},
    )
    barrier = pltpu.get_barrier_semaphore()
    for where in neighbours:
        signal(barrier, where)

    loads = [
        (ori_hbm, ori_ref), (off_hbm, off_ref), (cls_hbm, cls_ref), (slot_hbm, slot_ref),
        (defocus_hbm, defocus_ref), (img_hbm, img), (freq_hbm.at[z], freq), (ty_hbm.at[z], ty),
        (map_hbm, maps), (tri_hbm, tri), (ends_hbm.at[z], ends), (tx_hbm, tx),
        (shell_hbm.at[z], shell_of), (col_hbm, col), (rowt_hbm.at[z], rowt),
    ]
    loads = [pltpu.make_async_copy(a, b, load_sem.at[i]) for i, (a, b) in enumerate(loads)]
    for c in loads:
        c.start()
    ld_small = loads[:4]
    (ld_defocus, ld_img, ld_freq, ld_ty, ld_map, ld_tri, ld_ends, ld_tx, ld_shell, ld_col, ld_rowt) = loads[4:]

    for c in ld_small:
        c.wait()
    lane1 = lax.broadcasted_iota(I32, (1, 128), 1)
    owner_row = lax.broadcasted_iota(I32, (DOMS, 128), 0)
    lane16 = lax.broadcasted_iota(I32, (DOMS, 128), 1)
    owners = []
    ranks = []
    second = jnp.int32(0)
    message = jnp.zeros((DOMS, 128), I32)
    for p in range(PART):
        place = slot_ref[ori_ref[p]]
        owner = place // ORI
        rank = jnp.int32(0)
        for before in owners:
            rank = rank + jnp.where(before == owner, 1, 0)
        owners.append(owner)
        ranks.append(rank)
        second = jnp.where(rank == 1, p, second)
        fields = (cls_ref[p], off_ref[0, p] + 16, off_ref[1, p] + 16, place % ORI, jnp.int32(1), jnp.int32(p))
        at = lane16 - 8 * rank
        for f, value in enumerate(fields):
            message = jnp.where((owner_row == owner) & (at == f), value, message)
    for o in range(DOMS):
        meta_out[o // 4, o % 4] = message[o : o + 1]
    own_copy = pltpu.make_async_copy(meta_out, meta_own, own_sem.at[0])
    own_copy.start()

    pl.semaphore_wait(barrier, len(neighbours))

    map_copies = []
    for c in range(NCHUNK):
        source = map_hbm.at[pl.ds((1 - h) * (ORI // 2) + c * CHUNK, CHUNK)]
        copy = remote(
            source, other.at[pl.ds(c * CHUNK, CHUNK)], map_send.at[c], map_recv.at[c], {"half": 1 - h}
        )
        copy.start()
        map_copies.append(copy)
    copies = list(map_copies)

    def ring(k):
        for where in neighbours:
            signal(ring_sem.at[k], where)

    ring(0)

    own_copy.wait()
    ld_img.wait()

    def pack(o, carry):
        packed[o // 4, o % 4] = img[meta_own[o // 4, o % 4, 0, 5]]
        return carry

    lax.fori_loop(0, DOMS, pack, 0)
    for t in range(4):
        packed[t, 4] = img[second]
    pl.semaphore_wait(ring_sem.at[0], len(neighbours))
    ring(1)

    for r in FAR4:
        to = (y + r) % 4
        copy = remote(
            meta_out.at[to], meta_stage.at[:, y], meta1_send.at[r], meta1_recv.at[y], {"dom": to * 4 + q}
        )
        copy.start()
        copies.append(copy)
    for r in FAR4:
        to = (y + r) % 4
        copy = remote(packed.at[to], stage.at[:, y], img1_send.at[r], img1_recv.at[y], {"dom": to * 4 + q})
        copy.start()
        copies.append(copy)
    own_img = pltpu.make_async_copy(packed.at[y], stage.at[:, y], own_sem.at[1])
    own_img.start()
    own_meta = pltpu.make_async_copy(meta_out.at[y], meta_stage.at[:, y], own_sem.at[2])
    own_meta.start()

    ld_freq.wait()
    ld_defocus.wait()

    def one_class(k, carry):
        ctf[k] = ctf_rows(freq[...], defocus_ref[k])
        return carry

    lax.fori_loop(0, CLASSES, one_class, 0)
    pl.semaphore_wait(ring_sem.at[1], len(neighbours))
    ring(2)
    ld_ty.wait()
    for part_of in range(2):
        for s in range(33):
            eyb[s, part_of] = jnp.broadcast_to(ty[part_of, :, s : s + 1], (ROWS, 128))

    for r in FAR4:
        s = (y + r) % 4
        remote(meta_out.at[s], meta_stage.at[:, s], meta1_send.at[r], meta1_recv.at[s], {"dom": s * 4 + q}).wait_recv()
    own_meta.wait()
    for bits in (3, 2, 1):
        to = flip(bits)
        copy = remote(
            meta_stage.at[to], meta_in.at[q], meta2_send.at[bits], meta2_recv.at[q], {"dom": y * 4 + to}
        )
        copy.start()
        copies.append(copy)
    last_meta = pltpu.make_async_copy(meta_stage.at[q], meta_in.at[q], own_sem.at[3])
    last_meta.start()

    ld_map.wait()

    def own_power(i, total):
        m = maps[i].astype(F32)
        return total + m * m

    own_sq = lax.fori_loop(0, ORI, own_power, jnp.zeros((ROWS, BOX), F32))
    pl.semaphore_wait(ring_sem.at[2], len(neighbours))
    ld_tri.wait()
    ld_ends.wait()

    def shell_sums(values):
        running = jnp.dot(jnp.concatenate(split3(values), axis=0), tri[...], preferred_element_type=F32)
        c = running[:ROWS] + (running[ROWS : 2 * ROWS] + running[2 * ROWS :])
        blocks = []
        for b in range(2):
            e = ends[:, 128 * b : 128 * b + 128]
            low = jnp.take_along_axis(c[:, :128], jnp.clip(e - 1, 0, 127), axis=1)
            high = jnp.take_along_axis(c[:, 128:], jnp.clip(e - 129, 0, 127), axis=1)
            got = jnp.where(e > 128, high, jnp.where(e > 0, low, 0.0))
            blocks.append(jnp.sum(got, axis=0, keepdims=True))
        first = blocks[0] - jnp.where(lane1 == 0, 0.0, pltpu.roll(blocks[0], 1, 1))
        carry_in = jnp.where(lane1 == 0, blocks[0][:, 127:128], pltpu.roll(blocks[1], 1, 1))
        return first, blocks[1] - carry_in

    power_sums = shell_sums(own_sq)
    cross = jnp.zeros((ROWS, BOX), F32)
    for c in range(NCHUNK):
        if c == NCHUNK - 1:
            for r in FAR4:
                s = (y + r) % 4
                remote(
                    packed.at[s], stage.at[:, s], img1_send.at[r], img1_recv.at[s], {"dom": s * 4 + q}
                ).wait_recv()
            own_img.wait()
            for kind, (src, dst, send, recv) in enumerate(
                ((stage.at[4], extra, ext_send, ext_recv), (stage.at[flip(1)], regular, img2_send, img2_recv))
            ):
                copy = remote(src, dst.at[q], send.at[1], recv.at[q], {"dom": y * 4 + flip(1)})
                copy.start()
                copies.append(copy)
            own_regular = pltpu.make_async_copy(stage.at[q], regular.at[q], own_sem.at[4])
            own_regular.start()
            own_extra = pltpu.make_async_copy(stage.at[4], extra.at[q], own_sem.at[5])
            own_extra.start()
        map_copies[c].wait_recv()

        def cross_term(i, total):
            mine = maps[h * (ORI // 2) + c * CHUNK + i].astype(F32)
            return total + mine * other[c * CHUNK + i].astype(F32)

        cross = lax.fori_loop(0, CHUNK, cross_term, cross)

    copy = remote(stage.at[4], extra.at[q], ext_send.at[2], ext_recv.at[q], {"dom": y * 4 + flip(2)})
    copy.start()
    copies.append(copy)
    for bits in (2, 3):
        to = flip(bits)
        copy = remote(stage.at[to], regular.at[q], img2_send.at[bits], img2_recv.at[q], {"dom": y * 4 + to})
        copy.start()
        copies.append(copy)

    sums = (shell_sums(cross), power_sums)
    shifted = (z == 3) | (z == 4)
    zero = jnp.zeros((1, 128), F32)
    for v in range(3):
        s0, s1 = sums[min(v, 1)]
        for b in range(3):
            block = jnp.where(shifted, (zero, s0, s1)[b], (s0, s1, zero)[b])
            if v > 0:
                block = jnp.where(h == v - 1, block, zero)
            arx[0, :, SHELLS * v + 128 * b : SHELLS * v + 128 * b + 128] = block

    for r in FAR8:
        to = (z + r) % SLABS
        copy = remote(arx.at[0], ar1.at[z], ar1_send.at[r], ar1_recv.at[z], {"slab": to})
        copy.start()
        copies.append(copy)

    last_meta.wait()
    for bits in (1, 2, 3):
        s = flip(bits)
        remote(meta_stage.at[s], meta_in.at[s], meta2_send.at[bits], meta2_recv.at[s], {"dom": y * 4 + s}).wait_recv()
    to_smem = pltpu.make_async_copy(meta_in, meta_all, own_sem.at[6])
    to_smem.start()

    numbers = jnp.concatenate([meta_in[c, t] for c in range(4) for t in range(4)], axis=0).astype(F32)

    def field(f):
        return jnp.sum(jnp.where(lane16 == f, numbers, 0.0), axis=1, keepdims=True)

    key = jnp.concatenate(
        [jnp.where(field(8 * e + 4) > 0.5, field(8 * e + 3), -1.0) for e in range(2)], axis=0
    )
    item_lane = lax.broadcasted_iota(I32, (SLOTS, 128), 1)
    item_row = lax.broadcasted_iota(I32, (SLOTS, 128), 0)
    across = jnp.sum(jnp.where(item_lane == item_row, key, 0.0), axis=0, keepdims=True)
    where_f = item_lane.astype(F32)
    last = jnp.max(
        jnp.where((across == item_row.astype(F32)) & (item_lane < SLOTS), where_f, -1.0), axis=1, keepdims=True
    )
    same = (across == key) & (item_lane < item_row) & (key >= 0.0)
    previous = jnp.max(jnp.where(same, where_f, -1.0), axis=1, keepdims=True)
    link_v[...] = jnp.where(item_lane == 0, last, jnp.where(item_lane == 1, previous, 0.0)).astype(I32)
    link_copy = pltpu.make_async_copy(link_v, link, own_sem.at[7])
    link_copy.start()

    ld_tx.wait()
    own_regular.wait()
    own_extra.wait()
    to_smem.wait()
    low_half = lax.broadcasted_iota(I32, (ROWS, BOX), 1) < KX

    def items_of(source, column, e):
        def one_item(t, carry):
            at = 8 * e
            phase_x = tx[meta_all[column, t, 0, at + 1]]
            phase_y = eyb[meta_all[column, t, 0, at + 2]]
            cy = jnp.concatenate([phase_y[0]] * 3, axis=1)
            sy = jnp.concatenate([phase_y[1]] * 3, axis=1)
            cos_t = phase_x[0:1] * cy - phase_x[1:2] * sy
            sin_t = phase_x[3:4] * cy + phase_x[2:3] * sy
            x = source[column, t].astype(F32)
            c = ctf[meta_all[column, t, 0, at]] * meta_all[column, t, 0, at + 4].astype(F32)
            zz = c * (x * cos_t + flip_halves(x) * sin_t)
            contrib[16 * e + 4 * column + t] = zz.astype(BF16)
            m = maps[meta_all[column, t, 0, at + 3]].astype(F32)
            straight = zz * m
            crossed = zz * flip_halves(m)
            n = 2 * (4 * t + column) + e
            vprod[n] = jnp.where(low_half, straight, -crossed) + flip_halves(
                jnp.where(low_half, crossed, straight)
            )
            cm = c * m
            eprod[n] = cm * cm
            return carry

        lax.fori_loop(0, 4, one_item, 0)

    def wait_regular(bits):
        s = flip(bits)
        remote(
            stage.at[s], regular.at[s], img2_send.at[bits], img2_recv.at[s], {"dom": y * 4 + s}
        ).wait_recv()

    def wait_extra(bits):
        s = flip(bits)
        remote(stage.at[4], extra.at[s], ext_send.at[bits], ext_recv.at[s], {"dom": y * 4 + s}).wait_recv()

    items_of(regular, q, 0)
    items_of(extra, q, 1)
    wait_extra(1)
    items_of(extra, flip(1), 1)
    ar1[z] = arx[0]
    for r in NEAR8:
        s = (z + r) % SLABS
        remote(arx.at[0], ar1.at[s], ar1_send.at[r], ar1_recv.at[s], {"slab": s}).wait_recv()
    total = ar1[0]
    for s in range(1, SLABS):
        total = total + ar1[s]
    arx[1] = total
    for r in FAR4:
        to = (y + r) % 4
        copy = remote(arx.at[1], ar2.at[y], ar2_send.at[r], ar2_recv.at[y], {"dom": to * 4 + q})
        copy.start()
        copies.append(copy)
    wait_regular(1)
    items_of(regular, flip(1), 0)
    wait_extra(2)
    copy = remote(
        extra.at[flip(2)], extra.at[flip(2)], ext_send.at[3], ext_recv.at[flip(2)], {"dom": y * 4 + flip(1)}
    )
    copy.start()
    copies.append(copy)
    ar2[y] = total
    for r in NEAR4:
        s = (y + r) % 4
        remote(arx.at[1], ar2.at[s], ar2_send.at[r], ar2_recv.at[s], {"dom": s * 4 + q}).wait_recv()
    total = ar2[0]
    for s in range(1, 4):
        total = total + ar2[s]
    arx[2] = total
    for r in FAR8:
        to = (g + r) % 8
        copy = remote(
            arx.at[2], ar3.at[g], ar3_send.at[r], ar3_recv.at[g], {"half": to // 4, "dom": y * 4 + to % 4}
        )
        copy.start()
        copies.append(copy)
    items_of(extra, flip(2), 1)
    wait_regular(2)
    items_of(regular, flip(2), 0)
    wait_extra(3)
    items_of(extra, flip(3), 1)
    wait_regular(3)
    items_of(regular, flip(3), 0)
    ar3[g] = total
    for r in NEAR8:
        s = (g + r) % 8
        remote(
            arx.at[2], ar3.at[s], ar3_send.at[r], ar3_recv.at[s], {"half": s // 4, "dom": y * 4 + s % 4}
        ).wait_recv()
    total = ar3[0]
    for s in range(1, 8):
        total = total + ar3[s]

    power = total[:, SHELLS : 2 * SHELLS] * total[:, 2 * SHELLS : 3 * SHELLS]
    fsc = total[:, :SHELLS] / jnp.sqrt(power + 1e-06)
    corr_ref[...] = fsc[0, :NSHELL]
    floor = jnp.maximum(fsc, 0.1)
    table0 = jnp.where(shifted, floor[:, 128:256], floor[:, 0:128])
    table1 = jnp.where(shifted, floor[:, 256:384], floor[:, 128:256])
    table0 = jnp.broadcast_to(table0, (ROWS, 128))
    table1 = jnp.broadcast_to(table1, (ROWS, 128))
    ld_shell.wait()
    for b in range(3):
        at = shell_of[:, 128 * b : 128 * b + 128]
        low = jnp.take_along_axis(table0, jnp.minimum(at, 127), axis=1)
        high = jnp.take_along_axis(table1, jnp.maximum(at - 128, 0), axis=1)
        weight_ref[:, 128 * b : 128 * b + 128] = jnp.where(at < 128, low, high)
    w = weight_ref[...]

    ld_col.wait()
    ld_rowt.wait()
    for half, start in enumerate((3, 7)):

        def weigh(j, carry):
            t = (z + start + j) % SLABS
            energies = []
            for k in range(4):
                prod[4 * half + j, :, BOX * k : BOX * k + BOX] = (vprod[4 * t + k] * w).astype(BF16)
                e = jnp.sum(eprod[4 * t + k] * w, axis=0, keepdims=True)
                energies.append(e[:, 0:128] + e[:, 128:256] + e[:, 256:384])
            energies = jnp.concatenate(energies, axis=0)
            part[t, 32:48, :] = jnp.concatenate(list(split3(energies)) + [jnp.zeros((4, 128), BF16)], axis=0)
            return carry

        lax.fori_loop(0, 4, weigh, 0)
        section = jnp.dot(
            prod[4 * half : 4 * half + 4].reshape(4 * ROWS, 4 * BOX), col[...], preferred_element_type=F32
        ).astype(BF16)
        stacked = jnp.concatenate(
            [
                jnp.concatenate(
                    [section[ROWS * j : ROWS * j + ROWS, :128], section[ROWS * j : ROWS * j + ROWS, 128:]],
                    axis=0,
                )
                for j in range(4)
            ],
            axis=1,
        )
        partial = jnp.dot(rowt[...], stacked, preferred_element_type=F32).astype(BF16)
        for j in range(4):
            part[(z + start + j) % SLABS, 0:32, :] = partial[:, 128 * j : 128 * j + 128]
        for j in (1, 2, 0, 3):
            r = (start + j) % SLABS
            if r == 0:
                continue
            to = (z + r) % SLABS
            copy = remote(part.at[to], parts_in.at[z], part_send.at[r], part_recv.at[z], {"slab": to})
            copy.start()
            copies.append(copy)

    link_copy.wait()

    def add_item(u, carry):
        e = u // 16
        before = link[u, 1]
        has = jnp.where(before >= 0, 1.0, 0.0)
        from_u = jnp.minimum(jnp.maximum(before, 0), SLOTS - 1)
        column = (u % 16) // 4
        t = u % 4
        c = ctf[meta_all[column, t, 0, 8 * e]]
        valid = meta_all[column, t, 0, 8 * e + 4].astype(F32)
        vprod[u] = contrib[u].astype(F32) + has * vprod[from_u]
        eprod[u] = (c * c) * valid + has * eprod[from_u]
        return carry

    lax.fori_loop(0, SLOTS, add_item, 0)
    whole = part[z].astype(F32)
    for r in NEAR8:
        s = (z + r) % SLABS
        remote(part.at[s], parts_in.at[s], part_send.at[r], part_recv.at[s], {"slab": s}).wait_recv()
        whole = whole + parts_in[s].astype(F32)
    best = jnp.max(whole[0:32], axis=0, keepdims=True)
    lane4 = lax.broadcasted_iota(I32, (4, 128), 1)
    row4 = lax.broadcasted_iota(I32, (4, 128), 0)
    top = jnp.max(jnp.where(lane4 // 32 == row4, best, -jnp.inf), axis=1, keepdims=True)
    energy = jnp.sum(whole[32:36] + (whole[36:40] + whole[40:44]), axis=1, keepdims=True)
    value = top / jnp.sqrt(energy + 1e-06)
    answer = jnp.sum(jnp.where(lane4 == row4, value, 0.0), axis=0, keepdims=True)
    ret_out[...] = answer

    def score_copy(e, r):
        return remote(
            ret_out, ret.at[d], ret_send.at[8 * e + r], ret_recv.at[d],
            {"dom": 2 * z + e, "slab": (z + r) % SLABS},
        )

    for r in FAR8:
        for e in range(2):
            score_copy(e, r).start()
    for e in range(2):
        pl.when(2 * z + e != d)(score_copy(e, 0).start)

    @pl.when(d // 2 == z)
    def _():
        ret[d] = answer

    def one_slice(r, carry):
        at = link[r, 0]
        has = jnp.where(at >= 0, 1.0, 0.0)
        at = jnp.minimum(jnp.maximum(at, 0), SLOTS - 1)
        inverse = 1.0 / weight_ref[...]
        top = has * vprod[at] + maps[r].astype(F32) * inverse
        new_ref[r] = top / (has * eprod[at] + inverse)
        return carry

    lax.fori_loop(0, ORI, one_slice, 0)

    for copy in copies:
        copy.wait_send()
    for e in range(2):
        for r in FAR8:
            score_copy(e, r).wait_send()
        pl.when(2 * z + e != d)(score_copy(e, 0).wait_send)
    for r in range(DOMS):
        s = (d + r) % DOMS
        copy = remote(ret_out, ret.at[s], ret_send.at[r], ret_recv.at[s], {"dom": s, "slab": d // 2})
        if r == 0:
            pl.when(d // 2 != z)(copy.wait_recv)
        else:
            copy.wait_recv()
    picked = [jnp.where(lane1 == 2 * (d % 2) + ranks[p], ret[owners[p]], 0.0) for p in range(PART)]
    picked = jnp.sum(jnp.concatenate(picked, axis=0), axis=1, keepdims=True)
    lane8 = lax.broadcasted_iota(I32, (PART, 128), 1)
    row8 = lax.broadcasted_iota(I32, (PART, 128), 0)
    scores = jnp.sum(jnp.where(lane8 == row8, picked, 0.0), axis=0, keepdims=True)
    score_ref[...] = scores[:, :PART]


DELIVER = 8


def deliver_kernel(score_in, corr_in, new_in, score_out, corr_out, new_out, sem):
    step = ORI // DELIVER
    writes = []
    for t in range(DELIVER):
        block = pl.ds(step * t, step)
        writes.append(pltpu.make_async_copy(new_in.at[block], new_out.at[block], sem.at[t]))
    writes.append(pltpu.make_async_copy(score_in, score_out, sem.at[DELIVER]))
    writes.append(pltpu.make_async_copy(corr_in, corr_out, sem.at[DELIVER + 1]))
    for copy in writes:
        copy.start()
    for copy in writes:
        copy.wait()


def deliver(scores, fsc, new_maps):
    hbm = pl.BlockSpec(memory_space=pl.ANY)
    vmem = pl.BlockSpec(memory_space=pltpu.VMEM)
    return pl.pallas_call(
        deliver_kernel,
        out_shape=(
            jax.ShapeDtypeStruct((1, PART), F32),
            jax.ShapeDtypeStruct((NSHELL,), F32),
            jax.ShapeDtypeStruct((ORI, ROWS, BOX), F32),
        ),
        in_specs=[vmem, vmem, vmem],
        out_specs=(hbm, hbm, hbm),
        scratch_shapes=[
            pltpu.SemaphoreType.DMA((DELIVER + 2,)),
        ],
        compiler_params=pltpu.CompilerParams(vmem_limit_bytes=16 * 1024 * 1024),
        name="deliver",
    )(scores, fsc, new_maps)


def run_main(*operands):
    hbm = pl.BlockSpec(memory_space=pltpu.HBM)
    vmem = pl.BlockSpec(memory_space=pltpu.VMEM)
    v = pltpu.VMEM
    smem = pltpu.SMEM
    dma = pltpu.SemaphoreType.DMA
    return pl.pallas_call(
        main_kernel,
        out_shape=(
            pltpu.VMEM((1, PART), F32),
            pltpu.VMEM((NSHELL,), F32),
            pltpu.VMEM((ORI, ROWS, BOX), F32),
        ),
        in_specs=[hbm] * 15,
        out_specs=(vmem, vmem, vmem),
        scratch_shapes=[
            smem((PART,), I32), smem((2, PART), I32), smem((PART,), I32), smem((CLASSES,), F32),
            smem((512,), I32),
            v((PART, ROWS, BOX), BF16),
            v((ORI, ROWS, BOX), BF16),
            v((ORI // 2, ROWS, BOX), BF16),
            v((ROWS, BOX), I32),
            v((ROWS, 256), I32),
            v((ROWS, BOX), F32),
            v((33, 8, BOX), F32),
            v((2, ROWS, 128), F32),
            v((4 * BOX, 256), BF16),
            v((SHIFTS, 2 * ROWS), BF16),
            v((BOX, 256), BF16),
            v((ROWS, BOX), F32),
            v((4, 5, ROWS, BOX), BF16),
            v((5, 4, ROWS, BOX), BF16),
            v((4, 4, ROWS, BOX), BF16),
            v((4, 4, ROWS, BOX), BF16),
            v((SLOTS, ROWS, BOX), BF16),
            v((SLOTS, ROWS, BOX), F32),
            v((SLOTS, ROWS, BOX), F32),
            v((CLASSES, ROWS, BOX), F32),
            v((33, 2, ROWS, 128), F32),
            v((4, 4, 1, 128), I32),
            v((4, 4, 1, 128), I32),
            v((4, 4, 1, 128), I32),
            smem((4, 4, 1, 128), I32),
            smem((4, 4, 1, 128), I32),
            v((SLOTS, 128), I32),
            smem((SLOTS, 128), I32),
            v((8, 1, 3 * SHELLS), F32),
            v((4, 1, 3 * SHELLS), F32),
            v((8, 1, 3 * SHELLS), F32),
            v((3, 1, 3 * SHELLS), F32),
            v((SLABS, ROWS, 4 * BOX), BF16),
            v((SLABS, 48, 128), BF16),
            v((SLABS, 48, 128), BF16),
            v((DOMS, 1, 128), F32),
            v((1, 128), F32),
            dma((15,)),
            dma((8,)),
            pltpu.SemaphoreType.REGULAR((3,)),
            dma((NCHUNK,)), dma((NCHUNK,)),
            dma((4,)), dma((4,)),
            dma((4,)), dma((4,)),
            dma((4,)), dma((4,)),
            dma((4,)), dma((4,)),
            dma((4,)), dma((4,)),
            dma((8,)), dma((8,)),
            dma((4,)), dma((4,)),
            dma((8,)), dma((8,)),
            dma((8,)), dma((8,)),
            dma((16,)), dma((16,)),
        ],
        compiler_params=pltpu.CompilerParams(
            collective_id=0, has_side_effects=True, vmem_limit_bytes=44 * 1024 * 1024
        ),
        name="refine",
    )(*[pltpu.with_memory_space_constraint(x, pltpu.HBM) for x in operands])


def on_device(consts, images, orientation, offsets, defocus_class, defocus, ori_slot, half_maps):
    scores, fsc, new_maps = run_main(
        orientation[0], offsets[0].T, defocus_class[0], defocus, ori_slot, images[0], half_maps[0], *consts
    )
    scores, fsc, new_maps = deliver(scores, fsc, new_maps)
    return scores, new_maps[None], fsc


def solution(mesh):
    in_specs = (
        P("half", "dom", "slab", None),
        P("half", "dom"),
        P("half", "dom", None),
        P("half", "dom"),
        P(),
        P(),
        P("half", "dom", "slab", None),
    )
    out_specs = (P("half", "dom"), P("half", "dom", "slab", None), P())
    return jax.shard_map(
        functools.partial(on_device, tables()),
        mesh=mesh, in_specs=in_specs, out_specs=out_specs, check_vma=False,
    )
```

```python
import functools
import math

import jax
import jax.numpy as jnp
import ml_dtypes
import numpy as np
from jax import lax
from jax.experimental import pallas as pl
from jax.experimental.pallas import tpu as pltpu
from jax.sharding import PartitionSpec as P

BOX = 384
KX = 192
SHIFTS = 32
NSHELL = 267
ROWS = 48
SLABS = 8
DOMS = 16
PART = 8
ORI = 32
CLASSES = 16
SLOTS = 32
SHELLS = 384
CHUNK = 4
NCHUNK = 4
F32 = jnp.float32
BF16 = jnp.bfloat16
I32 = jnp.int32
MESH = pl.DeviceIdType.MESH
FAR8 = (4, 3, 5, 2, 6, 1, 7)
NEAR8 = FAR8[::-1]
FAR4 = (2, 1, 3)
NEAR4 = FAR4[::-1]


def tables():
    row = np.arange(BOX)
    ky = np.where(row < KX, row, row - BOX)
    kx = np.arange(KX)
    q = ky[:, None] ** 2 + kx[None, :] ** 2
    radius = np.floor(np.sqrt(q.astype(np.float64))).astype(np.int64)
    radius -= radius * radius > q
    radius += (radius + 1) * (radius + 1) <= q
    shell = np.clip(radius - 1, 0, NSHELL - 1)
    base = np.array([0, 0, 0, 128, 128, 0, 0, 0])
    local = shell.reshape(SLABS, ROWS, KX) - base[:, None, None]
    assert local.min() >= 0 and local.max() < 256
    shell_of = np.concatenate([local, local], axis=-1).astype(np.int32)
    ends = np.zeros((SLABS, ROWS, 256), np.int32)
    for s in range(256):
        ends[:, :, s] = (local <= s).sum(-1)
    freq = np.concatenate([q, q], axis=-1).reshape(SLABS, ROWS, BOX).astype(np.float32)
    freq = freq / np.float32(BOX * BOX)
    unit = np.float32(2.0 * math.pi / BOX)

    def trig(index):
        angle = (np.mod(index, BOX).astype(np.float32) * unit).astype(np.float32)
        return np.cos(angle).astype(np.float32), np.sin(angle).astype(np.float32)

    shift = np.arange(33) - 16
    cx, sx = trig(shift[:, None] * kx[None, :])
    tx = np.zeros((33, 8, BOX), np.float32)
    tx[:, 0] = np.concatenate([cx, cx], -1)
    tx[:, 1] = np.concatenate([sx, sx], -1)
    tx[:, 2] = np.concatenate([cx, -cx], -1)
    tx[:, 3] = np.concatenate([sx, -sx], -1)
    cy, sy = trig(ky[:, None] * shift[None, :])
    ty = np.zeros((SLABS, 2, ROWS, 128), np.float32)
    ty[:, 0, :, :33] = cy.reshape(SLABS, ROWS, 33)
    ty[:, 1, :, :33] = sy.reshape(SLABS, ROWS, 33)

    window = np.arange(SHIFTS) - SHIFTS // 2
    wcx, wsx = trig(kx[:, None] * window[None, :])
    wcy, wsy = trig(ky[:, None] * window[None, :])
    col_re = np.concatenate([wcx, -wsx], axis=0)
    col_im = np.concatenate([wsx, wcx], axis=0)
    col = np.zeros((4 * BOX, 256), np.float32)
    for k in range(4):
        col[k * BOX : (k + 1) * BOX, 32 * k : 32 * k + 32] = col_re
        col[k * BOX : (k + 1) * BOX, 128 + 32 * k : 160 + 32 * k] = col_im
    wcy = wcy.reshape(SLABS, ROWS, SHIFTS).transpose(0, 2, 1)
    wsy = wsy.reshape(SLABS, ROWS, SHIFTS).transpose(0, 2, 1)
    rowt = np.concatenate([wcy, -wsy], axis=-1)
    tri = (np.arange(BOX)[:, None] % KX <= np.arange(256)[None, :]).astype(np.float32)
    bf = ml_dtypes.bfloat16
    return (
        shell_of, ends, freq, tx, ty, col.astype(bf), rowt.astype(bf), tri.astype(bf),
    )


def flip_halves(x):
    return pltpu.roll(x, KX, 1)


def ctf_rows(freq, defocus):
    g = defocus * freq
    phi = math.atan2(0.1, 0.995)
    m = jnp.floor((g + phi) * (1.0 / math.pi) + 0.5)
    t = ((g - m * 3.140625) - m * 9.67653589793e-4) + phi
    odd = m - 2.0 * jnp.floor(m * 0.5)
    t2 = t * t
    p = -1.0 / 39916800.0
    for c in (1.0 / 362880.0, -1.0 / 5040.0, 1.0 / 120.0, -1.0 / 6.0, 1.0):
        p = p * t2 + c
    scale = math.sqrt(0.995 * 0.995 + 0.01)
    return (p * t) * ((2.0 * odd - 1.0) * scale)


def split3(x):
    hi = x.astype(BF16)
    rest = x - hi.astype(F32)
    mid = rest.astype(BF16)
    low = (rest - mid.astype(F32)).astype(BF16)
    return hi, mid, low


def main_kernel(
    ori_hbm, off_hbm, cls_hbm, defocus_hbm, slot_hbm, img_hbm, map_hbm,
    shell_hbm, ends_hbm, freq_hbm, tx_hbm, ty_hbm, col_hbm, rowt_hbm, tri_hbm,
    score_ref, corr_ref, new_ref,
    ori_ref, off_ref, cls_ref, defocus_ref, slot_ref,
    img, maps, other, shell_of, ends, freq, tx, ty, col, rowt, tri, weight_ref,
    packed, stage, regular, extra, contrib, vprod, eprod, ctf, eyb,
    meta_out, meta_stage, meta_in, meta_own, meta_all, link_v, link,
    ar1, ar2, ar3, arx, prod, part, parts_in, ret, ret_out,
    load_sem, own_sem, ring_sem, map_send, map_recv,
    img1_send, img1_recv, img2_send, img2_recv, ext_send, ext_recv,
    meta1_send, meta1_recv, meta2_send, meta2_recv,
    ar1_send, ar1_recv, ar2_send, ar2_recv, ar3_send, ar3_recv,
    part_send, part_recv, ret_send, ret_recv,
):
    h = lax.axis_index("half")
    d = lax.axis_index("dom")
    z = lax.axis_index("slab")
    y = d // 4
    q = d % 4
    g = h * 4 + q

    def flip(bits):
        hi = (q // 2 + bits // 2) % 2
        lo = (q % 2 + bits % 2) % 2
        return hi * 2 + lo

    def remote(src, dst, send, recv, where):
        return pltpu.make_async_remote_copy(
            src_ref=src, dst_ref=dst, send_sem=send, recv_sem=recv,
            device_id=where, device_id_type=MESH,
        )

    def signal(sem, where):
        pl.semaphore_signal(sem, inc=1, device_id=where, device_id_type=MESH)

    neighbours = (
        {"half": 1 - h}, {"half": 1 - h, "dom": y * 4 + flip(2)}, {"dom": y * 4 + flip(1)},
        {"dom": (y + 1) % 4 * 4 + q}, {"dom": (y + 3) % 4 * 4 + q},
        {"slab": (z + 1) % SLABS}, {"slab": (z + 7) % SLABS},
    )
    barrier = pltpu.get_barrier_semaphore()
    for where in neighbours:
        signal(barrier, where)

    loads = [
        (ori_hbm, ori_ref), (off_hbm, off_ref), (cls_hbm, cls_ref), (slot_hbm, slot_ref),
        (defocus_hbm, defocus_ref), (img_hbm, img), (freq_hbm.at[z], freq), (ty_hbm.at[z], ty),
        (map_hbm, maps), (tri_hbm, tri), (ends_hbm.at[z], ends), (tx_hbm, tx),
        (shell_hbm.at[z], shell_of), (col_hbm, col), (rowt_hbm.at[z], rowt),
    ]
    loads = [pltpu.make_async_copy(a, b, load_sem.at[i]) for i, (a, b) in enumerate(loads)]
    for c in loads:
        c.start()
    ld_small = loads[:4]
    (ld_defocus, ld_img, ld_freq, ld_ty, ld_map, ld_tri, ld_ends, ld_tx, ld_shell, ld_col, ld_rowt) = loads[4:]

    for c in ld_small:
        c.wait()
    lane1 = lax.broadcasted_iota(I32, (1, 128), 1)
    owner_row = lax.broadcasted_iota(I32, (DOMS, 128), 0)
    lane16 = lax.broadcasted_iota(I32, (DOMS, 128), 1)
    owners = []
    ranks = []
    second = jnp.int32(0)
    message = jnp.zeros((DOMS, 128), I32)
    for p in range(PART):
        place = slot_ref[ori_ref[p]]
        owner = place // ORI
        rank = jnp.int32(0)
        for before in owners:
            rank = rank + jnp.where(before == owner, 1, 0)
        owners.append(owner)
        ranks.append(rank)
        second = jnp.where(rank == 1, p, second)
        fields = (cls_ref[p], off_ref[0, p] + 16, off_ref[1, p] + 16, place % ORI, jnp.int32(1), jnp.int32(p))
        at = lane16 - 8 * rank
        for f, value in enumerate(fields):
            message = jnp.where((owner_row == owner) & (at == f), value, message)
    for o in range(DOMS):
        meta_out[o // 4, o % 4] = message[o : o + 1]
    own_copy = pltpu.make_async_copy(meta_out, meta_own, own_sem.at[0])
    own_copy.start()

    pl.semaphore_wait(barrier, len(neighbours))

    map_copies = []
    for c in range(NCHUNK):
        source = map_hbm.at[pl.ds((1 - h) * (ORI // 2) + c * CHUNK, CHUNK)]
        copy = remote(
            source, other.at[pl.ds(c * CHUNK, CHUNK)], map_send.at[c], map_recv.at[c], {"half": 1 - h}
        )
        copy.start()
        map_copies.append(copy)
    copies = list(map_copies)

    def ring(k):
        for where in neighbours:
            signal(ring_sem.at[k], where)

    ring(0)

    own_copy.wait()
    ld_img.wait()

    def pack(o, carry):
        packed[o // 4, o % 4] = img[meta_own[o // 4, o % 4, 0, 5]]
        return carry

    lax.fori_loop(0, DOMS, pack, 0)
    for t in range(4):
        packed[t, 4] = img[second]
    pl.semaphore_wait(ring_sem.at[0], len(neighbours))
    ring(1)

    for r in FAR4:
        to = (y + r) % 4
        copy = remote(
            meta_out.at[to], meta_stage.at[:, y], meta1_send.at[r], meta1_recv.at[y], {"dom": to * 4 + q}
        )
        copy.start()
        copies.append(copy)
    for r in FAR4:
        to = (y + r) % 4
        copy = remote(packed.at[to], stage.at[:, y], img1_send.at[r], img1_recv.at[y], {"dom": to * 4 + q})
        copy.start()
        copies.append(copy)
    own_img = pltpu.make_async_copy(packed.at[y], stage.at[:, y], own_sem.at[1])
    own_img.start()
    own_meta = pltpu.make_async_copy(meta_out.at[y], meta_stage.at[:, y], own_sem.at[2])
    own_meta.start()

    ld_freq.wait()
    ld_defocus.wait()

    def one_class(k, carry):
        ctf[k] = ctf_rows(freq[...], defocus_ref[k])
        return carry

    lax.fori_loop(0, CLASSES, one_class, 0)
    pl.semaphore_wait(ring_sem.at[1], len(neighbours))
    ring(2)
    ld_ty.wait()
    for part_of in range(2):
        for s in range(33):
            eyb[s, part_of] = jnp.broadcast_to(ty[part_of, :, s : s + 1], (ROWS, 128))

    for r in FAR4:
        s = (y + r) % 4
        remote(meta_out.at[s], meta_stage.at[:, s], meta1_send.at[r], meta1_recv.at[s], {"dom": s * 4 + q}).wait_recv()
    own_meta.wait()
    for bits in (3, 2, 1):
        to = flip(bits)
        copy = remote(
            meta_stage.at[to], meta_in.at[q], meta2_send.at[bits], meta2_recv.at[q], {"dom": y * 4 + to}
        )
        copy.start()
        copies.append(copy)
    last_meta = pltpu.make_async_copy(meta_stage.at[q], meta_in.at[q], own_sem.at[3])
    last_meta.start()

    ld_map.wait()

    def own_power(i, total):
        m = maps[i].astype(F32)
        return total + m * m

    own_sq = lax.fori_loop(0, ORI, own_power, jnp.zeros((ROWS, BOX), F32))
    pl.semaphore_wait(ring_sem.at[2], len(neighbours))
    ld_tri.wait()
    ld_ends.wait()

    def shell_sums(values):
        running = jnp.dot(jnp.concatenate(split3(values), axis=0), tri[...], preferred_element_type=F32)
        c = running[:ROWS] + (running[ROWS : 2 * ROWS] + running[2 * ROWS :])
        blocks = []
        for b in range(2):
            e = ends[:, 128 * b : 128 * b + 128]
            low = jnp.take_along_axis(c[:, :128], jnp.clip(e - 1, 0, 127), axis=1)
            high = jnp.take_along_axis(c[:, 128:], jnp.clip(e - 129, 0, 127), axis=1)
            got = jnp.where(e > 128, high, jnp.where(e > 0, low, 0.0))
            blocks.append(jnp.sum(got, axis=0, keepdims=True))
        first = blocks[0] - jnp.where(lane1 == 0, 0.0, pltpu.roll(blocks[0], 1, 1))
        carry_in = jnp.where(lane1 == 0, blocks[0][:, 127:128], pltpu.roll(blocks[1], 1, 1))
        return first, blocks[1] - carry_in

    power_sums = shell_sums(own_sq)
    cross = jnp.zeros((ROWS, BOX), F32)
    for c in range(NCHUNK):
        if c == NCHUNK - 1:
            for r in FAR4:
                s = (y + r) % 4
                remote(
                    packed.at[s], stage.at[:, s], img1_send.at[r], img1_recv.at[s], {"dom": s * 4 + q}
                ).wait_recv()
            own_img.wait()
            for kind, (src, dst, send, recv) in enumerate(
                ((stage.at[4], extra, ext_send, ext_recv), (stage.at[flip(1)], regular, img2_send, img2_recv))
            ):
                copy = remote(src, dst.at[q], send.at[1], recv.at[q], {"dom": y * 4 + flip(1)})
                copy.start()
                copies.append(copy)
            own_regular = pltpu.make_async_copy(stage.at[q], regular.at[q], own_sem.at[4])
            own_regular.start()
            own_extra = pltpu.make_async_copy(stage.at[4], extra.at[q], own_sem.at[5])
            own_extra.start()
        map_copies[c].wait_recv()

        def cross_term(i, total):
            mine = maps[h * (ORI // 2) + c * CHUNK + i].astype(F32)
            return total + mine * other[c * CHUNK + i].astype(F32)

        cross = lax.fori_loop(0, CHUNK, cross_term, cross)

    copy = remote(stage.at[4], extra.at[q], ext_send.at[2], ext_recv.at[q], {"dom": y * 4 + flip(2)})
    copy.start()
    copies.append(copy)
    for bits in (2, 3):
        to = flip(bits)
        copy = remote(stage.at[to], regular.at[q], img2_send.at[bits], img2_recv.at[q], {"dom": y * 4 + to})
        copy.start()
        copies.append(copy)

    sums = (shell_sums(cross), power_sums)
    shifted = (z == 3) | (z == 4)
    zero = jnp.zeros((1, 128), F32)
    for v in range(3):
        s0, s1 = sums[min(v, 1)]
        for b in range(3):
            block = jnp.where(shifted, (zero, s0, s1)[b], (s0, s1, zero)[b])
            if v > 0:
                block = jnp.where(h == v - 1, block, zero)
            arx[0, :, SHELLS * v + 128 * b : SHELLS * v + 128 * b + 128] = block

    for r in FAR8:
        to = (z + r) % SLABS
        copy = remote(arx.at[0], ar1.at[z], ar1_send.at[r], ar1_recv.at[z], {"slab": to})
        copy.start()
        copies.append(copy)

    last_meta.wait()
    for bits in (1, 2, 3):
        s = flip(bits)
        remote(meta_stage.at[s], meta_in.at[s], meta2_send.at[bits], meta2_recv.at[s], {"dom": y * 4 + s}).wait_recv()
    to_smem = pltpu.make_async_copy(meta_in, meta_all, own_sem.at[6])
    to_smem.start()

    numbers = jnp.concatenate([meta_in[c, t] for c in range(4) for t in range(4)], axis=0).astype(F32)

    def field(f):
        return jnp.sum(jnp.where(lane16 == f, numbers, 0.0), axis=1, keepdims=True)

    key = jnp.concatenate(
        [jnp.where(field(8 * e + 4) > 0.5, field(8 * e + 3), -1.0) for e in range(2)], axis=0
    )
    item_lane = lax.broadcasted_iota(I32, (SLOTS, 128), 1)
    item_row = lax.broadcasted_iota(I32, (SLOTS, 128), 0)
    across = jnp.sum(jnp.where(item_lane == item_row, key, 0.0), axis=0, keepdims=True)
    where_f = item_lane.astype(F32)
    last = jnp.max(
        jnp.where((across == item_row.astype(F32)) & (item_lane < SLOTS), where_f, -1.0), axis=1, keepdims=True
    )
    same = (across == key) & (item_lane < item_row) & (key >= 0.0)
    previous = jnp.max(jnp.where(same, where_f, -1.0), axis=1, keepdims=True)
    link_v[...] = jnp.where(item_lane == 0, last, jnp.where(item_lane == 1, previous, 0.0)).astype(I32)
    link_copy = pltpu.make_async_copy(link_v, link, own_sem.at[7])
    link_copy.start()

    ld_tx.wait()
    own_regular.wait()
    own_extra.wait()
    to_smem.wait()
    low_half = lax.broadcasted_iota(I32, (ROWS, BOX), 1) < KX

    def items_of(source, column, e):
        def one_item(t, carry):
            at = 8 * e
            phase_x = tx[meta_all[column, t, 0, at + 1]]
            phase_y = eyb[meta_all[column, t, 0, at + 2]]
            cy = jnp.concatenate([phase_y[0]] * 3, axis=1)
            sy = jnp.concatenate([phase_y[1]] * 3, axis=1)
            cos_t = phase_x[0:1] * cy - phase_x[1:2] * sy
            sin_t = phase_x[3:4] * cy + phase_x[2:3] * sy
            x = source[column, t].astype(F32)
            c = ctf[meta_all[column, t, 0, at]] * meta_all[column, t, 0, at + 4].astype(F32)
            zz = c * (x * cos_t + flip_halves(x) * sin_t)
            contrib[16 * e + 4 * column + t] = zz.astype(BF16)
            m = maps[meta_all[column, t, 0, at + 3]].astype(F32)
            straight = zz * m
            crossed = zz * flip_halves(m)
            n = 2 * (4 * t + column) + e
            vprod[n] = jnp.where(low_half, straight, -crossed) + flip_halves(
                jnp.where(low_half, crossed, straight)
            )
            cm = c * m
            eprod[n] = cm * cm
            return carry

        lax.fori_loop(0, 4, one_item, 0)

    def wait_regular(bits):
        s = flip(bits)
        remote(
            stage.at[s], regular.at[s], img2_send.at[bits], img2_recv.at[s], {"dom": y * 4 + s}
        ).wait_recv()

    def wait_extra(bits):
        s = flip(bits)
        remote(stage.at[4], extra.at[s], ext_send.at[bits], ext_recv.at[s], {"dom": y * 4 + s}).wait_recv()

    items_of(regular, q, 0)
    items_of(extra, q, 1)
    wait_extra(1)
    items_of(extra, flip(1), 1)
    ar1[z] = arx[0]
    for r in NEAR8:
        s = (z + r) % SLABS
        remote(arx.at[0], ar1.at[s], ar1_send.at[r], ar1_recv.at[s], {"slab": s}).wait_recv()
    total = ar1[0]
    for s in range(1, SLABS):
        total = total + ar1[s]
    arx[1] = total
    for r in FAR4:
        to = (y + r) % 4
        copy = remote(arx.at[1], ar2.at[y], ar2_send.at[r], ar2_recv.at[y], {"dom": to * 4 + q})
        copy.start()
        copies.append(copy)
    wait_regular(1)
    items_of(regular, flip(1), 0)
    wait_extra(2)
    copy = remote(
        extra.at[flip(2)], extra.at[flip(2)], ext_send.at[3], ext_recv.at[flip(2)], {"dom": y * 4 + flip(1)}
    )
    copy.start()
    copies.append(copy)
    ar2[y] = total
    for r in NEAR4:
        s = (y + r) % 4
        remote(arx.at[1], ar2.at[s], ar2_send.at[r], ar2_recv.at[s], {"dom": s * 4 + q}).wait_recv()
    total = ar2[0]
    for s in range(1, 4):
        total = total + ar2[s]
    arx[2] = total
    for r in FAR8:
        to = (g + r) % 8
        copy = remote(
            arx.at[2], ar3.at[g], ar3_send.at[r], ar3_recv.at[g], {"half": to // 4, "dom": y * 4 + to % 4}
        )
        copy.start()
        copies.append(copy)
    items_of(extra, flip(2), 1)
    wait_regular(2)
    items_of(regular, flip(2), 0)
    wait_extra(3)
    items_of(extra, flip(3), 1)
    wait_regular(3)
    items_of(regular, flip(3), 0)
    ar3[g] = total
    for r in NEAR8:
        s = (g + r) % 8
        remote(
            arx.at[2], ar3.at[s], ar3_send.at[r], ar3_recv.at[s], {"half": s // 4, "dom": y * 4 + s % 4}
        ).wait_recv()
    total = ar3[0]
    for s in range(1, 8):
        total = total + ar3[s]

    power = total[:, SHELLS : 2 * SHELLS] * total[:, 2 * SHELLS : 3 * SHELLS]
    fsc = total[:, :SHELLS] / jnp.sqrt(power + 1e-06)
    corr_ref[...] = fsc[0, :NSHELL]
    floor = jnp.maximum(fsc, 0.1)
    table0 = jnp.where(shifted, floor[:, 128:256], floor[:, 0:128])
    table1 = jnp.where(shifted, floor[:, 256:384], floor[:, 128:256])
    table0 = jnp.broadcast_to(table0, (ROWS, 128))
    table1 = jnp.broadcast_to(table1, (ROWS, 128))
    ld_shell.wait()
    for b in range(3):
        at = shell_of[:, 128 * b : 128 * b + 128]
        low = jnp.take_along_axis(table0, jnp.minimum(at, 127), axis=1)
        high = jnp.take_along_axis(table1, jnp.maximum(at - 128, 0), axis=1)
        weight_ref[:, 128 * b : 128 * b + 128] = jnp.where(at < 128, low, high)
    w = weight_ref[...]

    ld_col.wait()
    ld_rowt.wait()
    for half, start in enumerate((3, 5, 1, 7)):

        def weigh(j, carry):
            t = (z + start + j) % SLABS
            energies = []
            for k in range(4):
                prod[2 * half + j, :, BOX * k : BOX * k + BOX] = (vprod[4 * t + k] * w).astype(BF16)
                e = jnp.sum(eprod[4 * t + k] * w, axis=0, keepdims=True)
                energies.append(e[:, 0:128] + e[:, 128:256] + e[:, 256:384])
            energies = jnp.concatenate(energies, axis=0)
            part[t, 32:48, :] = jnp.concatenate(list(split3(energies)) + [jnp.zeros((4, 128), BF16)], axis=0)
            return carry

        lax.fori_loop(0, 2, weigh, 0)
        section = jnp.dot(
            prod[2 * half : 2 * half + 2].reshape(2 * ROWS, 4 * BOX), col[...], preferred_element_type=F32
        ).astype(BF16)
        stacked = jnp.concatenate(
            [
                jnp.concatenate(
                    [section[ROWS * j : ROWS * j + ROWS, :128], section[ROWS * j : ROWS * j + ROWS, 128:]],
                    axis=0,
                )
                for j in range(2)
            ],
            axis=1,
        )
        partial = jnp.dot(rowt[...], stacked, preferred_element_type=F32).astype(BF16)
        for j in range(2):
            part[(z + start + j) % SLABS, 0:32, :] = partial[:, 128 * j : 128 * j + 128]
        for j in (1, 0):
            r = (start + j) % SLABS
            if r == 0:
                continue
            to = (z + r) % SLABS
            copy = remote(part.at[to], parts_in.at[z], part_send.at[r], part_recv.at[z], {"slab": to})
            copy.start()
            copies.append(copy)

    link_copy.wait()

    def add_item(u, carry):
        e = u // 16
        before = link[u, 1]
        has = jnp.where(before >= 0, 1.0, 0.0)
        from_u = jnp.minimum(jnp.maximum(before, 0), SLOTS - 1)
        column = (u % 16) // 4
        t = u % 4
        c = ctf[meta_all[column, t, 0, 8 * e]]
        valid = meta_all[column, t, 0, 8 * e + 4].astype(F32)
        vprod[u] = contrib[u].astype(F32) + has * vprod[from_u]
        eprod[u] = (c * c) * valid + has * eprod[from_u]
        return carry

    lax.fori_loop(0, SLOTS, add_item, 0)
    whole = part[z].astype(F32)
    for r in NEAR8:
        s = (z + r) % SLABS
        remote(part.at[s], parts_in.at[s], part_send.at[r], part_recv.at[s], {"slab": s}).wait_recv()
        whole = whole + parts_in[s].astype(F32)
    best = jnp.max(whole[0:32], axis=0, keepdims=True)
    lane4 = lax.broadcasted_iota(I32, (4, 128), 1)
    row4 = lax.broadcasted_iota(I32, (4, 128), 0)
    top = jnp.max(jnp.where(lane4 // 32 == row4, best, -jnp.inf), axis=1, keepdims=True)
    energy = jnp.sum(whole[32:36] + (whole[36:40] + whole[40:44]), axis=1, keepdims=True)
    value = top / jnp.sqrt(energy + 1e-06)
    answer = jnp.sum(jnp.where(lane4 == row4, value, 0.0), axis=0, keepdims=True)
    ret_out[...] = answer

    def score_copy(e, r):
        return remote(
            ret_out, ret.at[d], ret_send.at[8 * e + r], ret_recv.at[d],
            {"dom": 2 * z + e, "slab": (z + r) % SLABS},
        )

    for r in FAR8:
        for e in range(2):
            score_copy(e, r).start()
    for e in range(2):
        pl.when(2 * z + e != d)(score_copy(e, 0).start)

    @pl.when(d // 2 == z)
    def _():
        ret[d] = answer

    def one_slice(r, carry):
        at = link[r, 0]
        has = jnp.where(at >= 0, 1.0, 0.0)
        at = jnp.minimum(jnp.maximum(at, 0), SLOTS - 1)
        inverse = 1.0 / weight_ref[...]
        top = has * vprod[at] + maps[r].astype(F32) * inverse
        new_ref[r] = top / (has * eprod[at] + inverse)
        return carry

    lax.fori_loop(0, ORI, one_slice, 0)

    for copy in copies:
        copy.wait_send()
    for e in range(2):
        for r in FAR8:
            score_copy(e, r).wait_send()
        pl.when(2 * z + e != d)(score_copy(e, 0).wait_send)
    for r in range(DOMS):
        s = (d + r) % DOMS
        copy = remote(ret_out, ret.at[s], ret_send.at[r], ret_recv.at[s], {"dom": s, "slab": d // 2})
        if r == 0:
            pl.when(d // 2 != z)(copy.wait_recv)
        else:
            copy.wait_recv()
    picked = [jnp.where(lane1 == 2 * (d % 2) + ranks[p], ret[owners[p]], 0.0) for p in range(PART)]
    picked = jnp.sum(jnp.concatenate(picked, axis=0), axis=1, keepdims=True)
    lane8 = lax.broadcasted_iota(I32, (PART, 128), 1)
    row8 = lax.broadcasted_iota(I32, (PART, 128), 0)
    scores = jnp.sum(jnp.where(lane8 == row8, picked, 0.0), axis=0, keepdims=True)
    score_ref[...] = scores[:, :PART]


DELIVER = 8


def deliver_kernel(score_in, corr_in, new_in, score_out, corr_out, new_out, sem):
    step = ORI // DELIVER
    writes = []
    for t in range(DELIVER):
        block = pl.ds(step * t, step)
        writes.append(pltpu.make_async_copy(new_in.at[block], new_out.at[block], sem.at[t]))
    writes.append(pltpu.make_async_copy(score_in, score_out, sem.at[DELIVER]))
    writes.append(pltpu.make_async_copy(corr_in, corr_out, sem.at[DELIVER + 1]))
    for copy in writes:
        copy.start()
    for copy in writes:
        copy.wait()


def deliver(scores, fsc, new_maps):
    hbm = pl.BlockSpec(memory_space=pl.ANY)
    vmem = pl.BlockSpec(memory_space=pltpu.VMEM)
    return pl.pallas_call(
        deliver_kernel,
        out_shape=(
            jax.ShapeDtypeStruct((1, PART), F32),
            jax.ShapeDtypeStruct((NSHELL,), F32),
            jax.ShapeDtypeStruct((ORI, ROWS, BOX), F32),
        ),
        in_specs=[vmem, vmem, vmem],
        out_specs=(hbm, hbm, hbm),
        scratch_shapes=[
            pltpu.SemaphoreType.DMA((DELIVER + 2,)),
        ],
        compiler_params=pltpu.CompilerParams(vmem_limit_bytes=16 * 1024 * 1024),
        name="deliver",
    )(scores, fsc, new_maps)


def run_main(*operands):
    hbm = pl.BlockSpec(memory_space=pltpu.HBM)
    vmem = pl.BlockSpec(memory_space=pltpu.VMEM)
    v = pltpu.VMEM
    smem = pltpu.SMEM
    dma = pltpu.SemaphoreType.DMA
    return pl.pallas_call(
        main_kernel,
        out_shape=(
            pltpu.VMEM((1, PART), F32),
            pltpu.VMEM((NSHELL,), F32),
            pltpu.VMEM((ORI, ROWS, BOX), F32),
        ),
        in_specs=[hbm] * 15,
        out_specs=(vmem, vmem, vmem),
        scratch_shapes=[
            smem((PART,), I32), smem((2, PART), I32), smem((PART,), I32), smem((CLASSES,), F32),
            smem((512,), I32),
            v((PART, ROWS, BOX), BF16),
            v((ORI, ROWS, BOX), BF16),
            v((ORI // 2, ROWS, BOX), BF16),
            v((ROWS, BOX), I32),
            v((ROWS, 256), I32),
            v((ROWS, BOX), F32),
            v((33, 8, BOX), F32),
            v((2, ROWS, 128), F32),
            v((4 * BOX, 256), BF16),
            v((SHIFTS, 2 * ROWS), BF16),
            v((BOX, 256), BF16),
            v((ROWS, BOX), F32),
            v((4, 5, ROWS, BOX), BF16),
            v((5, 4, ROWS, BOX), BF16),
            v((4, 4, ROWS, BOX), BF16),
            v((4, 4, ROWS, BOX), BF16),
            v((SLOTS, ROWS, BOX), BF16),
            v((SLOTS, ROWS, BOX), F32),
            v((SLOTS, ROWS, BOX), F32),
            v((CLASSES, ROWS, BOX), F32),
            v((33, 2, ROWS, 128), F32),
            v((4, 4, 1, 128), I32),
            v((4, 4, 1, 128), I32),
            v((4, 4, 1, 128), I32),
            smem((4, 4, 1, 128), I32),
            smem((4, 4, 1, 128), I32),
            v((SLOTS, 128), I32),
            smem((SLOTS, 128), I32),
            v((8, 1, 3 * SHELLS), F32),
            v((4, 1, 3 * SHELLS), F32),
            v((8, 1, 3 * SHELLS), F32),
            v((3, 1, 3 * SHELLS), F32),
            v((SLABS, ROWS, 4 * BOX), BF16),
            v((SLABS, 48, 128), BF16),
            v((SLABS, 48, 128), BF16),
            v((DOMS, 1, 128), F32),
            v((1, 128), F32),
            dma((15,)),
            dma((8,)),
            pltpu.SemaphoreType.REGULAR((3,)),
            dma((NCHUNK,)), dma((NCHUNK,)),
            dma((4,)), dma((4,)),
            dma((4,)), dma((4,)),
            dma((4,)), dma((4,)),
            dma((4,)), dma((4,)),
            dma((4,)), dma((4,)),
            dma((8,)), dma((8,)),
            dma((4,)), dma((4,)),
            dma((8,)), dma((8,)),
            dma((8,)), dma((8,)),
            dma((16,)), dma((16,)),
        ],
        compiler_params=pltpu.CompilerParams(
            collective_id=0, has_side_effects=True, vmem_limit_bytes=44 * 1024 * 1024
        ),
        name="refine",
    )(*[pltpu.with_memory_space_constraint(x, pltpu.HBM) for x in operands])


def on_device(consts, images, orientation, offsets, defocus_class, defocus, ori_slot, half_maps):
    scores, fsc, new_maps = run_main(
        orientation[0], offsets[0].T, defocus_class[0], defocus, ori_slot, images[0], half_maps[0], *consts
    )
    scores, fsc, new_maps = deliver(scores, fsc, new_maps)
    return scores, new_maps[None], fsc


def solution(mesh):
    in_specs = (
        P("half", "dom", "slab", None),
        P("half", "dom"),
        P("half", "dom", None),
        P("half", "dom"),
        P(),
        P(),
        P("half", "dom", "slab", None),
    )
    out_specs = (P("half", "dom"), P("half", "dom", "slab", None), P())
    return jax.shard_map(
        functools.partial(on_device, tables()),
        mesh=mesh, in_specs=in_specs, out_specs=out_specs, check_vma=False,
    )
```
